512 devices in a mesh: row: 32 (over y, z_hi), col: 16 (over z_lo, x, core).
Axes of the slice: x: 4, y: 8, z: 8 (z_hi: 4, z_lo: 2; z = z_hi * 2 + z_lo), core: 2. Of those that a mesh axis runs over, the one named last changes fastest.
Arguments:
- right_side: float32 [1, 256, 256, 256], P(None, 'row', 'col'), may hold values from -6 to 6
- lift_scale: float32 [16], replicated, may hold values from 0.5 to 2
- lift_shift: float32 [16], replicated, may hold values from -1.5 to 1.5
- spectral_weight: bfloat16 [64, 64, 16, 16, 128], P('row', 'col'), may hold values from -4 to 4
- local_weight: float32 [16, 16], replicated, may hold values from -1.5 to 1.5
- local_bias: float32 [16], replicated, may hold values from -3 to 3
- readout: float32 [16], replicated, may hold values from -1.5 to 1.5
Outputs:
- residual: float32 [1, 256, 256, 256], P(None, 'row', 'col')
- spectral_grad: bfloat16 [64, 64, 16, 16, 128], P('row', 'col')
The draws below stay inside these ranges and needn't reach their ends.
All inputs are finite; a program needn't handle non-finite values.
Results may differ from the reference program's by a relative error of at most 0.001.
Values sent between devices are 32-bit elements; how exact they have to be, the bound alone decides.
No kernel may reach another device: no remote copies, remote signals or barrier semaphores. Data moves between devices by JAX's collectives and lax.ppermute only.
A program may use at most 64 MiB of HBM per device.

```python
import math
import jax
import jax.numpy as jnp
from jax import lax

SAMPLES = 1
WIDTH = 16
MODES = 64
NX = 256
NY = 256
NZ = 256


def level_of(stream_key, shape, cuts, smallest, high):
    factor_of, own = 1.0, jax.random.fold_in(stream_key, 6)
    for dim, blocks in cuts:
        heights = jnp.exp(jax.random.uniform(jax.random.fold_in(own, dim), (blocks,), jnp.float32, smallest / len(cuts), high / len(cuts)))
        factor_of = factor_of * jnp.repeat(heights, shape[dim] // blocks).reshape([-1 if axis == dim else 1 for axis in range(len(shape))])
    return factor_of


def gaussian(key, shape, width, limit, split=(), kind=jnp.bfloat16):
    factor_of = level_of(key, shape, split, -0.22, 0.18) if split else 1.0
    result = jax.random.normal(key, shape, jnp.float32) * width * factor_of
    return jnp.minimum(jnp.maximum(result, -limit), limit).astype(kind)


def setup_inputs(seed: int = 0) -> dict:
    arg_keys = jax.random.split(jax.random.key(seed), 8)
    return {
        "right_side": gaussian(arg_keys[0], (SAMPLES, NX, NY, NZ), 1.0, 6.0, ((1, 32), (2, 16)), jnp.float32),
        "lift_scale": jnp.clip(jnp.exp(jax.random.uniform(arg_keys[1], (WIDTH,), jnp.float32, math.log(0.5), math.log(2.0))), 0.5, 2.0),
        "lift_shift": jnp.clip(jax.random.uniform(arg_keys[2], (WIDTH,), jnp.float32, -1.5, 1.5), -1.5, 1.5),
        "spectral_weight": gaussian(arg_keys[3], (MODES, MODES, WIDTH, WIDTH, 2 * MODES), 0.7, 4.0, ((0, 32), (1, 16))),
        "local_weight": gaussian(arg_keys[4], (WIDTH, WIDTH), WIDTH ** -0.5, 1.5, (), jnp.float32),
        "local_bias": gaussian(arg_keys[5], (WIDTH,), 0.5, 3.0, (), jnp.float32),
        "readout": gaussian(arg_keys[6], (WIDTH,), WIDTH ** -0.5, 1.5, (), jnp.float32),
    }


HIGHEST_PRECISION = lax.Precision.HIGHEST

def lifting(right_side, lift_scale, lift_shift):
    sample = right_side[:, None]
    gain_row = lift_scale[None, :, None, None, None]
    offset = lift_shift[None, :, None, None, None]
    return jax.nn.gelu(gain_row * sample + offset) - jax.nn.gelu(offset - gain_row * sample)

def laplace(values):
    padded = jnp.pad(values, ((0, 0), (1, 1), (1, 1), (1, 1)))
    centre = padded[:, 1:-1, 1:-1, 1:-1]
    beside = padded[:, 2:, 1:-1, 1:-1] + padded[:, :-2, 1:-1, 1:-1]
    beside = beside + padded[:, 1:-1, 2:, 1:-1] + padded[:, 1:-1, :-2, 1:-1]
    beside = beside + padded[:, 1:-1, 1:-1, 2:] + padded[:, 1:-1, 1:-1, :-2]
    return 6.0 * centre - beside

def select_modes(spectrum, along, length):
    half_modes = MODES // 2
    upper_half = lax.slice_in_dim(spectrum, length - half_modes, length, axis=along)
    lower_half = lax.slice_in_dim(spectrum, 0, half_modes, axis=along)
    return jnp.concatenate([upper_half, lower_half], axis=along)

def spread_modes(spectrum, along, length):
    half_modes = MODES // 2
    upper_half = lax.slice_in_dim(spectrum, half_modes, MODES, axis=along)
    lower_half = lax.slice_in_dim(spectrum, 0, half_modes, axis=along)
    filler_shape = list(spectrum.shape)
    filler_shape[along] = length - MODES
    filler = jnp.zeros(tuple(filler_shape), spectrum.dtype)
    return jnp.concatenate([upper_half, filler, lower_half], axis=along)

def forward_one(values):
    spectrum = jnp.fft.rfft(values, axis=2, norm='ortho')[:, :, :MODES]
    spectrum = select_modes(jnp.fft.fft(spectrum, axis=1, norm='ortho'), 1, NY)
    spectrum = select_modes(jnp.fft.fft(spectrum, axis=0, norm='ortho'), 0, NX)
    return spectrum

def inverse_one(spectrum):
    expanded = jnp.fft.ifft(spread_modes(spectrum, 0, NX), axis=0, norm='ortho')
    expanded = jnp.fft.ifft(spread_modes(expanded, 1, NY), axis=1, norm='ortho')
    filler = jnp.zeros((NX, NY, NZ // 2 + 1 - MODES), expanded.dtype)
    padded = jnp.concatenate([expanded, filler], axis=2)
    return jnp.fft.irfft(padded, n=NZ, axis=2, norm='ortho')

def reference(right_side, lift_scale, lift_shift, spectral_weight, local_weight, local_bias, readout):
    lifted = lifting(right_side, lift_scale, lift_shift)
    flat = lifted.reshape((SAMPLES * WIDTH, NX, NY, NZ))
    spectra = lax.map(forward_one, flat).reshape((SAMPLES, WIDTH, MODES, MODES, MODES))
    spectra_real = jnp.real(spectra)
    spectra_imag = jnp.imag(spectra)
    weight = spectral_weight.astype(jnp.float32).reshape((MODES, MODES, WIDTH, WIDTH, 2, MODES))
    weight_real = weight[:, :, :, :, 0]
    weight_imag = weight[:, :, :, :, 1]
    form = 'bixyz,yziox->boxyz'
    mixed_real = jnp.einsum(form, spectra_real, weight_real, precision=HIGHEST_PRECISION) - jnp.einsum(form, spectra_imag, weight_imag, precision=HIGHEST_PRECISION)
    mixed_imag = jnp.einsum(form, spectra_real, weight_imag, precision=HIGHEST_PRECISION) + jnp.einsum(form, spectra_imag, weight_real, precision=HIGHEST_PRECISION)
    mixed_modes = jnp.transpose(lax.complex(mixed_real, mixed_imag), (1, 0, 2, 3, 4))

    def channel_preact(mixed_one, weight_one, bias_one):
        spectral = jax.vmap(inverse_one)(mixed_one)
        local_term = jnp.einsum('i,bixyz->bxyz', weight_one, lifted, precision=HIGHEST_PRECISION)
        return spectral + local_term + bias_one
    channel_inputs = (mixed_modes, jnp.transpose(local_weight), local_bias, readout)

    def accumulate(running, inputs):
        mixed_one, weight_one, bias_one, read_one = inputs
        return (running + read_one * jax.nn.gelu(channel_preact(mixed_one, weight_one, bias_one)), None)
    potential, _ = lax.scan(accumulate, jnp.zeros(right_side.shape, right_side.dtype), channel_inputs)
    residual = laplace(potential) - right_side
    adjoint = laplace(residual)

    def gradient_of(inputs):
        mixed_one, weight_one, bias_one, read_one = inputs
        preact = channel_preact(mixed_one, weight_one, bias_one)
        _, pullback = jax.vjp(jax.nn.gelu, preact)
        grad_preact = pullback(read_one * adjoint)[0]
        return jax.vmap(forward_one)(grad_preact)
    grad_spectra = jnp.transpose(lax.map(gradient_of, channel_inputs), (1, 0, 2, 3, 4))
    kz_weight = jnp.where(jnp.arange(MODES) == 0, 1.0, 2.0).astype(right_side.dtype)
    grad_real = jnp.real(grad_spectra) * kz_weight
    grad_imag = jnp.imag(grad_spectra) * kz_weight
    outer = 'bixyz,boxyz->yziox'
    result_real = jnp.einsum(outer, spectra_real, grad_real, precision=HIGHEST_PRECISION) + jnp.einsum(outer, spectra_imag, grad_imag, precision=HIGHEST_PRECISION)
    result_imag = jnp.einsum(outer, spectra_real, grad_imag, precision=HIGHEST_PRECISION) - jnp.einsum(outer, spectra_imag, grad_real, precision=HIGHEST_PRECISION)
    spectral_grad = jnp.stack([result_real, result_imag], axis=4).reshape((MODES, MODES, WIDTH, WIDTH, 2 * MODES))
    return (residual, spectral_grad.astype(jnp.bfloat16))
```

```python
import math

import jax
import jax.numpy as jnp
import numpy as np
from jax import lax
from jax.experimental import pallas as pl
from jax.experimental.pallas import tpu as pltpu
from jax.sharding import Mesh
from jax.sharding import PartitionSpec as P

MODES = 64
GRID = 256
WIDTH = 16
HALF = 8
ROWS = 32
PLANES = 8
COLS = 16
ROW = ("y", "zh")
COL = ("zl", "x", "core")
F32 = jnp.float32
BF16 = jnp.bfloat16
VMEM_LIMIT = 40 * 1024 * 1024


def halves(table):
    high = table.astype(jnp.bfloat16)
    low = (table - high.astype(np.float64)).astype(jnp.bfloat16)
    return high, low


def wave(frequencies, points):
    phase = (np.outer(frequencies, points) % GRID) * (2.0 * math.pi / GRID)
    return np.cos(phase) / 16.0, np.sin(phase) / 16.0


def tables():
    points = np.arange(GRID)
    cos_z, sin_z = wave(np.arange(MODES), points)
    z_forward = np.concatenate([cos_z, -sin_z], axis=0)
    weight = np.where(np.arange(MODES) == 0, 1.0, 2.0)[:, None]
    z_inverse = np.concatenate([cos_z * weight, -sin_z * weight], axis=0).T
    ky = np.array([2 * r + a - MODES // 2 for a in range(2) for r in range(ROWS)])
    cos_y, sin_y = wave(ky, points)
    y_table = np.concatenate(
        [np.concatenate([cos_y, sin_y], axis=1), np.concatenate([-sin_y, cos_y], axis=1)], axis=0
    )
    places = np.array([8 * r + q for q in range(PLANES) for r in range(ROWS)])
    cos_x, sin_x = wave(np.arange(MODES) - MODES // 2, places)
    x_table = np.concatenate([cos_x.T, -sin_x.T], axis=1)
    return halves(z_forward), halves(z_inverse), halves(y_table), halves(x_table)


def split(value):
    high = value.astype(BF16)
    return high, (value - high.astype(F32)).astype(BF16)


def dot(left, right, dims):
    return lax.dot_general(left, right, (dims, ((), ())), preferred_element_type=F32)


NN = ((1,), (0,))
NT = ((1,), (1,))


def dot3(left, right, dims):
    total = dot(left[0], right[1], dims) + dot(left[1], right[0], dims)
    return total + dot(left[0], right[0], dims)


ROOT = math.sqrt(2.0 / math.pi)
CUBE = 0.044715


def gelu(value):
    inner = value * (ROOT + (ROOT * CUBE) * (value * value))
    half = 0.5 * value
    return half + half * jnp.tanh(inner)


def gelu_both(value):
    square = value * value
    inner = value * (ROOT + (ROOT * CUBE) * square)
    bent = jnp.tanh(inner)
    cdf = 0.5 + 0.5 * bent
    slope = ROOT + (3.0 * ROOT * CUBE) * square
    return value * cdf, cdf + (0.5 * value) * ((1.0 - bent * bent) * slope)


def lift(field, scale, shift):
    scaled = scale * field
    return gelu(shift + scaled) - gelu(shift - scaled)


def lane_index(shape):
    return lax.broadcasted_iota(jnp.int32, shape, len(shape) - 1)


def swapped(value):
    return pltpu.roll(value, MODES, 1)


def plane_forward(fill, zf, yt, stage_high, stage_low, lines, out):
    for channel in range(HALF):
        fill(channel, stage_high, stage_low)
        z = dot3((zf[0][...], zf[1][...]), (stage_high[...], stage_low[...]), NN)
        lines[:, channel, 0:GRID] = z[:MODES]
        lines[:, channel, GRID:] = z[MODES:]
    modes = split(lines[...].reshape(MODES * HALF, 2 * GRID))
    spectrum = dot3((yt[0][...], yt[1][...]), modes, NT)
    lane = lane_index((ROWS, 128)) // 32
    for tile in range(4):
        parts = [spectrum[b * 32 : b * 32 + 32, tile * 128 : tile * 128 + 128] for b in range(4)]
        for e in range(4):
            total = None
            for b in range(4):
                turn = ((b - e) % 4) * 32
                moved = pltpu.roll(parts[b], turn, 1) if turn else parts[b]
                total = moved if total is None else jnp.where(lane == b, moved, total)
            column = 4 * tile + e
            out[column * 32 : column * 32 + 32, :] = total


def lift_kernel(place, scale, shift, plane, zf0, zf1, yt0, yt1, out, turned, high, low, lines):
    core = place[0]
    turned[...] = plane[...].T

    def fill(channel, stage_high, stage_low):
        gain, offset = scale[core * HALF + channel], shift[core * HALF + channel]
        for t in range(8):
            rows = slice(32 * t, 32 * t + 32)
            stage_high[rows, :], stage_low[rows, :] = split(lift(turned[rows, :], gain, offset))

    plane_forward(fill, (zf0, zf1), (yt0, yt1), high, low, lines, out)


def grad_kernel(adjoint, slope, zf0, zf1, yt0, yt1, out, turned, high, low, lines):
    turned[...] = adjoint[...].T

    def fill(channel, stage_high, stage_low):
        for t in range(8):
            rows = slice(32 * t, 32 * t + 32)
            stage_high[rows, :], stage_low[rows, :] = split(turned[rows, :] * slope[channel, rows, :])

    plane_forward(fill, (zf0, zf1), (yt0, yt1), high, low, lines, out)


def local_kernel(place, scale, shift, weight, bias, plane, out, turned):
    first = place[0] * HALF
    turned[...] = plane[...].T

    def step(t, carry):
        rows = pl.ds(pl.multiple_of(t * 8, 8), 8)
        field = turned[rows, :]
        sums = [jnp.full((8, GRID), bias[first + o], F32) for o in range(HALF)]
        for i in range(WIDTH):
            lifted = lift(field, scale[i], shift[i])
            sums = [sums[o] + weight[i, first + o] * lifted for o in range(HALF)]
        for o in range(HALF):
            out[o, rows, :] = sums[o]
        return carry

    lax.fori_loop(0, GRID // 8, step, 0)


def inverse_kernel(
    place, readout, received, local, plane, zi0, zi1, yt0, yt1, out, slope, grid, lines, spectral, total, padded
):
    core = place[0]
    lane = lane_index((ROWS, 128)) // 32
    for tile in range(4):
        parts = [received[(4 * tile + e) * 32 : (4 * tile + e) * 32 + 32, :] for e in range(4)]
        for b in range(4):
            whole = None
            for e in range(4):
                turn = ((e - b) % 4) * 32
                moved = pltpu.roll(parts[e], turn, 1) if turn else parts[e]
                whole = moved if whole is None else jnp.where(lane == e, moved, whole)
            grid[b * 32 : b * 32 + 32, tile * 128 : tile * 128 + 128] = whole
    lines[...] = dot3(split(grid[...].T), (yt0[...], yt1[...]), NN).reshape(MODES, HALF, 2 * GRID)
    for o in range(HALF):
        modes = jnp.concatenate([lines[:, o, 0:GRID], lines[:, o, GRID:]], axis=0)
        spectral[...] = dot3((zi0[...], zi1[...]), split(modes), NN)
        read = readout[core * HALF + o]
        for t in range(8):
            rows = slice(32 * t, 32 * t + 32)
            value, derivative = gelu_both(spectral[rows, :] + local[o, rows, :])
            slope[o, rows, :] = read * derivative
            if o == 0:
                total[rows, :] = read * value
            else:
                total[rows, :] += read * value
    padded[0:8, :] = jnp.zeros((8, GRID), F32)
    padded[256:264, :] = jnp.zeros((8, GRID), F32)
    padded[4:260, :] = total[...].T
    keep = jnp.where(core == 0, 1.0, 0.0).astype(F32)
    blank = jnp.zeros((1, GRID), F32)
    row = lax.broadcasted_iota(jnp.int32, (24, GRID), 0)
    for c in range(COLS):
        before = plane[16 * c - 1 : 16 * c, :] * keep if c > 0 else blank
        after = plane[16 * c + 16 : 16 * c + 17, :] * keep if c < COLS - 1 else blank
        block = padded[16 * c : 16 * c + 24, :]
        block = jnp.where(row == 1, before, jnp.where(row == 22, after, block))
        out[c, 0:24, :] = block[:, 0:128]
        out[c, 24:48, :] = block[:, 128:256]


def gather_spectra(received, xt0, xt1, sign):
    spectra = []
    for k in range(2):
        lines = jnp.concatenate(
            [received[(2 * q + k) * 32 : (2 * q + k) * 32 + 32, :] for q in range(PLANES)], axis=0
        )
        product = dot3(split(lines.T), (xt0[...], xt1[...]), NN)
        spectra.append(product[:64] + sign * swapped(product[64:]))
    return spectra


def mix_kernel(received, weight, xt0, xt1, out, spectra_out, real, imag):
    low = lane_index((64, 128)) < MODES
    sign = jnp.where(low, -1.0, 1.0).astype(F32)
    for k, spectra in enumerate(gather_spectra(received, xt0, xt1, sign)):
        spectra_out[k] = spectra
        other = swapped(spectra)
        real[k] = jnp.where(low, spectra, other)
        imag[k] = jnp.where(low, other, spectra)
    parts = [[], []]
    for group in range(8):
        a, j = group // 4, group % 4
        first = jnp.zeros((WIDTH, 128), F32)
        second = jnp.zeros((WIDTH, 128), F32)
        for i in range(WIDTH):
            k, row = i // HALF, group * HALF + i % HALF
            tile = weight[a, j, i].astype(F32)
            first = first + tile * real[k, row : row + 1, :]
            second = second + tile * imag[k, row : row + 1, :]
        mixed = first + sign[:WIDTH] * swapped(second)
        parts[0].append(mixed[:HALF])
        parts[1].append(mixed[HALF:])
    for k in range(2):
        mixed = jnp.concatenate(parts[k], axis=0)
        both = jnp.concatenate([mixed, -sign * swapped(mixed)], axis=0)
        result = dot3((xt0[...], xt1[...]), split(both), NT)
        for q in range(PLANES):
            out[(2 * q + k) * 32 : (2 * q + k) * 32 + 32, :] = result[q * 32 : q * 32 + 32]


def outer_kernel(place, received, spectra_in, xt0, xt1, out, real, imag):
    low = lane_index((64, 128)) < MODES
    sign = jnp.where(low, -1.0, 1.0).astype(F32)
    row = lax.broadcasted_iota(jnp.int32, (64, 128), 0)
    zero_mode = jnp.logical_and((row // HALF) % 4 == 0, place[2] == 0)
    doubling = jnp.where(zero_mode, 1.0, 2.0).astype(F32)
    grads = [doubling * g for g in gather_spectra(received, xt0, xt1, sign)]
    turned = [-sign * swapped(g) for g in grads]
    for k in range(2):
        spectra = spectra_in[k]
        other = swapped(spectra)
        real[k] = jnp.where(low, spectra, other)
        imag[k] = jnp.where(low, other, spectra)
    for group in range(8):
        a, j = group // 4, group % 4
        rows = slice(group * HALF, group * HALF + HALF)
        straight = jnp.concatenate([grads[0][rows], grads[1][rows]], axis=0)
        crossed = jnp.concatenate([turned[0][rows], turned[1][rows]], axis=0)
        for i in range(WIDTH):
            k, line = i // HALF, group * HALF + i % HALF
            value = straight * real[k, line : line + 1, :] + crossed * imag[k, line : line + 1, :]
            out[a, j, i] = value.astype(BF16)


def edge_kernel(received, field, planes, lower, upper):
    for q in range(PLANES):
        planes[q] = received[2 * q] + received[2 * q + 1]
    for ref, first, own in ((lower, 0, 0), (upper, PLANES - 2, PLANES - 1)):
        ref[0:48, :] = planes[first]
        ref[48:96, :] = planes[first + 1]
        ref[96:112, :] = field[own, :, 0:128]
        ref[112:128, :] = field[own, :, 128:256]


def stencil_kernel(place, planes, before, after, field, residual, adjoint, wide, sources):
    row_place, col_place = place[1], place[2]
    for q in range(PLANES):
        wide[q + 2, :, 0:128] = planes[q, 0:24, :]
        wide[q + 2, :, 128:256] = planes[q, 24:48, :]
    for p in range(2):
        for base, ref in ((0, before), (PLANES + 2, after)):
            wide[base + p, :, 0:128] = ref[48 * p : 48 * p + 24, :]
            wide[base + p, :, 128:256] = ref[48 * p + 24 : 48 * p + 48, :]
    row = lax.broadcasted_iota(jnp.int32, (24, GRID), 0)
    lane = lane_index((24, GRID))
    sources[...] = jnp.zeros(sources.shape, F32)
    for q in range(PLANES):
        sources[q + 1, 4:20, :] = field[q]
        sources[q + 1, 3:4, :] = wide[q + 2, 1:2, :]
        sources[q + 1, 20:21, :] = wide[q + 2, 22:23, :]
    for base, ref in ((0, before), (PLANES + 1, after)):
        sources[base, 4:20, 0:128] = ref[96:112, :]
        sources[base, 4:20, 128:256] = ref[112:128, :]
    first_row = jnp.where(col_place == 0, 4, 3)
    last_row = jnp.where(col_place == COLS - 1, 19, 20)
    inside = jnp.logical_and(row >= first_row, row <= last_row)

    def cross(get, index):
        centre = get(index)
        beside = get(index - 1) + get(index + 1)
        beside = beside + pltpu.roll(centre, 1, 0) + pltpu.roll(centre, 23, 0)
        left = jnp.where(lane == 0, 0.0, pltpu.roll(centre, 1, 1))
        right = jnp.where(lane == GRID - 1, 0.0, pltpu.roll(centre, GRID - 1, 1))
        return 6.0 * centre - (beside + left + right)

    rest = []
    for p in range(PLANES + 2):
        value = cross(lambda n: wide[n], p + 1) - sources[p]
        keep = inside
        if p == 0:
            keep = jnp.logical_and(inside, row_place > 0)
        if p == PLANES + 1:
            keep = jnp.logical_and(inside, row_place < ROWS - 1)
        value = jnp.where(keep, value, 0.0)
        rest.append(value)
        if 1 <= p <= PLANES:
            residual[p - 1] = value[4:20]
    for q in range(PLANES):
        value = cross(lambda n: rest[n], q + 1)[4:20]
        adjoint[2 * q] = value
        adjoint[2 * q + 1] = value


def call(kernel, operands, scalars, outputs, scratch, flops=0):
    many = isinstance(outputs, list)
    vmem = pl.BlockSpec(memory_space=pltpu.VMEM)
    smem = pl.BlockSpec(memory_space=pltpu.SMEM)
    cost = pl.CostEstimate(flops=flops, bytes_accessed=4 << 20, transcendentals=flops // 16)
    return pl.pallas_call(
        kernel,
        in_specs=[smem] * len(scalars) + [vmem] * len(operands),
        out_specs=[vmem] * len(outputs) if many else vmem,
        out_shape=outputs,
        scratch_shapes=scratch,
        compiler_params=pltpu.CompilerParams(vmem_limit_bytes=VMEM_LIMIT),
        cost_estimate=cost if flops else None,
    )(*scalars, *operands)


def exchange(value, axes):
    return lax.all_to_all(value, axes, split_axis=0, concat_axis=0, tiled=True)


def shape(*sizes):
    return jax.ShapeDtypeStruct(sizes, F32)


def shards(right_side, lift_scale, lift_shift, spectral_weight, local_weight, local_bias, readout):
    zf, zi, yt, xt = tables()
    core = lax.axis_index("core")
    row_place = lax.axis_index(ROW)
    col_place = lax.axis_index(COL)
    place = jnp.stack([core, row_place, col_place]).astype(jnp.int32)
    everywhere = COL + ROW
    field = right_side[0]

    plane = exchange(jnp.repeat(field, 2, axis=0), COL).reshape(GRID, GRID)
    line_scratch = pltpu.VMEM((MODES, HALF, 2 * GRID), F32)
    plane_scratch = [
        pltpu.VMEM((GRID, GRID), F32),
        pltpu.VMEM((GRID, GRID), BF16),
        pltpu.VMEM((GRID, GRID), BF16),
        line_scratch,
    ]
    lifted = call(
        lift_kernel, (plane, *zf, *yt), (place, lift_scale, lift_shift), shape(512, 128), plane_scratch
    )
    lifted = exchange(lifted, everywhere)
    local = call(
        local_kernel,
        (plane,),
        (place, lift_scale, lift_shift, local_weight, local_bias),
        shape(HALF, GRID, GRID),
        [pltpu.VMEM((GRID, GRID), F32)],
        flops=1 << 27,
    )
    pair = pltpu.VMEM((2, 64, 128), F32)
    mixed, spectra = call(
        mix_kernel, (lifted, spectral_weight, *xt), (), [shape(512, 128), shape(2, 64, 128)], [pair, pair]
    )
    mixed = exchange(mixed, everywhere)
    message, slope = call(
        inverse_kernel,
        (mixed, local, plane, *zi, *yt),
        (place, readout),
        [shape(COLS, 48, 128), shape(HALF, GRID, GRID)],
        [
            pltpu.VMEM((128, 512), F32),
            line_scratch,
            pltpu.VMEM((GRID, GRID), F32),
            pltpu.VMEM((GRID, GRID), F32),
            pltpu.VMEM((GRID + 8, GRID), F32),
        ],
    )
    message = exchange(message, COL)
    planes, lower, upper = call(
        edge_kernel, (message, field), (), [shape(PLANES, 48, 128), shape(128, 128), shape(128, 128)], []
    )
    forward = [(i, i + 1) for i in range(ROWS - 1)]
    backward = [(target, source) for source, target in forward]
    before = lax.ppermute(upper, ROW, forward)
    after = lax.ppermute(lower, ROW, backward)
    residual, adjoint = call(
        stencil_kernel,
        (planes, before, after, field),
        (place,),
        [shape(PLANES, COLS, GRID), shape(2 * PLANES, COLS, GRID)],
        [pltpu.VMEM((PLANES + 4, 24, GRID), F32), pltpu.VMEM((PLANES + 2, 24, GRID), F32)],
    )
    adjoint = exchange(adjoint, COL).reshape(GRID, GRID)
    grads = call(grad_kernel, (adjoint, slope, *zf, *yt), (), shape(512, 128), plane_scratch)
    grads = exchange(grads, everywhere)
    spectral_grad = call(
        outer_kernel,
        (grads, spectra, *xt),
        (place,),
        jax.ShapeDtypeStruct(spectral_weight.shape, BF16),
        [pair, pair],
    )
    return residual[None], spectral_grad


def solution(mesh):
    fine = Mesh(mesh.devices.reshape(8, 4, 2, 4, 2), ROW + COL)
    in_specs = (P(None, ROW, COL, None), P(), P(), P(ROW, COL, None, None, None), P(), P(), P())
    out_specs = (P(None, ROW, COL, None), P(ROW, COL, None, None, None))
    return jax.shard_map(shards, mesh=fine, in_specs=in_specs, out_specs=out_specs, check_vma=False)
```

```python
import math

import jax
import jax.numpy as jnp
import numpy as np
from jax import lax
from jax.experimental import pallas as pl
from jax.experimental.pallas import tpu as pltpu
from jax.sharding import Mesh
from jax.sharding import PartitionSpec as P

MODES = 64
GRID = 256
WIDTH = 16
HALF = 8
ROWS = 32
PLANES = 8
COLS = 16
ROW = ("y", "zh")
COL = ("zl", "x", "core")
F32 = jnp.float32
BF16 = jnp.bfloat16
VMEM_LIMIT = 40 * 1024 * 1024


def halves(table):
    high = table.astype(jnp.bfloat16)
    low = (table - high.astype(np.float64)).astype(jnp.bfloat16)
    return high, low


def wave(frequencies, points):
    phase = (np.outer(frequencies, points) % GRID) * (2.0 * math.pi / GRID)
    return np.cos(phase) / 16.0, np.sin(phase) / 16.0


def tables():
    points = np.arange(GRID)
    cos_z, sin_z = wave(np.arange(MODES), points)
    z_forward = np.concatenate(halves(np.concatenate([cos_z, -sin_z], axis=0)), axis=0)
    weight = np.where(np.arange(MODES) == 0, 1.0, 2.0)[:, None]
    high, low = halves(np.concatenate([cos_z * weight, -sin_z * weight], axis=0).T)
    z_inverse = np.block([[high, high], [low, np.zeros_like(low)]])
    ky = np.array([2 * r + a - MODES // 2 for a in range(2) for r in range(ROWS)])
    cos_y, sin_y = wave(ky, points)
    y_table = np.concatenate(
        [np.concatenate([cos_y, sin_y], axis=1), np.concatenate([-sin_y, cos_y], axis=1)], axis=0
    )
    y_table = np.concatenate(halves(y_table), axis=0)
    places = np.array([8 * r + q for q in range(PLANES) for r in range(ROWS)])
    cos_x, sin_x = wave(np.arange(MODES) - MODES // 2, places)
    x_table = np.concatenate(halves(np.concatenate([cos_x.T, -sin_x.T], axis=1)), axis=1)
    return z_forward, z_inverse, y_table, x_table


def split(value):
    high = value.astype(BF16)
    return high, (value - high.astype(F32)).astype(BF16)


def dot(left, right, dims):
    return lax.dot_general(left, right, (dims, ((), ())), preferred_element_type=F32)


NN = ((1,), (0,))
NT = ((1,), (1,))


ROOT = math.sqrt(2.0 / math.pi)
CUBE = 0.044715


def gelu(value):
    inner = value * (ROOT + (ROOT * CUBE) * (value * value))
    half = 0.5 * value
    return half + half * jnp.tanh(inner)


def gelu_both(value):
    square = value * value
    inner = value * (ROOT + (ROOT * CUBE) * square)
    bent = jnp.tanh(inner)
    cdf = 0.5 + 0.5 * bent
    slope = ROOT + (3.0 * ROOT * CUBE) * square
    return value * cdf, cdf + (0.5 * value) * ((1.0 - bent * bent) * slope)


def lift(field, scale, shift):
    scaled = scale * field
    return gelu(shift + scaled) - gelu(shift - scaled)


def lane_index(shape):
    return lax.broadcasted_iota(jnp.int32, shape, len(shape) - 1)


def swapped(value):
    return pltpu.roll(value, MODES, 1)


def plane_forward(fill, z_table, y_table, stage_high, stage_low, lines, out):
    for channel in range(HALF):
        fill(channel, stage_high, stage_low)
        z = dot(z_table[...], stage_high[...], NN)
        z = z[:128] + z[128:] + dot(z_table[0:128, :], stage_low[...], NN)
        lines[:, channel, 0:GRID] = z[:MODES]
        lines[:, channel, GRID:] = z[MODES:]
    high, low = split(lines[...].reshape(MODES * HALF, 2 * GRID))
    spectrum = dot(y_table[...], high, NT)
    spectrum = spectrum[:128] + spectrum[128:] + dot(y_table[0:128, :], low, NT)
    lane = lane_index((ROWS, 128)) // 32
    for tile in range(4):
        parts = [spectrum[b * 32 : b * 32 + 32, tile * 128 : tile * 128 + 128] for b in range(4)]
        for e in range(4):
            total = None
            for b in range(4):
                turn = ((b - e) % 4) * 32
                moved = pltpu.roll(parts[b], turn, 1) if turn else parts[b]
                total = moved if total is None else jnp.where(lane == b, moved, total)
            column = 4 * tile + e
            out[column * 32 : column * 32 + 32, :] = total


def lift_kernel(place, params, plane, z_far, y_far, out, turned, high, low, lines, z_table, y_table, sems):
    z_copy = pltpu.make_async_copy(z_far, z_table, sems.at[0])
    y_copy = pltpu.make_async_copy(y_far, y_table, sems.at[1])
    z_copy.start()
    y_copy.start()
    core = place[0]
    turned[...] = plane[...].T
    z_copy.wait()
    y_copy.wait()

    def fill(channel, stage_high, stage_low):
        gain, offset = params[0, core * HALF + channel], params[1, core * HALF + channel]
        for t in range(8):
            rows = slice(32 * t, 32 * t + 32)
            stage_high[rows, :], stage_low[rows, :] = split(lift(turned[rows, :], gain, offset))

    plane_forward(fill, z_table, y_table, high, low, lines, out)


def grad_kernel(adjoint, slope, z_table, y_table, out, turned, high, low, lines):
    turned[...] = adjoint[...].T

    def fill(channel, stage_high, stage_low):
        for t in range(8):
            rows = slice(32 * t, 32 * t + 32)
            stage_high[rows, :], stage_low[rows, :] = split(turned[rows, :] * slope[channel, rows, :])

    plane_forward(fill, z_table, y_table, high, low, lines, out)


def spread_kernel(field, out, sems):
    copies = [pltpu.make_async_copy(field, out.at[:, k], sems.at[k]) for k in range(2)]
    for copy in copies:
        copy.start()
    for copy in copies:
        copy.wait()


def local_kernel(place, params, plane, out, turned):
    first = place[0] * HALF
    turned[...] = plane[...].T

    def step(t, carry):
        rows = pl.ds(pl.multiple_of(t * 8, 8), 8)
        field = turned[rows, :]
        sums = [jnp.full((8, GRID), params[2, first + o], F32) for o in range(HALF)]
        for i in range(WIDTH):
            lifted = lift(field, params[0, i], params[1, i])
            sums = [sums[o] + params[4 + i, first + o] * lifted for o in range(HALF)]
        for o in range(HALF):
            out[o, rows, :] = sums[o]
        return carry

    lax.fori_loop(0, GRID // 8, step, 0)


def inverse_kernel(
    place, params, received, local, plane, z_table, y_table, out, slope, grid, lines, spectral, total, padded
):
    core = place[0]
    lane = lane_index((ROWS, 128)) // 32
    for tile in range(4):
        parts = [received[(4 * tile + e) * 32 : (4 * tile + e) * 32 + 32, :] for e in range(4)]
        for b in range(4):
            whole = None
            for e in range(4):
                turn = ((e - b) % 4) * 32
                moved = pltpu.roll(parts[e], turn, 1) if turn else parts[e]
                whole = moved if whole is None else jnp.where(lane == e, moved, whole)
            grid[b * 32 : b * 32 + 32, tile * 128 : tile * 128 + 128] = whole
    high, low = split(grid[...].T)
    modes = dot(jnp.concatenate([high, high], axis=1), y_table[...], NN) + dot(low, y_table[0:128, :], NN)
    lines[...] = modes.reshape(MODES, HALF, 2 * GRID)
    for o in range(HALF):
        modes = jnp.concatenate([lines[:, o, 0:GRID], lines[:, o, GRID:]], axis=0)
        product = dot(z_table[...], jnp.concatenate(split(modes), axis=0), NN)
        spectral[...] = product[:GRID] + product[GRID:]
        read = params[3, core * HALF + o]
        for t in range(8):
            rows = slice(32 * t, 32 * t + 32)
            value, derivative = gelu_both(spectral[rows, :] + local[o, rows, :])
            slope[o, rows, :] = read * derivative
            if o == 0:
                total[rows, :] = read * value
            else:
                total[rows, :] += read * value
    padded[0:8, :] = jnp.zeros((8, GRID), F32)
    padded[256:264, :] = jnp.zeros((8, GRID), F32)
    padded[4:260, :] = total[...].T
    keep = jnp.where(core == 0, 1.0, 0.0).astype(F32)
    blank = jnp.zeros((1, GRID), F32)
    row = lax.broadcasted_iota(jnp.int32, (24, GRID), 0)
    for c in range(COLS):
        before = plane[16 * c - 1 : 16 * c, :] * keep if c > 0 else blank
        after = plane[16 * c + 16 : 16 * c + 17, :] * keep if c < COLS - 1 else blank
        block = padded[16 * c : 16 * c + 24, :]
        block = jnp.where(row == 1, before, jnp.where(row == 22, after, block))
        out[c, 0:24, :] = block[:, 0:128]
        out[c, 24:48, :] = block[:, 128:256]


def gather_spectra(received, x_table, sign):
    lines = []
    for k in range(2):
        parts = [received[(2 * q + k) * 32 : (2 * q + k) * 32 + 32, :] for q in range(PLANES)]
        lines.append(jnp.concatenate(parts, axis=0).T)
    product = dot(jnp.concatenate(split(jnp.concatenate(lines, axis=0)), axis=0), x_table[...], NN)
    product = product[:, :128] + product[:, 128:]
    product = product[:256] + product[256:]
    first = [product[128 * k : 128 * k + 64] for k in range(2)]
    second = [product[128 * k + 64 : 128 * k + 128] for k in range(2)]
    return [first[k] + sign * swapped(second[k]) for k in range(2)]


def mix_kernel(received, weight, x_table, out, spectra_out, real, imag):
    low = lane_index((64, 128)) < MODES
    sign = jnp.where(low, -1.0, 1.0).astype(F32)
    for k, spectra in enumerate(gather_spectra(received, x_table, sign)):
        spectra_out[k] = spectra
        other = swapped(spectra)
        real[k] = jnp.where(low, spectra, other)
        imag[k] = jnp.where(low, other, spectra)
    parts = [[], []]
    for group in range(8):
        a, j = group // 4, group % 4
        first = jnp.zeros((WIDTH, 128), F32)
        second = jnp.zeros((WIDTH, 128), F32)
        for i in range(WIDTH):
            k, row = i // HALF, group * HALF + i % HALF
            tile = weight[a, j, i].astype(F32)
            first = first + tile * real[k, row : row + 1, :]
            second = second + tile * imag[k, row : row + 1, :]
        mixed = first + sign[:WIDTH] * swapped(second)
        parts[0].append(mixed[:HALF])
        parts[1].append(mixed[HALF:])
    both = []
    for k in range(2):
        mixed = jnp.concatenate(parts[k], axis=0)
        both += [mixed, -sign * swapped(mixed)]
    high, low = split(jnp.concatenate(both, axis=0))
    result = dot(x_table[...], jnp.concatenate([high, high], axis=1), NT) + dot(x_table[:, 0:128], low, NT)
    for q in range(PLANES):
        for k in range(2):
            place = (2 * q + k) * 32
            out[place : place + 32, :] = result[q * 32 : q * 32 + 32, k * 128 : k * 128 + 128]


def outer_kernel(place, received, spectra_in, x_table, out, real, imag):
    low = lane_index((64, 128)) < MODES
    sign = jnp.where(low, -1.0, 1.0).astype(F32)
    row = lax.broadcasted_iota(jnp.int32, (64, 128), 0)
    zero_mode = jnp.logical_and((row // HALF) % 4 == 0, place[2] == 0)
    doubling = jnp.where(zero_mode, 1.0, 2.0).astype(F32)
    grads = [doubling * g for g in gather_spectra(received, x_table, sign)]
    turned = [-sign * swapped(g) for g in grads]
    for k in range(2):
        spectra = spectra_in[k]
        other = swapped(spectra)
        real[k] = jnp.where(low, spectra, other)
        imag[k] = jnp.where(low, other, spectra)
    for group in range(8):
        a, j = group // 4, group % 4
        rows = slice(group * HALF, group * HALF + HALF)
        straight = jnp.concatenate([grads[0][rows], grads[1][rows]], axis=0)
        crossed = jnp.concatenate([turned[0][rows], turned[1][rows]], axis=0)
        for i in range(WIDTH):
            k, line = i // HALF, group * HALF + i % HALF
            value = straight * real[k, line : line + 1, :] + crossed * imag[k, line : line + 1, :]
            out[a, j, i] = value.astype(BF16)


def beside_z(value, lane):
    left = jnp.where(lane == 0, 0.0, pltpu.roll(value, 1, 1))
    return left + jnp.where(lane == GRID - 1, 0.0, pltpu.roll(value, GRID - 1, 1))


def beside_y(value):
    return pltpu.roll(value, 1, 0) + pltpu.roll(value, 23, 0)


def edge_kernel(received, field, wide, lower, upper):
    lane = lane_index((24, GRID))
    for q in range(PLANES):
        for h in range(2):
            rows, lanes = slice(24 * h, 24 * h + 24), slice(128 * h, 128 * h + 128)
            wide[q, :, lanes] = received[2 * q, rows, :] + received[2 * q + 1, rows, :]
    for ref, edge, inner in ((lower, 0, 1), (upper, PLANES - 1, PLANES - 2)):
        value = wide[edge]
        rest = 6.0 * value - (wide[inner] + beside_y(value) + beside_z(value, lane))
        rest = rest[4:20] - field[edge]
        ref[0:24, :] = value[:, 0:128]
        ref[24:48, :] = value[:, 128:256]
        ref[48:64, :] = rest[:, 0:128]
        ref[64:80, :] = rest[:, 128:256]


def stencil_kernel(place, wide, before, after, field, residual, adjoint, sources):
    row_place, col_place = place[1], place[2]
    row = lax.broadcasted_iota(jnp.int32, (24, GRID), 0)
    lane = lane_index((24, GRID))
    first_row = jnp.where(col_place == 0, 4, 3)
    last_row = jnp.where(col_place == COLS - 1, 19, 20)
    inside = jnp.logical_and(row >= first_row, row <= last_row)
    beyond = [jnp.concatenate([ref[0:24, :], ref[24:48, :]], axis=1) for ref in (before, after)]
    values = [beyond[0]] + [wide[q] for q in range(PLANES)] + [beyond[1]]
    rest = []
    for q in range(PLANES):
        sources[q] = jnp.zeros((24, GRID), F32)
        sources[q, 4:20, :] = field[q]
        sources[q, 3:4, :] = wide[q, 1:2, :]
        sources[q, 20:21, :] = wide[q, 22:23, :]
        centre = values[q + 1]
        near = values[q] + values[q + 2] + beside_y(centre) + beside_z(centre, lane)
        value = jnp.where(inside, 6.0 * centre - near - sources[q], 0.0)
        rest.append(value)
        residual[q] = value[4:20]
    outer = []
    for ref, edge, some in ((before, 0, row_place > 0), (after, PLANES - 1, row_place < ROWS - 1)):
        part = jnp.concatenate([ref[48:64, :], ref[64:80, :]], axis=1) - wide[edge, 4:20, :]
        outer.append(jnp.where(some, part, 0.0))
    for q in range(PLANES):
        low = outer[0] if q == 0 else rest[q - 1][4:20]
        high = outer[1] if q == PLANES - 1 else rest[q + 1][4:20]
        near = (beside_y(rest[q]) + beside_z(rest[q], lane))[4:20]
        value = 6.0 * rest[q][4:20] - (low + high + near)
        adjoint[2 * q] = value
        adjoint[2 * q + 1] = value


def call(kernel, operands, scalars, outputs, scratch, flops=0, far=0):
    many = isinstance(outputs, list)
    vmem = pl.BlockSpec(memory_space=pltpu.VMEM)
    smem = pl.BlockSpec(memory_space=pltpu.SMEM)
    hbm = pl.BlockSpec(memory_space=pltpu.HBM)
    cost = pl.CostEstimate(flops=flops, bytes_accessed=4 << 20, transcendentals=flops // 16)
    return pl.pallas_call(
        kernel,
        in_specs=[smem] * len(scalars) + [vmem] * (len(operands) - far) + [hbm] * far,
        out_specs=[vmem] * len(outputs) if many else vmem,
        out_shape=outputs,
        scratch_shapes=scratch,
        compiler_params=pltpu.CompilerParams(vmem_limit_bytes=VMEM_LIMIT),
        cost_estimate=cost if flops else None,
    )(*scalars, *operands)


def exchange(value, axes):
    return lax.all_to_all(value, axes, split_axis=0, concat_axis=0, tiled=True)


def shape(*sizes):
    return jax.ShapeDtypeStruct(sizes, F32)


def shards(right_side, lift_scale, lift_shift, spectral_weight, local_weight, local_bias, readout):
    z_forward, z_inverse, y_table, x_table = tables()
    place = jnp.stack([lax.axis_index("core"), lax.axis_index(ROW), lax.axis_index(COL)]).astype(jnp.int32)
    params = jnp.concatenate([jnp.stack([lift_scale, lift_shift, local_bias, readout]), local_weight], axis=0)
    everywhere = COL + ROW
    field = right_side[0]
    copies = pltpu.SemaphoreType.DMA((2,))

    spread = call(spread_kernel, (field,), (), shape(PLANES, 2, COLS, GRID), [copies], far=1)
    plane = exchange(spread.reshape(COLS, COLS, GRID), COL).reshape(GRID, GRID)
    line_scratch = pltpu.VMEM((MODES, HALF, 2 * GRID), F32)
    plane_scratch = [
        pltpu.VMEM((GRID, GRID), F32),
        pltpu.VMEM((GRID, GRID), BF16),
        pltpu.VMEM((GRID, GRID), BF16),
        line_scratch,
    ]
    lifted = call(
        lift_kernel,
        (plane, z_forward, y_table),
        (place, params),
        shape(512, 128),
        plane_scratch + [pltpu.VMEM(z_forward.shape, BF16), pltpu.VMEM(y_table.shape, BF16), copies],
        far=2,
    )
    lifted = exchange(lifted, everywhere)
    local = call(
        local_kernel,
        (plane,),
        (place, params),
        shape(HALF, GRID, GRID),
        [pltpu.VMEM((GRID, GRID), F32)],
        flops=1 << 27,
    )
    pair = pltpu.VMEM((2, 64, 128), F32)
    mixed, spectra = call(
        mix_kernel, (lifted, spectral_weight, x_table), (), [shape(512, 128), shape(2, 64, 128)], [pair, pair]
    )
    mixed = exchange(mixed, everywhere)
    message, slope = call(
        inverse_kernel,
        (mixed, local, plane, z_inverse, y_table),
        (place, params),
        [shape(COLS, 48, 128), shape(HALF, GRID, GRID)],
        [
            pltpu.VMEM((128, 512), F32),
            line_scratch,
            pltpu.VMEM((GRID, GRID), F32),
            pltpu.VMEM((GRID, GRID), F32),
            pltpu.VMEM((GRID + 8, GRID), F32),
        ],
    )
    message = exchange(message, COL)
    wide, lower, upper = call(
        edge_kernel, (message, field), (), [shape(PLANES, 24, GRID), shape(80, 128), shape(80, 128)], []
    )
    forward = [(i, i + 1) for i in range(ROWS - 1)]
    backward = [(target, source) for source, target in forward]
    before = lax.ppermute(upper, ROW, forward)
    after = lax.ppermute(lower, ROW, backward)
    residual, adjoint = call(
        stencil_kernel,
        (wide, before, after, field),
        (place,),
        [shape(PLANES, COLS, GRID), shape(2 * PLANES, COLS, GRID)],
        [pltpu.VMEM((PLANES, 24, GRID), F32)],
    )
    adjoint = exchange(adjoint, COL).reshape(GRID, GRID)
    grads = call(grad_kernel, (adjoint, slope, z_forward, y_table), (), shape(512, 128), plane_scratch)
    grads = exchange(grads, everywhere)
    spectral_grad = call(
        outer_kernel,
        (grads, spectra, x_table),
        (place,),
        jax.ShapeDtypeStruct(spectral_weight.shape, BF16),
        [pair, pair],
    )
    return residual[None], spectral_grad


def solution(mesh):
    fine = Mesh(mesh.devices.reshape(8, 4, 2, 4, 2), ROW + COL)
    in_specs = (P(None, ROW, COL, None), P(), P(), P(ROW, COL, None, None, None), P(), P(), P())
    out_specs = (P(None, ROW, COL, None), P(ROW, COL, None, None, None))
    return jax.shard_map(shards, mesh=fine, in_specs=in_specs, out_specs=out_specs, check_vma=False)
```

```python
import math

import jax
import jax.numpy as jnp
import numpy as np
from jax import lax
from jax.experimental import pallas as pl
from jax.experimental.pallas import tpu as pltpu
from jax.sharding import Mesh
from jax.sharding import PartitionSpec as P

MODES = 64
GRID = 256
WIDTH = 16
HALF = 8
ROWS = 32
PLANES = 8
COLS = 16
ROW = ("y", "zh")
COL = ("zl", "x", "core")
F32 = jnp.float32
BF16 = jnp.bfloat16
VMEM_LIMIT = 40 * 1024 * 1024


def halves(table):
    high = table.astype(jnp.bfloat16)
    low = (table - high.astype(np.float64)).astype(jnp.bfloat16)
    return high, low


def wave(frequencies, points):
    phase = (np.outer(frequencies, points) % GRID) * (2.0 * math.pi / GRID)
    return np.cos(phase) / 16.0, np.sin(phase) / 16.0


def tables():
    points = np.arange(GRID)
    cos_z, sin_z = wave(np.arange(MODES), points)
    z_forward = np.concatenate(halves(np.concatenate([cos_z, -sin_z], axis=0)), axis=0)
    weight = np.where(np.arange(MODES) == 0, 1.0, 2.0)[:, None]
    high, low = halves(np.concatenate([cos_z * weight, -sin_z * weight], axis=0).T)
    z_inverse = np.block([[high, high], [low, np.zeros_like(low)]])
    ky = np.array([2 * r + a - MODES // 2 for a in range(2) for r in range(ROWS)])
    cos_y, sin_y = wave(ky, points)
    y_table = np.concatenate(
        [np.concatenate([cos_y, sin_y], axis=1), np.concatenate([-sin_y, cos_y], axis=1)], axis=0
    )
    y_table = np.concatenate(halves(y_table), axis=0)
    places = np.array([8 * r + q for q in range(PLANES) for r in range(ROWS)])
    cos_x, sin_x = wave(np.arange(MODES) - MODES // 2, places)
    x_table = np.concatenate(halves(np.concatenate([cos_x.T, -sin_x.T], axis=1)), axis=1)
    return z_forward, z_inverse, y_table, x_table


def split(value):
    high = value.astype(BF16)
    return high, (value - high.astype(F32)).astype(BF16)


def dot(left, right, dims):
    return lax.dot_general(left, right, (dims, ((), ())), preferred_element_type=F32)


NN = ((1,), (0,))
NT = ((1,), (1,))


ROOT = math.sqrt(2.0 / math.pi)
CUBE = 0.044715


def gelu(value):
    inner = value * (ROOT + (ROOT * CUBE) * (value * value))
    half = 0.5 * value
    return half + half * jnp.tanh(inner)


def gelu_slope(value):
    square = value * value
    bent = jnp.tanh(value * (ROOT + (ROOT * CUBE) * square))
    slope = ROOT + (3.0 * ROOT * CUBE) * square
    return 0.5 + 0.5 * bent + (0.5 * value) * ((1.0 - bent * bent) * slope)


def bent_half(half):
    return half * jnp.tanh(half * (2.0 * ROOT + (8.0 * ROOT * CUBE) * (half * half)))


def lift(field, half_scale, half_shift):
    scaled = half_scale * field
    return (scaled + scaled) + (bent_half(half_shift + scaled) - bent_half(half_shift - scaled))


def lane_index(shape):
    return lax.broadcasted_iota(jnp.int32, shape, len(shape) - 1)


def swapped(value):
    return pltpu.roll(value, MODES, 1)


def plane_forward(fill, z_table, y_table, stage_high, stage_low, lines, out, ready=lambda n: None):
    for channel in range(HALF):
        fill(channel, stage_high, stage_low)
        if channel == 0:
            ready(0)
        z = dot(z_table[...], stage_high[...], NN)
        z = z[:128] + z[128:] + dot(z_table[0:128, :], stage_low[...], NN)
        lines[:, channel, 0:GRID] = z[:MODES]
        lines[:, channel, GRID:] = z[MODES:]
    ready(1)
    high, low = split(lines[...].reshape(MODES * HALF, 2 * GRID))
    spectrum = dot(y_table[...], high, NT)
    spectrum = spectrum[:128] + spectrum[128:] + dot(y_table[0:128, :], low, NT)
    lane = lane_index((ROWS, 128)) // 32
    for tile in range(4):
        parts = [spectrum[b * 32 : b * 32 + 32, tile * 128 : tile * 128 + 128] for b in range(4)]
        for e in range(4):
            total = None
            for b in range(4):
                turn = ((b - e) % 4) * 32
                moved = pltpu.roll(parts[b], turn, 1) if turn else parts[b]
                total = moved if total is None else jnp.where(lane == b, moved, total)
            column = 4 * tile + e
            out[column * 32 : column * 32 + 32, :] = total


def lift_kernel(place, params, plane, z_far, y_far, out, turned, high, low, lines, z_table, y_table, sems):
    z_copy = pltpu.make_async_copy(z_far, z_table, sems.at[0])
    y_copy = pltpu.make_async_copy(y_far, y_table, sems.at[1])
    z_copy.start()
    y_copy.start()
    core = place[0]
    turned[...] = plane[...].T

    def fill(channel, stage_high, stage_low):
        gain, offset = 0.5 * params[0, core * HALF + channel], 0.5 * params[1, core * HALF + channel]
        for t in range(8):
            rows = slice(32 * t, 32 * t + 32)
            stage_high[rows, :], stage_low[rows, :] = split(lift(turned[rows, :], gain, offset))

    plane_forward(fill, z_table, y_table, high, low, lines, out, lambda n: (z_copy, y_copy)[n].wait())


def grad_kernel(adjoint, slope, z_table, y_table, out, turned, high, low, lines):
    turned[...] = adjoint[...].T

    def fill(channel, stage_high, stage_low):
        for t in range(8):
            rows = slice(32 * t, 32 * t + 32)
            stage_high[rows, :], stage_low[rows, :] = split(turned[rows, :] * slope[channel, rows, :])

    plane_forward(fill, z_table, y_table, high, low, lines, out)


def spread_kernel(field, out, sems):
    copies = [pltpu.make_async_copy(field, out.at[:, k], sems.at[k]) for k in range(2)]
    for copy in copies:
        copy.start()
    for copy in copies:
        copy.wait()


def local_kernel(place, params, plane, out, turned):
    first = place[0] * HALF
    turned[...] = plane[...].T

    def step(t, carry):
        rows = pl.ds(pl.multiple_of(t * 8, 8), 8)
        field = turned[rows, :]
        sums = [jnp.full((8, GRID), params[2, first + o], F32) for o in range(HALF)]
        for i in range(WIDTH):
            lifted = lift(field, 0.5 * params[0, i], 0.5 * params[1, i])
            sums = [sums[o] + params[4 + i, first + o] * lifted for o in range(HALF)]
        for o in range(HALF):
            out[o, rows, :] = sums[o]
        return carry

    lax.fori_loop(0, GRID // 8, step, 0)


def inverse_kernel(
    place, params, received, local, plane, z_table, y_table, out, preact, grid, lines, spectral, total, padded
):
    core = place[0]
    lane = lane_index((ROWS, 128)) // 32
    for tile in range(4):
        parts = [received[(4 * tile + e) * 32 : (4 * tile + e) * 32 + 32, :] for e in range(4)]
        for b in range(4):
            whole = None
            for e in range(4):
                turn = ((e - b) % 4) * 32
                moved = pltpu.roll(parts[e], turn, 1) if turn else parts[e]
                whole = moved if whole is None else jnp.where(lane == e, moved, whole)
            grid[b * 32 : b * 32 + 32, tile * 128 : tile * 128 + 128] = whole
    high, low = split(grid[...].T)
    modes = dot(jnp.concatenate([high, high], axis=1), y_table[...], NN) + dot(low, y_table[0:128, :], NN)
    lines[...] = modes.reshape(MODES, HALF, 2 * GRID)
    for o in range(HALF):
        modes = jnp.concatenate([lines[:, o, 0:GRID], lines[:, o, GRID:]], axis=0)
        product = dot(z_table[...], jnp.concatenate(split(modes), axis=0), NN)
        spectral[...] = product[:GRID] + product[GRID:]
        read = params[3, core * HALF + o]
        for t in range(8):
            rows = slice(32 * t, 32 * t + 32)
            value = spectral[rows, :] + local[o, rows, :]
            preact[o, rows, :] = value
            if o == 0:
                total[rows, :] = read * gelu(value)
            else:
                total[rows, :] += read * gelu(value)
    padded[0:8, :] = jnp.zeros((8, GRID), F32)
    padded[256:264, :] = jnp.zeros((8, GRID), F32)
    padded[4:260, :] = total[...].T
    keep = jnp.where(core == 0, 1.0, 0.0).astype(F32)
    blank = jnp.zeros((1, GRID), F32)
    row = lax.broadcasted_iota(jnp.int32, (24, GRID), 0)
    for c in range(COLS):
        before = plane[16 * c - 1 : 16 * c, :] * keep if c > 0 else blank
        after = plane[16 * c + 16 : 16 * c + 17, :] * keep if c < COLS - 1 else blank
        block = padded[16 * c : 16 * c + 24, :]
        block = jnp.where(row == 1, before, jnp.where(row == 22, after, block))
        out[c, 0:24, :] = block[:, 0:128]
        out[c, 24:48, :] = block[:, 128:256]


def slope_kernel(place, params, preact, out):
    for o in range(HALF):
        read = params[3, place[0] * HALF + o]
        for t in range(8):
            rows = slice(32 * t, 32 * t + 32)
            out[o, rows, :] = read * gelu_slope(preact[o, rows, :])


def gather_spectra(received, x_table, sign):
    lines = []
    for k in range(2):
        parts = [received[(2 * q + k) * 32 : (2 * q + k) * 32 + 32, :] for q in range(PLANES)]
        lines.append(jnp.concatenate(parts, axis=0).T)
    product = dot(jnp.concatenate(split(jnp.concatenate(lines, axis=0)), axis=0), x_table[...], NN)
    product = product[:, :128] + product[:, 128:]
    product = product[:256] + product[256:]
    first = [product[128 * k : 128 * k + 64] for k in range(2)]
    second = [product[128 * k + 64 : 128 * k + 128] for k in range(2)]
    return [first[k] + sign * swapped(second[k]) for k in range(2)]


def mix_kernel(received, weight, x_table, out, spectra_out, real, imag):
    low = lane_index((64, 128)) < MODES
    sign = jnp.where(low, -1.0, 1.0).astype(F32)
    for k, spectra in enumerate(gather_spectra(received, x_table, sign)):
        spectra_out[k] = spectra
        other = swapped(spectra)
        real[k] = jnp.where(low, spectra, other)
        imag[k] = jnp.where(low, other, spectra)
    parts = [[], []]
    for group in range(8):
        a, j = group // 4, group % 4
        first = jnp.zeros((WIDTH, 128), F32)
        second = jnp.zeros((WIDTH, 128), F32)
        for i in range(WIDTH):
            k, row = i // HALF, group * HALF + i % HALF
            tile = weight[a, j, i].astype(F32)
            first = first + tile * real[k, row : row + 1, :]
            second = second + tile * imag[k, row : row + 1, :]
        mixed = first + sign[:WIDTH] * swapped(second)
        parts[0].append(mixed[:HALF])
        parts[1].append(mixed[HALF:])
    both = []
    for k in range(2):
        mixed = jnp.concatenate(parts[k], axis=0)
        both += [mixed, -sign * swapped(mixed)]
    high, low = split(jnp.concatenate(both, axis=0))
    result = dot(x_table[...], jnp.concatenate([high, high], axis=1), NT) + dot(x_table[:, 0:128], low, NT)
    for q in range(PLANES):
        for k in range(2):
            place = (2 * q + k) * 32
            out[place : place + 32, :] = result[q * 32 : q * 32 + 32, k * 128 : k * 128 + 128]


def outer_kernel(place, received, spectra_in, x_table, out, real, imag, stage, sems):
    low = lane_index((64, 128)) < MODES
    sign = jnp.where(low, -1.0, 1.0).astype(F32)
    row = lax.broadcasted_iota(jnp.int32, (64, 128), 0)
    zero_mode = jnp.logical_and((row // HALF) % 4 == 0, place[2] == 0)
    doubling = jnp.where(zero_mode, 1.0, 2.0).astype(F32)
    grads = [doubling * g for g in gather_spectra(received, x_table, sign)]
    turned = [-sign * swapped(g) for g in grads]
    for k in range(2):
        spectra = spectra_in[k]
        other = swapped(spectra)
        real[k] = jnp.where(low, spectra, other)
        imag[k] = jnp.where(low, other, spectra)
    copies = []
    for group in range(8):
        a, j = group // 4, group % 4
        rows = slice(group * HALF, group * HALF + HALF)
        straight = jnp.concatenate([grads[0][rows], grads[1][rows]], axis=0)
        crossed = jnp.concatenate([turned[0][rows], turned[1][rows]], axis=0)
        for i in range(WIDTH):
            k, line = i // HALF, group * HALF + i % HALF
            value = straight * real[k, line : line + 1, :] + crossed * imag[k, line : line + 1, :]
            stage[a, j, i] = value.astype(BF16)
        copies.append(pltpu.make_async_copy(stage.at[a, j], out.at[a, j], sems.at[group]))
        copies[-1].start()
    for copy in copies:
        copy.wait()


def beside_z(value, lane):
    left = jnp.where(lane == 0, 0.0, pltpu.roll(value, 1, 1))
    return left + jnp.where(lane == GRID - 1, 0.0, pltpu.roll(value, GRID - 1, 1))


def beside_y(value):
    return pltpu.roll(value, 1, 0) + pltpu.roll(value, 23, 0)


def edge_kernel(received, field, wide, lower, upper):
    lane = lane_index((24, GRID))
    for q in range(PLANES):
        for h in range(2):
            rows, lanes = slice(24 * h, 24 * h + 24), slice(128 * h, 128 * h + 128)
            wide[q, :, lanes] = received[2 * q, rows, :] + received[2 * q + 1, rows, :]
    for ref, edge, inner in ((lower, 0, 1), (upper, PLANES - 1, PLANES - 2)):
        value = wide[edge]
        rest = 6.0 * value - (wide[inner] + beside_y(value) + beside_z(value, lane))
        rest = rest[4:20] - field[edge]
        ref[0:24, :] = value[:, 0:128]
        ref[24:48, :] = value[:, 128:256]
        ref[48:64, :] = rest[:, 0:128]
        ref[64:80, :] = rest[:, 128:256]


def inside_rows(col_place):
    row = lax.broadcasted_iota(jnp.int32, (24, GRID), 0)
    first_row = jnp.where(col_place == 0, 4, 3)
    last_row = jnp.where(col_place == COLS - 1, 19, 20)
    return jnp.logical_and(row >= first_row, row <= last_row)


def inner_kernel(place, wide, field, rest, sources):
    lane = lane_index((24, GRID))
    inside = inside_rows(place[2])
    for q in range(PLANES):
        sources[q] = jnp.zeros((24, GRID), F32)
        sources[q, 4:20, :] = field[q]
        sources[q, 3:4, :] = wide[q, 1:2, :]
        sources[q, 20:21, :] = wide[q, 22:23, :]
        centre = wide[q]
        near = beside_y(centre) + beside_z(centre, lane) + sources[q]
        if q > 0:
            near = near + wide[q - 1]
        if q < PLANES - 1:
            near = near + wide[q + 1]
        rest[q] = jnp.where(inside, 6.0 * centre - near, 0.0)


def stencil_kernel(place, rest, wide, before, after, ends, adjoint):
    row_place = place[1]
    lane = lane_index((24, GRID))
    inside = inside_rows(place[2])
    values = [rest[q] for q in range(PLANES)]
    outer = []
    for n, ref, edge, some in ((0, before, 0, row_place > 0), (1, after, PLANES - 1, row_place < ROWS - 1)):
        beyond = jnp.concatenate([ref[0:24, :], ref[24:48, :]], axis=1)
        values[edge] = values[edge] - jnp.where(inside, beyond, 0.0)
        ends[n] = values[edge][4:20]
        part = jnp.concatenate([ref[48:64, :], ref[64:80, :]], axis=1) - wide[edge, 4:20, :]
        outer.append(jnp.where(some, part, 0.0))
    for q in range(PLANES):
        low = outer[0] if q == 0 else values[q - 1][4:20]
        high = outer[1] if q == PLANES - 1 else values[q + 1][4:20]
        near = (beside_y(values[q]) + beside_z(values[q], lane))[4:20]
        value = 6.0 * values[q][4:20] - (low + high + near)
        adjoint[2 * q] = value
        adjoint[2 * q + 1] = value


def residual_kernel(rest, ends, out):
    for q in range(PLANES):
        out[q] = ends[0] if q == 0 else ends[1] if q == PLANES - 1 else rest[q, 4:20, :]


def call(kernel, operands, scalars, outputs, scratch, flops=0, far=0, far_out=False):
    many = isinstance(outputs, list)
    vmem = pl.BlockSpec(memory_space=pltpu.VMEM)
    smem = pl.BlockSpec(memory_space=pltpu.SMEM)
    hbm = pl.BlockSpec(memory_space=pltpu.HBM)
    place_out = hbm if far_out else vmem
    operands = list(operands)
    for n in range(len(operands) - far, len(operands)):
        operands[n] = pltpu.with_memory_space_constraint(operands[n], pltpu.HBM)
    cost = pl.CostEstimate(flops=flops, bytes_accessed=4 << 20, transcendentals=flops // 16)
    return pl.pallas_call(
        kernel,
        in_specs=[smem] * len(scalars) + [vmem] * (len(operands) - far) + [hbm] * far,
        out_specs=[place_out] * len(outputs) if many else place_out,
        out_shape=outputs,
        scratch_shapes=scratch,
        compiler_params=pltpu.CompilerParams(vmem_limit_bytes=VMEM_LIMIT),
        cost_estimate=cost if flops else None,
    )(*scalars, *operands)


def exchange(value, axes):
    return lax.all_to_all(value, axes, split_axis=0, concat_axis=0, tiled=True)


def shape(*sizes):
    return jax.ShapeDtypeStruct(sizes, F32)


def shards(right_side, lift_scale, lift_shift, spectral_weight, local_weight, local_bias, readout):
    z_forward, z_inverse, y_table, x_table = tables()
    place = jnp.stack([lax.axis_index("core"), lax.axis_index(ROW), lax.axis_index(COL)]).astype(jnp.int32)
    params = jnp.concatenate([jnp.stack([lift_scale, lift_shift, local_bias, readout]), local_weight], axis=0)
    everywhere = COL + ROW
    field = right_side[0]
    copies = pltpu.SemaphoreType.DMA((2,))

    spread = call(spread_kernel, (field,), (), shape(PLANES, 2, COLS, GRID), [copies], far=1)
    plane = exchange(spread.reshape(COLS, COLS, GRID), COL).reshape(GRID, GRID)
    line_scratch = pltpu.VMEM((MODES, HALF, 2 * GRID), F32)
    plane_scratch = [
        pltpu.VMEM((GRID, GRID), F32),
        pltpu.VMEM((GRID, GRID), BF16),
        pltpu.VMEM((GRID, GRID), BF16),
        line_scratch,
    ]
    lifted = call(
        lift_kernel,
        (plane, z_forward, y_table),
        (place, params),
        shape(512, 128),
        plane_scratch + [pltpu.VMEM(z_forward.shape, BF16), pltpu.VMEM(y_table.shape, BF16), copies],
        far=2,
    )
    lifted = exchange(lifted, everywhere)
    local = call(
        local_kernel,
        (plane,),
        (place, params),
        shape(HALF, GRID, GRID),
        [pltpu.VMEM((GRID, GRID), F32)],
        flops=1 << 27,
    )
    pair = pltpu.VMEM((2, 64, 128), F32)
    mixed, spectra = call(
        mix_kernel, (lifted, spectral_weight, x_table), (), [shape(512, 128), shape(2, 64, 128)], [pair, pair]
    )
    mixed = exchange(mixed, everywhere)
    message, preact = call(
        inverse_kernel,
        (mixed, local, plane, z_inverse, y_table),
        (place, params),
        [shape(COLS, 48, 128), shape(HALF, GRID, GRID)],
        [
            pltpu.VMEM((128, 512), F32),
            line_scratch,
            pltpu.VMEM((GRID, GRID), F32),
            pltpu.VMEM((GRID, GRID), F32),
            pltpu.VMEM((GRID + 8, GRID), F32),
        ],
    )
    message = exchange(message, COL)
    slope = call(
        slope_kernel, (preact,), (place, params), shape(HALF, GRID, GRID), [], flops=1 << 25
    )
    wide, lower, upper = call(
        edge_kernel, (message, field), (), [shape(PLANES, 24, GRID), shape(80, 128), shape(80, 128)], []
    )
    forward = [(i, i + 1) for i in range(ROWS - 1)]
    backward = [(target, source) for source, target in forward]
    before = lax.ppermute(upper, ROW, forward)
    after = lax.ppermute(lower, ROW, backward)
    rest = call(
        inner_kernel,
        (wide, field),
        (place,),
        shape(PLANES, 24, GRID),
        [pltpu.VMEM((PLANES, 24, GRID), F32)],
        flops=1 << 22,
    )
    ends, adjoint = call(
        stencil_kernel,
        (rest, wide, before, after),
        (place,),
        [shape(2, COLS, GRID), shape(2 * PLANES, COLS, GRID)],
        [],
    )
    residual = call(residual_kernel, (rest, ends), (), shape(PLANES, COLS, GRID), [], flops=1 << 22)
    adjoint = exchange(adjoint, COL).reshape(GRID, GRID)
    grads = call(grad_kernel, (adjoint, slope, z_forward, y_table), (), shape(512, 128), plane_scratch)
    grads = exchange(grads, everywhere)
    spectral_grad = call(
        outer_kernel,
        (grads, spectra, x_table),
        (place,),
        jax.ShapeDtypeStruct(spectral_weight.shape, BF16),
        [pair, pair, pltpu.VMEM(spectral_weight.shape, BF16), pltpu.SemaphoreType.DMA((8,))],
        far_out=True,
    )
    return residual[None], spectral_grad


def solution(mesh):
    fine = Mesh(mesh.devices.reshape(8, 4, 2, 4, 2), ROW + COL)
    in_specs = (P(None, ROW, COL, None), P(), P(), P(ROW, COL, None, None, None), P(), P(), P())
    out_specs = (P(None, ROW, COL, None), P(ROW, COL, None, None, None))
    return jax.shard_map(shards, mesh=fine, in_specs=in_specs, out_specs=out_specs, check_vma=False)
```

```python
import math

import jax
import jax.numpy as jnp
import numpy as np
from jax import lax
from jax.experimental import pallas as pl
from jax.experimental.pallas import tpu as pltpu
from jax.sharding import Mesh
from jax.sharding import PartitionSpec as P

MODES = 64
GRID = 256
WIDTH = 16
HALF = 8
ROWS = 32
PLANES = 8
COLS = 16
ROW = ("y", "zh")
COL = ("zl", "x", "core")
F32 = jnp.float32
BF16 = jnp.bfloat16
VMEM_LIMIT = 40 * 1024 * 1024


def halves(table):
    high = table.astype(jnp.bfloat16)
    low = (table - high.astype(np.float64)).astype(jnp.bfloat16)
    return high, low


def wave(frequencies, points):
    phase = (np.outer(frequencies, points) % GRID) * (2.0 * math.pi / GRID)
    return np.cos(phase) / 16.0, np.sin(phase) / 16.0


def tables():
    points = np.arange(GRID)
    cos_z, sin_z = wave(np.arange(MODES), points)
    z_forward = np.concatenate(halves(np.concatenate([cos_z, -sin_z], axis=0)), axis=0)
    weight = np.where(np.arange(MODES) == 0, 1.0, 2.0)[:, None]
    high, low = halves(np.concatenate([cos_z * weight, -sin_z * weight], axis=0).T)
    z_inverse = np.block([[high, high], [low, np.zeros_like(low)]])
    ky = np.array([2 * r + a - MODES // 2 for a in range(2) for r in range(ROWS)])
    cos_y, sin_y = wave(ky, points)
    y_table = np.concatenate(
        [np.concatenate([cos_y, sin_y], axis=1), np.concatenate([-sin_y, cos_y], axis=1)], axis=0
    )
    y_table = np.concatenate(halves(y_table), axis=0)
    places = np.array([8 * r + q for q in range(PLANES) for r in range(ROWS)])
    cos_x, sin_x = wave(np.arange(MODES) - MODES // 2, places)
    x_table = np.concatenate(halves(np.concatenate([cos_x.T, -sin_x.T], axis=1)), axis=1)
    return z_forward, z_inverse, y_table, x_table


def split(value):
    high = value.astype(BF16)
    return high, (value - high.astype(F32)).astype(BF16)


def dot(left, right, dims):
    return lax.dot_general(left, right, (dims, ((), ())), preferred_element_type=F32)


NN = ((1,), (0,))
NT = ((1,), (1,))


ROOT = math.sqrt(2.0 / math.pi)
CUBE = 0.044715


def gelu(value):
    inner = value * (ROOT + (ROOT * CUBE) * (value * value))
    half = 0.5 * value
    return half + half * jnp.tanh(inner)


def gelu_both(value):
    square = value * value
    bent = jnp.tanh(value * (ROOT + (ROOT * CUBE) * square))
    slope = ROOT + (3.0 * ROOT * CUBE) * square
    cdf = 0.5 + 0.5 * bent
    return value * cdf, cdf + (0.5 * value) * ((1.0 - bent * bent) * slope)


def bent_half(half):
    return half * jnp.tanh(half * (2.0 * ROOT + (8.0 * ROOT * CUBE) * (half * half)))


def lift(field, half_scale, half_shift):
    scaled = half_scale * field
    return (scaled + scaled) + (bent_half(half_shift + scaled) - bent_half(half_shift - scaled))


def lane_index(shape):
    return lax.broadcasted_iota(jnp.int32, shape, len(shape) - 1)


def swapped(value):
    return pltpu.roll(value, MODES, 1)


def plane_forward(fill, z_table, y_table, stage_high, stage_low, lines, out):
    for channel in range(HALF):
        fill(channel, stage_high, stage_low)
        z = dot(z_table[...], stage_high[...], NN)
        z = z[:128] + z[128:] + dot(z_table[0:128, :], stage_low[...], NN)
        lines[:, channel, 0:GRID] = z[:MODES]
        lines[:, channel, GRID:] = z[MODES:]
    high, low = split(lines[...].reshape(MODES * HALF, 2 * GRID))
    spectrum = dot(y_table[...], high, NT)
    spectrum = spectrum[:128] + spectrum[128:] + dot(y_table[0:128, :], low, NT)
    lane = lane_index((ROWS, 128)) // 32
    for tile in range(4):
        parts = [spectrum[b * 32 : b * 32 + 32, tile * 128 : tile * 128 + 128] for b in range(4)]
        for e in range(4):
            total = None
            for b in range(4):
                turn = ((b - e) % 4) * 32
                moved = pltpu.roll(parts[b], turn, 1) if turn else parts[b]
                total = moved if total is None else jnp.where(lane == b, moved, total)
            column = 4 * tile + e
            out[column * 32 : column * 32 + 32, :] = total


def lift_kernel(place, params, plane, z_table, y_table, out, turned, high, low, lines):
    core = place[0]
    turned[...] = plane[...].T

    def fill(channel, stage_high, stage_low):
        gain, offset = 0.5 * params[0, core * HALF + channel], 0.5 * params[1, core * HALF + channel]
        for t in range(8):
            rows = slice(32 * t, 32 * t + 32)
            stage_high[rows, :], stage_low[rows, :] = split(lift(turned[rows, :], gain, offset))

    plane_forward(fill, z_table, y_table, high, low, lines, out)


def grad_kernel(adjoint, z_table, y_table, *refs):
    slope = refs[:HALF]
    out, turned, high, low, lines = refs[HALF:]
    turned[...] = adjoint[...].T

    def fill(channel, stage_high, stage_low):
        for t in range(8):
            rows = slice(32 * t, 32 * t + 32)
            stage_high[rows, :], stage_low[rows, :] = split(turned[rows, :] * slope[channel][rows, :])

    plane_forward(fill, z_table, y_table, high, low, lines, out)


def ready_kernel(z_far, y_far, z_table, y_table, sems):
    copies = [pltpu.make_async_copy(z_far, z_table, sems.at[0]), pltpu.make_async_copy(y_far, y_table, sems.at[1])]
    for copy in copies:
        copy.start()
    for copy in copies:
        copy.wait()


def spread_kernel(field, out, sems):
    copies = [pltpu.make_async_copy(field, out.at[:, k], sems.at[k]) for k in range(2)]
    for copy in copies:
        copy.start()
    for copy in copies:
        copy.wait()


def local_kernel(place, params, plane, margin, *refs):
    out, turned = refs[:HALF], refs[HALF]
    first = place[0] * HALF
    keep = jnp.where(place[0] == 0, 1.0, 0.0).astype(F32)
    turned[...] = plane[...].T
    margin[...] = jnp.zeros(margin.shape, F32)
    for c in range(1, COLS):
        margin[c : c + 1, :] = plane[16 * c - 1 : 16 * c, :] * keep
        margin[COLS + c - 1 : COLS + c, :] = plane[16 * c : 16 * c + 1, :] * keep

    def step(t, carry):
        rows = pl.ds(pl.multiple_of(t * 16, 16), 16)
        field = turned[rows, :]
        sums = [jnp.full((16, GRID), params[2, first + o], F32) for o in range(HALF)]
        for i in range(WIDTH):
            lifted = lift(field, 0.5 * params[0, i], 0.5 * params[1, i])
            sums = [sums[o] + params[4 + i, first + o] * lifted for o in range(HALF)]
        for o in range(HALF):
            out[o][rows, :] = sums[o]
        return carry

    lax.fori_loop(0, GRID // 16, step, 0)


def inverse_kernel(place, params, received, margin, z_table, y_table, *refs):
    local, out, slope = refs[:HALF], refs[HALF], refs[HALF + 1 : 2 * HALF + 1]
    grid, lines, spectral, total, padded = refs[2 * HALF + 1 :]
    core = place[0]
    lane = lane_index((ROWS, 128)) // 32
    for tile in range(4):
        parts = [received[(4 * tile + e) * 32 : (4 * tile + e) * 32 + 32, :] for e in range(4)]
        for b in range(4):
            whole = None
            for e in range(4):
                turn = ((e - b) % 4) * 32
                moved = pltpu.roll(parts[e], turn, 1) if turn else parts[e]
                whole = moved if whole is None else jnp.where(lane == e, moved, whole)
            grid[b * 32 : b * 32 + 32, tile * 128 : tile * 128 + 128] = whole
    high, low = split(grid[...].T)
    modes = dot(jnp.concatenate([high, high], axis=1), y_table[...], NN) + dot(low, y_table[0:128, :], NN)
    lines[...] = modes.reshape(MODES, HALF, 2 * GRID)
    for o in range(HALF):
        modes = jnp.concatenate([lines[:, o, 0:GRID], lines[:, o, GRID:]], axis=0)
        product = dot(z_table[...], jnp.concatenate(split(modes), axis=0), NN)
        spectral[...] = product[:GRID] + product[GRID:]
        read = params[3, core * HALF + o]
        for t in range(8):
            rows = slice(32 * t, 32 * t + 32)
            value = spectral[rows, :] + local[o][rows, :]
            value, derivative = gelu_both(value)
            slope[o][rows, :] = read * derivative
            if o == 0:
                total[rows, :] = read * value
            else:
                total[rows, :] += read * value
    padded[0:8, :] = jnp.zeros((8, GRID), F32)
    padded[256:264, :] = jnp.zeros((8, GRID), F32)
    padded[4:260, :] = total[...].T
    row = lax.broadcasted_iota(jnp.int32, (24, GRID), 0)
    for c in range(COLS):
        before, after = margin[c : c + 1, :], margin[COLS + c : COLS + c + 1, :]
        block = padded[16 * c : 16 * c + 24, :]
        block = jnp.where(row == 1, before, jnp.where(row == 22, after, block))
        out[c, 0:24, :] = block[:, 0:128]
        out[c, 24:48, :] = block[:, 128:256]


def gather_spectra(received, x_table, sign):
    lines = []
    for k in range(2):
        parts = [received[(2 * q + k) * 32 : (2 * q + k) * 32 + 32, :] for q in range(PLANES)]
        lines.append(jnp.concatenate(parts, axis=0).T)
    product = dot(jnp.concatenate(split(jnp.concatenate(lines, axis=0)), axis=0), x_table[...], NN)
    product = product[:, :128] + product[:, 128:]
    product = product[:256] + product[256:]
    first = [product[128 * k : 128 * k + 64] for k in range(2)]
    second = [product[128 * k + 64 : 128 * k + 128] for k in range(2)]
    return [first[k] + sign * swapped(second[k]) for k in range(2)]


def mix_kernel(received, weight, x_table, out, spectra_out, real, imag):
    low = lane_index((64, 128)) < MODES
    sign = jnp.where(low, -1.0, 1.0).astype(F32)
    for k, spectra in enumerate(gather_spectra(received, x_table, sign)):
        spectra_out[k] = spectra
        other = swapped(spectra)
        real[k] = jnp.where(low, spectra, other)
        imag[k] = jnp.where(low, other, spectra)
    parts = [[], []]
    for group in range(8):
        a, j = group // 4, group % 4
        first = jnp.zeros((WIDTH, 128), F32)
        second = jnp.zeros((WIDTH, 128), F32)
        for i in range(WIDTH):
            k, row = i // HALF, group * HALF + i % HALF
            tile = weight[a, j, i].astype(F32)
            first = first + tile * real[k, row : row + 1, :]
            second = second + tile * imag[k, row : row + 1, :]
        mixed = first + sign[:WIDTH] * swapped(second)
        parts[0].append(mixed[:HALF])
        parts[1].append(mixed[HALF:])
    both = []
    for k in range(2):
        mixed = jnp.concatenate(parts[k], axis=0)
        both += [mixed, -sign * swapped(mixed)]
    high, low = split(jnp.concatenate(both, axis=0))
    result = dot(x_table[...], jnp.concatenate([high, high], axis=1), NT) + dot(x_table[:, 0:128], low, NT)
    for q in range(PLANES):
        for k in range(2):
            place = (2 * q + k) * 32
            out[place : place + 32, :] = result[q * 32 : q * 32 + 32, k * 128 : k * 128 + 128]


def outer_kernel(place, received, spectra_in, x_table, out, real, imag, stage, sems):
    low = lane_index((64, 128)) < MODES
    sign = jnp.where(low, -1.0, 1.0).astype(F32)
    row = lax.broadcasted_iota(jnp.int32, (64, 128), 0)
    zero_mode = jnp.logical_and((row // HALF) % 4 == 0, place[2] == 0)
    doubling = jnp.where(zero_mode, 1.0, 2.0).astype(F32)
    grads = [doubling * g for g in gather_spectra(received, x_table, sign)]
    turned = [-sign * swapped(g) for g in grads]
    for k in range(2):
        spectra = spectra_in[k]
        other = swapped(spectra)
        real[k] = jnp.where(low, spectra, other)
        imag[k] = jnp.where(low, other, spectra)
    copies = []
    for group in range(8):
        a, j = group // 4, group % 4
        rows = slice(group * HALF, group * HALF + HALF)
        straight = jnp.concatenate([grads[0][rows], grads[1][rows]], axis=0)
        crossed = jnp.concatenate([turned[0][rows], turned[1][rows]], axis=0)
        for i in range(WIDTH):
            k, line = i // HALF, group * HALF + i % HALF
            value = straight * real[k, line : line + 1, :] + crossed * imag[k, line : line + 1, :]
            stage[a, j, i] = value.astype(BF16)
        copies.append(pltpu.make_async_copy(stage.at[a, j], out.at[a, j], sems.at[group]))
        copies[-1].start()
    for copy in copies:
        copy.wait()


def beside_z(value, lane):
    left = jnp.where(lane == 0, 0.0, pltpu.roll(value, 1, 1))
    return left + jnp.where(lane == GRID - 1, 0.0, pltpu.roll(value, GRID - 1, 1))


def beside_y(value):
    return pltpu.roll(value, 1, 0) + pltpu.roll(value, 23, 0)


def edge_kernel(received, field, wide, lower, upper):
    lane = lane_index((24, GRID))
    for q in range(PLANES):
        for h in range(2):
            rows, lanes = slice(24 * h, 24 * h + 24), slice(128 * h, 128 * h + 128)
            wide[q, :, lanes] = received[2 * q, rows, :] + received[2 * q + 1, rows, :]
    for ref, edge, inner in ((lower, 0, 1), (upper, PLANES - 1, PLANES - 2)):
        value = wide[edge]
        rest = 6.0 * value - (wide[inner] + beside_y(value) + beside_z(value, lane))
        rest = rest[4:20] - field[edge]
        ref[0:24, :] = value[:, 0:128]
        ref[24:48, :] = value[:, 128:256]
        ref[48:64, :] = rest[:, 0:128]
        ref[64:80, :] = rest[:, 128:256]


def inside_rows(col_place):
    row = lax.broadcasted_iota(jnp.int32, (24, GRID), 0)
    first_row = jnp.where(col_place == 0, 4, 3)
    last_row = jnp.where(col_place == COLS - 1, 19, 20)
    return jnp.logical_and(row >= first_row, row <= last_row)


def inner_kernel(place, wide, field, rest, sources):
    lane = lane_index((24, GRID))
    inside = inside_rows(place[2])
    for q in range(PLANES):
        sources[q] = jnp.zeros((24, GRID), F32)
        sources[q, 4:20, :] = field[q]
        sources[q, 3:4, :] = wide[q, 1:2, :]
        sources[q, 20:21, :] = wide[q, 22:23, :]
        centre = wide[q]
        near = beside_y(centre) + beside_z(centre, lane) + sources[q]
        if q > 0:
            near = near + wide[q - 1]
        if q < PLANES - 1:
            near = near + wide[q + 1]
        rest[q] = jnp.where(inside, 6.0 * centre - near, 0.0)


def stencil_kernel(place, rest, wide, before, after, ends, adjoint):
    row_place = place[1]
    lane = lane_index((24, GRID))
    inside = inside_rows(place[2])
    values = [rest[q] for q in range(PLANES)]
    outer = []
    for n, ref, edge, some in ((0, before, 0, row_place > 0), (1, after, PLANES - 1, row_place < ROWS - 1)):
        beyond = jnp.concatenate([ref[0:24, :], ref[24:48, :]], axis=1)
        values[edge] = values[edge] - jnp.where(inside, beyond, 0.0)
        ends[n] = values[edge][4:20]
        part = jnp.concatenate([ref[48:64, :], ref[64:80, :]], axis=1) - wide[edge, 4:20, :]
        outer.append(jnp.where(some, part, 0.0))
    for q in range(PLANES):
        low = outer[0] if q == 0 else values[q - 1][4:20]
        high = outer[1] if q == PLANES - 1 else values[q + 1][4:20]
        near = (beside_y(values[q]) + beside_z(values[q], lane))[4:20]
        value = 6.0 * values[q][4:20] - (low + high + near)
        adjoint[2 * q] = value
        adjoint[2 * q + 1] = value


def residual_kernel(rest, ends, out):
    for q in range(PLANES):
        out[q] = ends[0] if q == 0 else ends[1] if q == PLANES - 1 else rest[q, 4:20, :]


def call(kernel, operands, scalars, outputs, scratch, flops=0, far=0, far_out=()):
    many = isinstance(outputs, list)
    vmem = pl.BlockSpec(memory_space=pltpu.VMEM)
    smem = pl.BlockSpec(memory_space=pltpu.SMEM)
    hbm = pl.BlockSpec(memory_space=pltpu.HBM)
    out_specs = [hbm if n in far_out else vmem for n in range(len(outputs) if many else 1)]
    operands = list(operands)
    for n in range(len(operands) - far, len(operands)):
        operands[n] = pltpu.with_memory_space_constraint(operands[n], pltpu.HBM)
    cost = pl.CostEstimate(flops=flops, bytes_accessed=4 << 20, transcendentals=flops // 16)
    return pl.pallas_call(
        kernel,
        in_specs=[smem] * len(scalars) + [vmem] * (len(operands) - far) + [hbm] * far,
        out_specs=out_specs if many else out_specs[0],
        out_shape=outputs,
        scratch_shapes=scratch,
        compiler_params=pltpu.CompilerParams(vmem_limit_bytes=VMEM_LIMIT),
        cost_estimate=cost if flops else None,
    )(*scalars, *operands)


def exchange(value, axes):
    return lax.all_to_all(value, axes, split_axis=0, concat_axis=0, tiled=True)


def shape(*sizes):
    return jax.ShapeDtypeStruct(sizes, F32)


def shards(right_side, lift_scale, lift_shift, spectral_weight, local_weight, local_bias, readout):
    z_forward, z_inverse, y_table, x_table = tables()
    place = jnp.stack([lax.axis_index("core"), lax.axis_index(ROW), lax.axis_index(COL)]).astype(jnp.int32)
    params = jnp.concatenate([jnp.stack([lift_scale, lift_shift, local_bias, readout]), local_weight], axis=0)
    everywhere = COL + ROW
    field = right_side[0]
    copies = pltpu.SemaphoreType.DMA((2,))
    fields = [shape(GRID, GRID)] * HALF

    spread = call(spread_kernel, (field,), (), shape(PLANES, 2, COLS, GRID), [copies], far=1)
    plane = exchange(spread.reshape(COLS, COLS, GRID), COL)
    near = call(
        ready_kernel,
        (z_forward, y_table),
        (),
        [jax.ShapeDtypeStruct(z_forward.shape, BF16), jax.ShapeDtypeStruct(y_table.shape, BF16)],
        [copies],
        flops=1 << 24,
        far=2,
    )
    plane, near = lax.optimization_barrier((plane, near))
    plane = plane.reshape(GRID, GRID)
    line_scratch = pltpu.VMEM((MODES, HALF, 2 * GRID), F32)
    plane_scratch = [
        pltpu.VMEM((GRID, GRID), F32),
        pltpu.VMEM((GRID, GRID), BF16),
        pltpu.VMEM((GRID, GRID), BF16),
        line_scratch,
    ]
    lifted = call(lift_kernel, (plane, *near), (place, params), shape(512, 128), plane_scratch)
    lifted = exchange(lifted, everywhere)
    margin, *local = call(
        local_kernel,
        (plane,),
        (place, params),
        [shape(2 * COLS, GRID)] + fields,
        [pltpu.VMEM((GRID, GRID), F32)],
        flops=1 << 27,
    )
    pair = pltpu.VMEM((2, 64, 128), F32)
    mixed, spectra = call(
        mix_kernel, (lifted, spectral_weight, x_table), (), [shape(512, 128), shape(2, 64, 128)], [pair, pair]
    )
    mixed = exchange(mixed, everywhere)
    message, *slope = call(
        inverse_kernel,
        (mixed, margin, z_inverse, y_table, *local),
        (place, params),
        [shape(COLS, 48, 128)] + fields,
        [
            pltpu.VMEM((128, 512), F32),
            line_scratch,
            pltpu.VMEM((GRID, GRID), F32),
            pltpu.VMEM((GRID, GRID), F32),
            pltpu.VMEM((GRID + 8, GRID), F32),
        ],
    )
    message = exchange(message, COL)
    wide, lower, upper = call(
        edge_kernel, (message, field), (), [shape(PLANES, 24, GRID), shape(80, 128), shape(80, 128)], []
    )
    forward = [(i, i + 1) for i in range(ROWS - 1)]
    backward = [(target, source) for source, target in forward]
    before = lax.ppermute(upper, ROW, forward)
    after = lax.ppermute(lower, ROW, backward)
    rest = call(
        inner_kernel,
        (wide, field),
        (place,),
        shape(PLANES, 24, GRID),
        [pltpu.VMEM((PLANES, 24, GRID), F32)],
        flops=1 << 22,
    )
    ends, adjoint = call(
        stencil_kernel,
        (rest, wide, before, after),
        (place,),
        [shape(2, COLS, GRID), shape(2 * PLANES, COLS, GRID)],
        [],
    )
    residual = call(residual_kernel, (rest, ends), (), shape(PLANES, COLS, GRID), [], flops=1 << 22)
    adjoint = exchange(adjoint, COL).reshape(GRID, GRID)
    grads = call(grad_kernel, (adjoint, z_forward, y_table, *slope), (), shape(512, 128), plane_scratch)
    grads = exchange(grads, everywhere)
    spectral_grad = call(
        outer_kernel,
        (grads, spectra, x_table),
        (place,),
        jax.ShapeDtypeStruct(spectral_weight.shape, BF16),
        [pair, pair, pltpu.VMEM(spectral_weight.shape, BF16), pltpu.SemaphoreType.DMA((8,))],
        far_out=(0,),
    )
    return residual[None], spectral_grad


def solution(mesh):
    fine = Mesh(mesh.devices.reshape(8, 4, 2, 4, 2), ROW + COL)
    in_specs = (P(None, ROW, COL, None), P(), P(), P(ROW, COL, None, None, None), P(), P(), P())
    out_specs = (P(None, ROW, COL, None), P(ROW, COL, None, None, None))
    return jax.shard_map(shards, mesh=fine, in_specs=in_specs, out_specs=out_specs, check_vma=False)
```

```python
import math

import jax
import jax.numpy as jnp
import numpy as np
from jax import lax
from jax.experimental import pallas as pl
from jax.experimental.pallas import tpu as pltpu
from jax.sharding import Mesh
from jax.sharding import PartitionSpec as P

MODES = 64
GRID = 256
WIDTH = 16
HALF = 8
ROWS = 32
PLANES = 8
COLS = 16
ROW = ("y", "zh")
COL = ("zl", "x", "core")
F32 = jnp.float32
BF16 = jnp.bfloat16
VMEM_LIMIT = 40 * 1024 * 1024


def halves(table):
    high = table.astype(jnp.bfloat16)
    low = (table - high.astype(np.float64)).astype(jnp.bfloat16)
    return high, low


def wave(frequencies, points):
    phase = (np.outer(frequencies, points) % GRID) * (2.0 * math.pi / GRID)
    return np.cos(phase) / 16.0, np.sin(phase) / 16.0


def tables():
    points = np.arange(GRID)
    cos_z, sin_z = wave(np.arange(MODES), points)
    z_forward = np.concatenate(halves(np.concatenate([cos_z, -sin_z], axis=0)), axis=0)
    weight = np.where(np.arange(MODES) == 0, 1.0, 2.0)[:, None]
    high, low = halves(np.concatenate([cos_z * weight, -sin_z * weight], axis=0).T)
    z_inverse = np.block([[high, high], [low, np.zeros_like(low)]])
    ky = np.array([2 * r + a - MODES // 2 for a in range(2) for r in range(ROWS)])
    cos_y, sin_y = wave(ky, points)
    y_table = np.concatenate(
        [np.concatenate([cos_y, sin_y], axis=1), np.concatenate([-sin_y, cos_y], axis=1)], axis=0
    )
    y_table = np.concatenate(halves(y_table), axis=0)
    places = np.array([8 * r + q for q in range(PLANES) for r in range(ROWS)])
    cos_x, sin_x = wave(np.arange(MODES) - MODES // 2, places)
    x_table = np.concatenate(halves(np.concatenate([cos_x.T, -sin_x.T], axis=1)), axis=1)
    return z_forward, z_inverse, y_table, x_table


def split(value):
    high = value.astype(BF16)
    return high, (value - high.astype(F32)).astype(BF16)


def dot(left, right, dims):
    return lax.dot_general(left, right, (dims, ((), ())), preferred_element_type=F32)


NN = ((1,), (0,))
NT = ((1,), (1,))


ROOT = math.sqrt(2.0 / math.pi)
CUBE = 0.044715


def gelu(value):
    inner = value * (ROOT + (ROOT * CUBE) * (value * value))
    half = 0.5 * value
    return half + half * jnp.tanh(inner)


def gelu_both(value):
    square = value * value
    bent = jnp.tanh(value * (ROOT + (ROOT * CUBE) * square))
    slope = ROOT + (3.0 * ROOT * CUBE) * square
    cdf = 0.5 + 0.5 * bent
    return value * cdf, cdf + (0.5 * value) * ((1.0 - bent * bent) * slope)


def bent_half(half):
    return half * jnp.tanh(half * (2.0 * ROOT + (8.0 * ROOT * CUBE) * (half * half)))


def lift(field, half_scale, half_shift):
    scaled = half_scale * field
    return (scaled + scaled) + (bent_half(half_shift + scaled) - bent_half(half_shift - scaled))


def lane_index(shape):
    return lax.broadcasted_iota(jnp.int32, shape, len(shape) - 1)


def swapped(value):
    return pltpu.roll(value, MODES, 1)


def plane_forward(fill, z_table, y_table, stage_high, stage_low, lines, out):
    for channel in range(HALF):
        fill(channel, stage_high, stage_low)
        z = dot(z_table[...], stage_high[...], NN)
        z = z[:128] + z[128:] + dot(z_table[0:128, :], stage_low[...], NN)
        lines[:, channel, 0:GRID] = z[:MODES]
        lines[:, channel, GRID:] = z[MODES:]
    high, low = split(lines[...].reshape(MODES * HALF, 2 * GRID))
    spectrum = dot(y_table[...], high, NT)
    spectrum = spectrum[:128] + spectrum[128:] + dot(y_table[0:128, :], low, NT)
    lane = lane_index((ROWS, 128)) // 32
    for tile in range(4):
        parts = [spectrum[b * 32 : b * 32 + 32, tile * 128 : tile * 128 + 128] for b in range(4)]
        for e in range(4):
            total = None
            for b in range(4):
                turn = ((b - e) % 4) * 32
                moved = pltpu.roll(parts[b], turn, 1) if turn else parts[b]
                total = moved if total is None else jnp.where(lane == b, moved, total)
            column = 4 * tile + e
            out[column * 32 : column * 32 + 32, :] = total


def lift_kernel(plane, z_table, y_table, scalars, out, turned, high, low, lines):
    turned[...] = plane[...].T

    def fill(channel, stage_high, stage_low):
        gain, offset = scalars[channel : channel + 1, :], scalars[HALF + channel : HALF + channel + 1, :]
        for t in range(8):
            rows = slice(32 * t, 32 * t + 32)
            stage_high[rows, :], stage_low[rows, :] = split(lift(turned[rows, :], gain, offset))

    plane_forward(fill, z_table, y_table, high, low, lines, out)


def grad_kernel(adjoint, rest, z_table, y_table, *refs):
    slope = refs[:HALF]
    out, residual, turned, high, low, lines, sem = refs[HALF:]
    copy = pltpu.make_async_copy(rest, residual, sem)
    copy.start()
    turned[...] = adjoint[...].T

    def fill(channel, stage_high, stage_low):
        for t in range(8):
            rows = slice(32 * t, 32 * t + 32)
            stage_high[rows, :], stage_low[rows, :] = split(turned[rows, :] * slope[channel][rows, :])

    plane_forward(fill, z_table, y_table, high, low, lines, out)
    copy.wait()


def ready_kernel(place, scale, shift, readout, z_far, y_far, z_table, y_table, scalars, ring, doubling, sems):
    copies = [pltpu.make_async_copy(z_far, z_table, sems.at[0]), pltpu.make_async_copy(y_far, y_table, sems.at[1])]
    for copy in copies:
        copy.start()
    first = place[0] * HALF
    for n in range(HALF):
        for m, value in enumerate((0.5 * scale[first + n], 0.5 * shift[first + n], readout[first + n])):
            scalars[HALF * m + n : HALF * m + n + 1, :] = jnp.full((1, GRID), value, F32)
    row = lax.broadcasted_iota(jnp.int32, (24, GRID), 0)
    first_row = jnp.where(place[2] == 0, 4, 3)
    last_row = jnp.where(place[2] == COLS - 1, 19, 20)
    ring[0:24, :] = jnp.where(jnp.logical_and(row >= first_row, row <= last_row), 1.0, 0.0).astype(F32)
    row = lax.broadcasted_iota(jnp.int32, (8, GRID), 0)
    before, after = jnp.where(place[1] > 0, 1.0, 0.0), jnp.where(place[1] < ROWS - 1, 1.0, 0.0)
    ring[24:32, :] = jnp.where(row == 0, before, after).astype(F32)
    row = lax.broadcasted_iota(jnp.int32, (64, 128), 0)
    zero_mode = jnp.logical_and((row // HALF) % 4 == 0, place[2] == 0)
    doubling[...] = jnp.where(zero_mode, 1.0, 2.0).astype(F32)
    for copy in copies:
        copy.wait()


def spread_kernel(field, out, sems):
    copies = [pltpu.make_async_copy(field, out.at[:, k], sems.at[k]) for k in range(2)]
    for copy in copies:
        copy.start()
    for copy in copies:
        copy.wait()


def local_kernel(place, scale, shift, bias, weight, plane, margin, *refs):
    out, turned = refs[:HALF], refs[HALF]
    first = place[0] * HALF
    keep = jnp.where(place[0] == 0, 1.0, 0.0).astype(F32)
    turned[...] = plane[...].T
    margin[...] = jnp.zeros(margin.shape, F32)
    for c in range(1, COLS):
        margin[c : c + 1, :] = plane[16 * c - 1 : 16 * c, :] * keep
        margin[COLS + c - 1 : COLS + c, :] = plane[16 * c : 16 * c + 1, :] * keep

    def step(t, carry):
        rows = pl.ds(pl.multiple_of(t * 16, 16), 16)
        field = turned[rows, :]
        sums = [jnp.full((16, GRID), bias[first + o], F32) for o in range(HALF)]
        for i in range(WIDTH):
            lifted = lift(field, 0.5 * scale[i], 0.5 * shift[i])
            sums = [sums[o] + weight[i, first + o] * lifted for o in range(HALF)]
        for o in range(HALF):
            out[o][rows, :] = sums[o]
        return carry

    lax.fori_loop(0, GRID // 16, step, 0)


def inverse_kernel(received, margin, z_table, y_table, scalars, *refs):
    local, out, slope = refs[:HALF], refs[HALF], refs[HALF + 1 : 2 * HALF + 1]
    grid, lines, spectral, total, padded = refs[2 * HALF + 1 :]
    lane = lane_index((ROWS, 128)) // 32
    for tile in range(4):
        parts = [received[(4 * tile + e) * 32 : (4 * tile + e) * 32 + 32, :] for e in range(4)]
        for b in range(4):
            whole = None
            for e in range(4):
                turn = ((e - b) % 4) * 32
                moved = pltpu.roll(parts[e], turn, 1) if turn else parts[e]
                whole = moved if whole is None else jnp.where(lane == e, moved, whole)
            grid[b * 32 : b * 32 + 32, tile * 128 : tile * 128 + 128] = whole
    high, low = split(grid[...].T)
    modes = dot(jnp.concatenate([high, high], axis=1), y_table[...], NN) + dot(low, y_table[0:128, :], NN)
    lines[...] = modes.reshape(MODES, HALF, 2 * GRID)
    for o in range(HALF):
        modes = jnp.concatenate([lines[:, o, 0:GRID], lines[:, o, GRID:]], axis=0)
        product = dot(z_table[...], jnp.concatenate(split(modes), axis=0), NN)
        spectral[...] = product[:GRID] + product[GRID:]
        read = scalars[2 * HALF + o : 2 * HALF + o + 1, :]
        for t in range(8):
            rows = slice(32 * t, 32 * t + 32)
            value = spectral[rows, :] + local[o][rows, :]
            value, derivative = gelu_both(value)
            slope[o][rows, :] = read * derivative
            if o == 0:
                total[rows, :] = read * value
            else:
                total[rows, :] += read * value
    padded[0:8, :] = jnp.zeros((8, GRID), F32)
    padded[256:264, :] = jnp.zeros((8, GRID), F32)
    padded[4:260, :] = total[...].T
    row = lax.broadcasted_iota(jnp.int32, (24, GRID), 0)
    for c in range(COLS):
        before, after = margin[c : c + 1, :], margin[COLS + c : COLS + c + 1, :]
        block = padded[16 * c : 16 * c + 24, :]
        block = jnp.where(row == 1, before, jnp.where(row == 22, after, block))
        out[c, 0:24, :] = block[:, 0:128]
        out[c, 24:48, :] = block[:, 128:256]


def gather_spectra(received, x_table, sign):
    lines = []
    for k in range(2):
        parts = [received[(2 * q + k) * 32 : (2 * q + k) * 32 + 32, :] for q in range(PLANES)]
        lines.append(jnp.concatenate(parts, axis=0).T)
    product = dot(jnp.concatenate(split(jnp.concatenate(lines, axis=0)), axis=0), x_table[...], NN)
    product = product[:, :128] + product[:, 128:]
    product = product[:256] + product[256:]
    first = [product[128 * k : 128 * k + 64] for k in range(2)]
    second = [product[128 * k + 64 : 128 * k + 128] for k in range(2)]
    return [first[k] + sign * swapped(second[k]) for k in range(2)]


def mix_kernel(received, weight, x_table, out, spectra_out, real, imag):
    low = lane_index((64, 128)) < MODES
    sign = jnp.where(low, -1.0, 1.0).astype(F32)
    for k, spectra in enumerate(gather_spectra(received, x_table, sign)):
        spectra_out[k] = spectra
        other = swapped(spectra)
        real[k] = jnp.where(low, spectra, other)
        imag[k] = jnp.where(low, other, spectra)
    parts = [[], []]
    for group in range(8):
        a, j = group // 4, group % 4
        first = jnp.zeros((WIDTH, 128), F32)
        second = jnp.zeros((WIDTH, 128), F32)
        for i in range(WIDTH):
            k, row = i // HALF, group * HALF + i % HALF
            tile = weight[a, j, i].astype(F32)
            first = first + tile * real[k, row : row + 1, :]
            second = second + tile * imag[k, row : row + 1, :]
        mixed = first + sign[:WIDTH] * swapped(second)
        parts[0].append(mixed[:HALF])
        parts[1].append(mixed[HALF:])
    both = []
    for k in range(2):
        mixed = jnp.concatenate(parts[k], axis=0)
        both += [mixed, -sign * swapped(mixed)]
    high, low = split(jnp.concatenate(both, axis=0))
    result = dot(x_table[...], jnp.concatenate([high, high], axis=1), NT) + dot(x_table[:, 0:128], low, NT)
    for q in range(PLANES):
        for k in range(2):
            place = (2 * q + k) * 32
            out[place : place + 32, :] = result[q * 32 : q * 32 + 32, k * 128 : k * 128 + 128]


def outer_kernel(received, spectra_in, x_table, doubling, out, real, imag, stage, sems):
    low = lane_index((64, 128)) < MODES
    sign = jnp.where(low, -1.0, 1.0).astype(F32)
    grads = [doubling[...] * g for g in gather_spectra(received, x_table, sign)]
    turned = [-sign * swapped(g) for g in grads]
    for k in range(2):
        spectra = spectra_in[k]
        other = swapped(spectra)
        real[k] = jnp.where(low, spectra, other)
        imag[k] = jnp.where(low, other, spectra)
    copies = []
    for group in range(8):
        a, j = group // 4, group % 4
        rows = slice(group * HALF, group * HALF + HALF)
        straight = jnp.concatenate([grads[0][rows], grads[1][rows]], axis=0)
        crossed = jnp.concatenate([turned[0][rows], turned[1][rows]], axis=0)
        for i in range(WIDTH):
            k, line = i // HALF, group * HALF + i % HALF
            value = straight * real[k, line : line + 1, :] + crossed * imag[k, line : line + 1, :]
            stage[a, j, i] = value.astype(BF16)
        copies.append(pltpu.make_async_copy(stage.at[a, j], out.at[a, j], sems.at[group]))
        copies[-1].start()
    for copy in copies:
        copy.wait()


def beside_z(value, lane):
    left = jnp.where(lane == 0, 0.0, pltpu.roll(value, 1, 1))
    return left + jnp.where(lane == GRID - 1, 0.0, pltpu.roll(value, GRID - 1, 1))


def beside_y(value):
    return pltpu.roll(value, 1, 0) + pltpu.roll(value, 23, 0)


def edge_kernel(received, field, wide, lower, upper):
    lane = lane_index((24, GRID))
    for q in range(PLANES):
        for h in range(2):
            rows, lanes = slice(24 * h, 24 * h + 24), slice(128 * h, 128 * h + 128)
            wide[q, :, lanes] = received[2 * q, rows, :] + received[2 * q + 1, rows, :]
    for ref, edge, inner in ((lower, 0, 1), (upper, PLANES - 1, PLANES - 2)):
        value = wide[edge]
        rest = 6.0 * value - (wide[inner] + beside_y(value) + beside_z(value, lane))
        rest = rest[4:20] - field[edge]
        ref[0:24, :] = value[:, 0:128]
        ref[24:48, :] = value[:, 128:256]
        ref[48:64, :] = rest[:, 0:128]
        ref[64:80, :] = rest[:, 128:256]


def inner_kernel(wide, field, ring, rest, sources):
    lane = lane_index((24, GRID))
    inside = ring[0:24, :]
    for q in range(PLANES):
        sources[q] = jnp.zeros((24, GRID), F32)
        sources[q, 4:20, :] = field[q]
        sources[q, 3:4, :] = wide[q, 1:2, :]
        sources[q, 20:21, :] = wide[q, 22:23, :]
        centre = wide[q]
        near = beside_y(centre) + beside_z(centre, lane) + sources[q]
        if q > 0:
            near = near + wide[q - 1]
        if q < PLANES - 1:
            near = near + wide[q + 1]
        rest[q] = inside * (6.0 * centre - near)


def stencil_kernel(rest, wide, before, after, ring, residual, adjoint):
    lane = lane_index((24, GRID))
    inside = ring[0:24, :]
    values = [rest[q] for q in range(PLANES)]
    outer = []
    for n, ref, edge in ((0, before, 0), (1, after, PLANES - 1)):
        beyond = jnp.concatenate([ref[0:24, :], ref[24:48, :]], axis=1)
        values[edge] = values[edge] - inside * beyond
        part = jnp.concatenate([ref[48:64, :], ref[64:80, :]], axis=1) - wide[edge, 4:20, :]
        outer.append(ring[24 + n : 25 + n, :] * part)
    for q in range(PLANES):
        low = outer[0] if q == 0 else values[q - 1][4:20]
        high = outer[1] if q == PLANES - 1 else values[q + 1][4:20]
        residual[q] = values[q][4:20]
        near = (beside_y(values[q]) + beside_z(values[q], lane))[4:20]
        value = 6.0 * values[q][4:20] - (low + high + near)
        adjoint[2 * q] = value
        adjoint[2 * q + 1] = value


def call(kernel, operands, scalars, outputs, scratch, flops=0, far=0, far_out=()):
    many = isinstance(outputs, list)
    vmem = pl.BlockSpec(memory_space=pltpu.VMEM)
    smem = pl.BlockSpec(memory_space=pltpu.SMEM)
    hbm = pl.BlockSpec(memory_space=pltpu.HBM)
    out_specs = [hbm if n in far_out else vmem for n in range(len(outputs) if many else 1)]
    operands = list(operands)
    for n in range(len(operands) - far, len(operands)):
        operands[n] = pltpu.with_memory_space_constraint(operands[n], pltpu.HBM)
    cost = pl.CostEstimate(flops=flops, bytes_accessed=4 << 20, transcendentals=flops // 16)
    return pl.pallas_call(
        kernel,
        in_specs=[smem] * len(scalars) + [vmem] * (len(operands) - far) + [hbm] * far,
        out_specs=out_specs if many else out_specs[0],
        out_shape=outputs,
        scratch_shapes=scratch,
        compiler_params=pltpu.CompilerParams(vmem_limit_bytes=VMEM_LIMIT),
        cost_estimate=cost if flops else None,
    )(*scalars, *operands)


def exchange(value, axes):
    return lax.all_to_all(value, axes, split_axis=0, concat_axis=0, tiled=True)


def shape(*sizes):
    return jax.ShapeDtypeStruct(sizes, F32)


def shards(right_side, lift_scale, lift_shift, spectral_weight, local_weight, local_bias, readout):
    z_forward, z_inverse, y_table, x_table = tables()
    place = jnp.stack([lax.axis_index("core"), lax.axis_index(ROW), lax.axis_index(COL)]).astype(jnp.int32)
    everywhere = COL + ROW
    field = right_side[0]
    copies = pltpu.SemaphoreType.DMA((2,))
    fields = [shape(GRID, GRID)] * HALF

    spread = call(spread_kernel, (field,), (), shape(PLANES, 2, COLS, GRID), [copies], far=1)
    plane = exchange(spread.reshape(COLS, COLS, GRID), COL)
    near = call(
        ready_kernel,
        (z_forward, y_table),
        (place, lift_scale, lift_shift, readout),
        [
            jax.ShapeDtypeStruct(z_forward.shape, BF16),
            jax.ShapeDtypeStruct(y_table.shape, BF16),
            shape(24, GRID),
            shape(32, GRID),
            shape(64, 128),
        ],
        [copies],
        flops=1 << 24,
        far=2,
    )
    plane, near = lax.optimization_barrier((plane, near))
    z_near, y_near, scalars, ring, doubling = near
    plane = plane.reshape(GRID, GRID)
    line_scratch = pltpu.VMEM((MODES, HALF, 2 * GRID), F32)
    plane_scratch = [
        pltpu.VMEM((GRID, GRID), F32),
        pltpu.VMEM((GRID, GRID), BF16),
        pltpu.VMEM((GRID, GRID), BF16),
        line_scratch,
    ]
    lifted = call(lift_kernel, (plane, z_near, y_near, scalars), (), shape(512, 128), plane_scratch)
    lifted = exchange(lifted, everywhere)
    margin, *local = call(
        local_kernel,
        (plane,),
        (place, lift_scale, lift_shift, local_bias, local_weight),
        [shape(2 * COLS, GRID)] + fields,
        [pltpu.VMEM((GRID, GRID), F32)],
        flops=1 << 27,
    )
    pair = pltpu.VMEM((2, 64, 128), F32)
    mixed, spectra = call(
        mix_kernel, (lifted, spectral_weight, x_table), (), [shape(512, 128), shape(2, 64, 128)], [pair, pair]
    )
    mixed = exchange(mixed, everywhere)
    message, *slope = call(
        inverse_kernel,
        (mixed, margin, z_inverse, y_table, scalars, *local),
        (),
        [shape(COLS, 48, 128)] + fields,
        [
            pltpu.VMEM((128, 512), F32),
            line_scratch,
            pltpu.VMEM((GRID, GRID), F32),
            pltpu.VMEM((GRID, GRID), F32),
            pltpu.VMEM((GRID + 8, GRID), F32),
        ],
    )
    message = exchange(message, COL)
    wide, lower, upper = call(
        edge_kernel, (message, field), (), [shape(PLANES, 24, GRID), shape(80, 128), shape(80, 128)], []
    )
    forward = [(i, i + 1) for i in range(ROWS - 1)]
    backward = [(target, source) for source, target in forward]
    before = lax.ppermute(upper, ROW, forward)
    after = lax.ppermute(lower, ROW, backward)
    rest = call(
        inner_kernel,
        (wide, field, ring),
        (),
        shape(PLANES, 24, GRID),
        [pltpu.VMEM((PLANES, 24, GRID), F32)],
        flops=1 << 22,
    )
    rest, adjoint = call(
        stencil_kernel,
        (rest, wide, before, after, ring),
        (),
        [shape(PLANES, COLS, GRID), shape(2 * PLANES, COLS, GRID)],
        [],
    )
    adjoint = exchange(adjoint, COL).reshape(GRID, GRID)
    grads, residual = call(
        grad_kernel,
        (adjoint, rest, z_forward, y_table, *slope),
        (),
        [shape(512, 128), shape(PLANES, COLS, GRID)],
        plane_scratch + [pltpu.SemaphoreType.DMA],
        far_out=(1,),
    )
    grads = exchange(grads, everywhere)
    spectral_grad = call(
        outer_kernel,
        (grads, spectra, x_table, doubling),
        (),
        jax.ShapeDtypeStruct(spectral_weight.shape, BF16),
        [pair, pair, pltpu.VMEM(spectral_weight.shape, BF16), pltpu.SemaphoreType.DMA((8,))],
        far_out=(0,),
    )
    return residual[None], spectral_grad


def solution(mesh):
    fine = Mesh(mesh.devices.reshape(8, 4, 2, 4, 2), ROW + COL)
    in_specs = (P(None, ROW, COL, None), P(), P(), P(ROW, COL, None, None, None), P(), P(), P())
    out_specs = (P(None, ROW, COL, None), P(ROW, COL, None, None, None))
    return jax.shard_map(shards, mesh=fine, in_specs=in_specs, out_specs=out_specs, check_vma=False)
```

```python
import math

import jax
import jax.numpy as jnp
import numpy as np
from jax import lax
from jax.experimental import pallas as pl
from jax.experimental.pallas import tpu as pltpu
from jax.sharding import Mesh
from jax.sharding import PartitionSpec as P

MODES = 64
GRID = 256
WIDTH = 16
HALF = 8
ROWS = 32
PLANES = 8
COLS = 16
ROW = ("y", "zh")
COL = ("zl", "x", "core")
F32 = jnp.float32
BF16 = jnp.bfloat16
VMEM_LIMIT = 40 * 1024 * 1024


def halves(table):
    high = table.astype(jnp.bfloat16)
    low = (table - high.astype(np.float64)).astype(jnp.bfloat16)
    return high, low


def wave(frequencies, points):
    phase = (np.outer(frequencies, points) % GRID) * (2.0 * math.pi / GRID)
    return np.cos(phase) / 16.0, np.sin(phase) / 16.0


def tables():
    points = np.arange(GRID)
    cos_z, sin_z = wave(np.arange(MODES), points)
    z_forward = np.concatenate(halves(np.concatenate([cos_z, -sin_z], axis=0)), axis=0)
    weight = np.where(np.arange(MODES) == 0, 1.0, 2.0)[:, None]
    high, low = halves(np.concatenate([cos_z * weight, -sin_z * weight], axis=0).T)
    z_inverse = np.block([[high, high], [low, np.zeros_like(low)]])
    ky = np.array([2 * r + a - MODES // 2 for a in range(2) for r in range(ROWS)])
    cos_y, sin_y = wave(ky, points)
    y_table = np.concatenate(
        [np.concatenate([cos_y, sin_y], axis=1), np.concatenate([-sin_y, cos_y], axis=1)], axis=0
    )
    y_table = np.concatenate(halves(y_table), axis=0)
    places = np.array([8 * r + q for q in range(PLANES) for r in range(ROWS)])
    cos_x, sin_x = wave(np.arange(MODES) - MODES // 2, places)
    x_table = np.concatenate(halves(np.concatenate([cos_x.T, -sin_x.T], axis=1)), axis=1)
    return z_forward, z_inverse, y_table, x_table


def split(value):
    high = value.astype(BF16)
    return high, (value - high.astype(F32)).astype(BF16)


def dot(left, right, dims):
    return lax.dot_general(left, right, (dims, ((), ())), preferred_element_type=F32)


NN = ((1,), (0,))
NT = ((1,), (1,))


ROOT = math.sqrt(2.0 / math.pi)
CUBE = 0.044715


def gelu(value):
    inner = value * (ROOT + (ROOT * CUBE) * (value * value))
    half = 0.5 * value
    return half + half * jnp.tanh(inner)


def gelu_both(value):
    square = value * value
    bent = jnp.tanh(value * (ROOT + (ROOT * CUBE) * square))
    slope = ROOT + (3.0 * ROOT * CUBE) * square
    cdf = 0.5 + 0.5 * bent
    return value * cdf, cdf + (0.5 * value) * ((1.0 - bent * bent) * slope)


def bent_half(half):
    return half * jnp.tanh(half * (2.0 * ROOT + (8.0 * ROOT * CUBE) * (half * half)))


def lift(field, half_scale, half_shift):
    scaled = half_scale * field
    return (scaled + scaled) + (bent_half(half_shift + scaled) - bent_half(half_shift - scaled))


def lane_index(shape):
    return lax.broadcasted_iota(jnp.int32, shape, len(shape) - 1)


def swapped(value):
    return pltpu.roll(value, MODES, 1)


def beside_z(value, lane):
    left = jnp.where(lane == 0, 0.0, pltpu.roll(value, 1, 1))
    return left + jnp.where(lane == GRID - 1, 0.0, pltpu.roll(value, GRID - 1, 1))


def plane_forward(fill, z_table, y_table, stage_high, stage_low, lines, out):
    for channel in range(HALF):
        fill(channel, stage_high, stage_low)
        z = dot(z_table[...], stage_high[...], NN)
        z = z[:128] + z[128:] + dot(z_table[0:128, :], stage_low[...], NN)
        lines[:, channel, 0:GRID] = z[:MODES]
        lines[:, channel, GRID:] = z[MODES:]
    high, low = split(lines[...].reshape(MODES * HALF, 2 * GRID))
    spectrum = dot(y_table[...], high, NT)
    spectrum = spectrum[:128] + spectrum[128:] + dot(y_table[0:128, :], low, NT)
    lane = lane_index((ROWS, 128)) // 32
    for tile in range(4):
        parts = [spectrum[b * 32 : b * 32 + 32, tile * 128 : tile * 128 + 128] for b in range(4)]
        for e in range(4):
            total = None
            for b in range(4):
                turn = ((b - e) % 4) * 32
                moved = pltpu.roll(parts[b], turn, 1) if turn else parts[b]
                total = moved if total is None else jnp.where(lane == b, moved, total)
            column = 4 * tile + e
            out[column * 32 : column * 32 + 32, :] = total


def lift_kernel(plane, z_table, y_table, scalars, out, turned, high, low, lines):
    turned[...] = plane[...].T

    def fill(channel, stage_high, stage_low):
        gain, offset = scalars[channel : channel + 1, :], scalars[HALF + channel : HALF + channel + 1, :]
        for t in range(8):
            rows = slice(32 * t, 32 * t + 32)
            stage_high[rows, :], stage_low[rows, :] = split(lift(turned[rows, :], gain, offset))

    plane_forward(fill, z_table, y_table, high, low, lines, out)


def grad_kernel(adjoint, rest, z_table, y_table, *refs):
    slope = refs[:HALF]
    out, residual, turned, high, low, lines, sem = refs[HALF:]
    copy = pltpu.make_async_copy(rest, residual, sem)
    copy.start()
    turned[...] = adjoint[...].T

    def fill(channel, stage_high, stage_low):
        for t in range(8):
            rows = slice(32 * t, 32 * t + 32)
            stage_high[rows, :], stage_low[rows, :] = split(turned[rows, :] * slope[channel][rows, :])

    plane_forward(fill, z_table, y_table, high, low, lines, out)
    copy.wait()


def ready_kernel(place, scale, shift, readout, z_far, y_far, z_table, y_table, scalars, ring, doubling, sems):
    copies = [pltpu.make_async_copy(z_far, z_table, sems.at[0]), pltpu.make_async_copy(y_far, y_table, sems.at[1])]
    for copy in copies:
        copy.start()
    first = place[0] * HALF
    for n in range(HALF):
        for m, value in enumerate((0.5 * scale[first + n], 0.5 * shift[first + n], readout[first + n])):
            scalars[HALF * m + n : HALF * m + n + 1, :] = jnp.full((1, GRID), value, F32)
    row = lax.broadcasted_iota(jnp.int32, (24, GRID), 0)
    first_row = jnp.where(place[2] == 0, 4, 3)
    last_row = jnp.where(place[2] == COLS - 1, 19, 20)
    ring[0:24, :] = jnp.where(jnp.logical_and(row >= first_row, row <= last_row), 1.0, 0.0).astype(F32)
    row = lax.broadcasted_iota(jnp.int32, (8, GRID), 0)
    before, after = jnp.where(place[1] > 0, 1.0, 0.0), jnp.where(place[1] < ROWS - 1, 1.0, 0.0)
    odd = jnp.where(place[1] % 2 == 1, 1.0, 0.0)
    ring[24:32, :] = jnp.where(row == 0, before, jnp.where(row == 1, after, odd)).astype(F32)
    row = lax.broadcasted_iota(jnp.int32, (64, 128), 0)
    zero_mode = jnp.logical_and((row // HALF) % 4 == 0, place[2] == 0)
    doubling[...] = jnp.where(zero_mode, 1.0, 2.0).astype(F32)
    for copy in copies:
        copy.wait()


def spread_kernel(field, out, sems):
    copies = [pltpu.make_async_copy(field, out.at[:, k], sems.at[k]) for k in range(2)]
    for copy in copies:
        copy.start()
    for copy in copies:
        copy.wait()


def local_kernel(place, scale, shift, bias, weight, plane, margin, *refs):
    out, turned = refs[:HALF], refs[HALF]
    first = place[0] * HALF
    keep = jnp.where(place[0] == 0, 1.0, 0.0).astype(F32)
    turned[...] = plane[...].T
    margin[...] = jnp.zeros(margin.shape, F32)
    for c in range(1, COLS):
        margin[c : c + 1, :] = plane[16 * c - 1 : 16 * c, :] * keep
        margin[COLS + c - 1 : COLS + c, :] = plane[16 * c : 16 * c + 1, :] * keep

    def step(t, carry):
        rows = pl.ds(pl.multiple_of(t * 16, 16), 16)
        field = turned[rows, :]
        sums = [jnp.full((16, GRID), bias[first + o], F32) for o in range(HALF)]
        for i in range(WIDTH):
            lifted = lift(field, 0.5 * scale[i], 0.5 * shift[i])
            sums = [sums[o] + weight[i, first + o] * lifted for o in range(HALF)]
        for o in range(HALF):
            out[o][rows, :] = sums[o]
        return carry

    lax.fori_loop(0, GRID // 16, step, 0)


def inverse_kernel(received, margin, z_table, y_table, scalars, *refs):
    local, out, slope = refs[:HALF], refs[HALF], refs[HALF + 1 : 2 * HALF + 1]
    grid, lines, spectral, total, padded = refs[2 * HALF + 1 :]
    lane = lane_index((ROWS, 128)) // 32
    for tile in range(4):
        parts = [received[(4 * tile + e) * 32 : (4 * tile + e) * 32 + 32, :] for e in range(4)]
        for b in range(4):
            whole = None
            for e in range(4):
                turn = ((e - b) % 4) * 32
                moved = pltpu.roll(parts[e], turn, 1) if turn else parts[e]
                whole = moved if whole is None else jnp.where(lane == e, moved, whole)
            grid[b * 32 : b * 32 + 32, tile * 128 : tile * 128 + 128] = whole
    high, low = split(grid[...].T)
    modes = dot(jnp.concatenate([high, high], axis=1), y_table[...], NN) + dot(low, y_table[0:128, :], NN)
    lines[...] = modes.reshape(MODES, HALF, 2 * GRID)
    for o in range(HALF):
        modes = jnp.concatenate([lines[:, o, 0:GRID], lines[:, o, GRID:]], axis=0)
        product = dot(z_table[...], jnp.concatenate(split(modes), axis=0), NN)
        spectral[...] = product[:GRID] + product[GRID:]
        read = scalars[2 * HALF + o : 2 * HALF + o + 1, :]
        for t in range(8):
            rows = slice(32 * t, 32 * t + 32)
            value = spectral[rows, :] + local[o][rows, :]
            value, derivative = gelu_both(value)
            slope[o][rows, :] = read * derivative
            if o == 0:
                total[rows, :] = read * value
            else:
                total[rows, :] += read * value
    padded[0:8, :] = jnp.zeros((8, GRID), F32)
    padded[256:264, :] = jnp.zeros((8, GRID), F32)
    value = total[...].T
    padded[4:260, :] = value
    beside = pltpu.roll(value, 1, 0) + pltpu.roll(value, GRID - 1, 0) + beside_z(value, lane_index((GRID, GRID)))
    spectral[...] = 6.0 * value - beside
    blank = jnp.zeros((1, GRID), F32)
    for c in range(COLS):
        before, after = blank, blank
        if c > 0:
            before = spectral[16 * c - 1 : 16 * c, :] - margin[c : c + 1, :]
        if c < COLS - 1:
            after = spectral[16 * c + 16 : 16 * c + 17, :] - margin[COLS + c : COLS + c + 1, :]
        for h in range(2):
            lanes = slice(128 * h, 128 * h + 128)
            out[c, 20 * h : 20 * h + 1, :] = before[:, lanes]
            out[c, 20 * h + 1 : 20 * h + 19, :] = padded[16 * c + 3 : 16 * c + 21, lanes]
            out[c, 20 * h + 19 : 20 * h + 20, :] = after[:, lanes]


def gather_spectra(received, x_table, sign):
    lines = []
    for k in range(2):
        parts = [received[(2 * q + k) * 32 : (2 * q + k) * 32 + 32, :] for q in range(PLANES)]
        lines.append(jnp.concatenate(parts, axis=0).T)
    product = dot(jnp.concatenate(split(jnp.concatenate(lines, axis=0)), axis=0), x_table[...], NN)
    product = product[:, :128] + product[:, 128:]
    product = product[:256] + product[256:]
    first = [product[128 * k : 128 * k + 64] for k in range(2)]
    second = [product[128 * k + 64 : 128 * k + 128] for k in range(2)]
    return [first[k] + sign * swapped(second[k]) for k in range(2)]


def mix_kernel(received, weight, x_table, out, spectra_out, real, imag):
    low = lane_index((64, 128)) < MODES
    sign = jnp.where(low, -1.0, 1.0).astype(F32)
    for k, spectra in enumerate(gather_spectra(received, x_table, sign)):
        spectra_out[k] = spectra
        other = swapped(spectra)
        real[k] = jnp.where(low, spectra, other)
        imag[k] = jnp.where(low, other, spectra)
    parts = [[], []]
    for group in range(8):
        a, j = group // 4, group % 4
        first = jnp.zeros((WIDTH, 128), F32)
        second = jnp.zeros((WIDTH, 128), F32)
        for i in range(WIDTH):
            k, row = i // HALF, group * HALF + i % HALF
            tile = weight[a, j, i].astype(F32)
            first = first + tile * real[k, row : row + 1, :]
            second = second + tile * imag[k, row : row + 1, :]
        mixed = first + sign[:WIDTH] * swapped(second)
        parts[0].append(mixed[:HALF])
        parts[1].append(mixed[HALF:])
    both = []
    for k in range(2):
        mixed = jnp.concatenate(parts[k], axis=0)
        both += [mixed, -sign * swapped(mixed)]
    high, low = split(jnp.concatenate(both, axis=0))
    result = dot(x_table[...], jnp.concatenate([high, high], axis=1), NT) + dot(x_table[:, 0:128], low, NT)
    for q in range(PLANES):
        for k in range(2):
            place = (2 * q + k) * 32
            out[place : place + 32, :] = result[q * 32 : q * 32 + 32, k * 128 : k * 128 + 128]


def outer_kernel(received, spectra_in, x_table, doubling, out, real, imag, stage, sems):
    low = lane_index((64, 128)) < MODES
    sign = jnp.where(low, -1.0, 1.0).astype(F32)
    grads = [doubling[...] * g for g in gather_spectra(received, x_table, sign)]
    turned = [-sign * swapped(g) for g in grads]
    for k in range(2):
        spectra = spectra_in[k]
        other = swapped(spectra)
        real[k] = jnp.where(low, spectra, other)
        imag[k] = jnp.where(low, other, spectra)
    copies = []
    for group in range(8):
        a, j = group // 4, group % 4
        rows = slice(group * HALF, group * HALF + HALF)
        straight = jnp.concatenate([grads[0][rows], grads[1][rows]], axis=0)
        crossed = jnp.concatenate([turned[0][rows], turned[1][rows]], axis=0)
        for i in range(WIDTH):
            k, line = i // HALF, group * HALF + i % HALF
            value = straight * real[k, line : line + 1, :] + crossed * imag[k, line : line + 1, :]
            stage[a, j, i] = value.astype(BF16)
        copies.append(pltpu.make_async_copy(stage.at[a, j], out.at[a, j], sems.at[group]))
        copies[-1].start()
    for copy in copies:
        copy.wait()


def beside_y(value):
    return pltpu.roll(value, 1, 0) + pltpu.roll(value, 23, 0)


def edge_kernel(received, field, ring, wide, first, second):
    lane = lane_index((24, GRID))
    for q in range(PLANES):
        wide[q] = jnp.zeros((24, GRID), F32)
        for h in range(2):
            lanes = slice(128 * h, 128 * h + 128)
            both = received[2 * q, 20 * h : 20 * h + 20, :] + received[2 * q + 1, 20 * h : 20 * h + 20, :]
            wide[q, 3:21, lanes] = both[1:19]
            wide[q, 1:2, lanes] = both[0:1]
            wide[q, 22:23, lanes] = both[19:20]
    sent = []
    for edge, inner in ((0, 1), (PLANES - 1, PLANES - 2)):
        value = wide[edge]
        rest = 6.0 * value - (wide[inner] + beside_y(value) + beside_z(value, lane))
        rest = rest[4:20] - field[edge]
        sent.append(jnp.concatenate([value[:, :128], value[:, 128:], rest[:, :128], rest[:, 128:]], axis=0))
    odd = jnp.broadcast_to(ring[26:27, 0:128], (80, 128)) > 0.5
    first[...] = jnp.where(odd, sent[1], sent[0])
    second[...] = jnp.where(odd, sent[0], sent[1])


def inner_kernel(wide, field, ring, rest):
    lane = lane_index((24, GRID))
    for q in range(PLANES):
        centre = wide[q]
        across = jnp.zeros((24, GRID), F32)
        if q > 0:
            across = across + wide[q - 1]
        if q < PLANES - 1:
            across = across + wide[q + 1]
        value = 6.0 * centre - (beside_y(centre) + beside_z(centre, lane) + across)
        rest[q] = value
        rest[q, 4:20, :] = value[4:20] - field[q]
        rest[q, 3:4, :] = ring[3:4, :] * (wide[q, 1:2, :] - across[3:4])
        rest[q, 20:21, :] = ring[20:21, :] * (wide[q, 22:23, :] - across[20:21])


def stencil_kernel(rest, wide, first, second, ring, residual, adjoint):
    lane = lane_index((24, GRID))
    inside = ring[0:24, :]
    values = [rest[q] for q in range(PLANES)]
    odd = jnp.broadcast_to(ring[26:27, 0:128], (80, 128)) > 0.5
    before, after = jnp.where(odd, second[...], first[...]), jnp.where(odd, first[...], second[...])
    outer = []
    for n, ref, edge in ((0, before, 0), (1, after, PLANES - 1)):
        beyond = jnp.concatenate([ref[0:24], ref[24:48]], axis=1)
        values[edge] = values[edge] - inside * beyond
        part = jnp.concatenate([ref[48:64], ref[64:80]], axis=1) - wide[edge, 4:20, :]
        outer.append(ring[24 + n : 25 + n, :] * part)
    for q in range(PLANES):
        low = outer[0] if q == 0 else values[q - 1][4:20]
        high = outer[1] if q == PLANES - 1 else values[q + 1][4:20]
        residual[q] = values[q][4:20]
        near = (beside_y(values[q]) + beside_z(values[q], lane))[4:20]
        value = 6.0 * values[q][4:20] - (low + high + near)
        adjoint[2 * q] = value
        adjoint[2 * q + 1] = value


def call(kernel, operands, scalars, outputs, scratch, flops=0, far=0, far_out=()):
    many = isinstance(outputs, list)
    vmem = pl.BlockSpec(memory_space=pltpu.VMEM)
    smem = pl.BlockSpec(memory_space=pltpu.SMEM)
    hbm = pl.BlockSpec(memory_space=pltpu.HBM)
    out_specs = [hbm if n in far_out else vmem for n in range(len(outputs) if many else 1)]
    operands = list(operands)
    for n in range(len(operands) - far, len(operands)):
        operands[n] = pltpu.with_memory_space_constraint(operands[n], pltpu.HBM)
    cost = pl.CostEstimate(flops=flops, bytes_accessed=4 << 20, transcendentals=flops // 16)
    return pl.pallas_call(
        kernel,
        in_specs=[smem] * len(scalars) + [vmem] * (len(operands) - far) + [hbm] * far,
        out_specs=out_specs if many else out_specs[0],
        out_shape=outputs,
        scratch_shapes=scratch,
        compiler_params=pltpu.CompilerParams(vmem_limit_bytes=VMEM_LIMIT),
        cost_estimate=cost if flops else None,
    )(*scalars, *operands)


def exchange(value, axes):
    return lax.all_to_all(value, axes, split_axis=0, concat_axis=0, tiled=True)


def shape(*sizes):
    return jax.ShapeDtypeStruct(sizes, F32)


def shards(right_side, lift_scale, lift_shift, spectral_weight, local_weight, local_bias, readout):
    z_forward, z_inverse, y_table, x_table = tables()
    place = jnp.stack([lax.axis_index("core"), lax.axis_index(ROW), lax.axis_index(COL)]).astype(jnp.int32)
    everywhere = COL + ROW
    field = right_side[0]
    copies = pltpu.SemaphoreType.DMA((2,))
    fields = [shape(GRID, GRID)] * HALF

    spread = call(spread_kernel, (field,), (), shape(PLANES, 2, COLS, GRID), [copies], far=1)
    plane = exchange(spread.reshape(COLS, COLS, GRID), COL)
    near = call(
        ready_kernel,
        (z_forward, y_table),
        (place, lift_scale, lift_shift, readout),
        [
            jax.ShapeDtypeStruct(z_forward.shape, BF16),
            jax.ShapeDtypeStruct(y_table.shape, BF16),
            shape(24, GRID),
            shape(32, GRID),
            shape(64, 128),
        ],
        [copies],
        flops=1 << 24,
        far=2,
    )
    plane, near = lax.optimization_barrier((plane, near))
    z_near, y_near, scalars, ring, doubling = near
    plane = plane.reshape(GRID, GRID)
    line_scratch = pltpu.VMEM((MODES, HALF, 2 * GRID), F32)
    plane_scratch = [
        pltpu.VMEM((GRID, GRID), F32),
        pltpu.VMEM((GRID, GRID), BF16),
        pltpu.VMEM((GRID, GRID), BF16),
        line_scratch,
    ]
    lifted = call(lift_kernel, (plane, z_near, y_near, scalars), (), shape(512, 128), plane_scratch)
    lifted = exchange(lifted, everywhere)
    margin, *local = call(
        local_kernel,
        (plane,),
        (place, lift_scale, lift_shift, local_bias, local_weight),
        [shape(2 * COLS, GRID)] + fields,
        [pltpu.VMEM((GRID, GRID), F32)],
        flops=1 << 27,
    )
    pair = pltpu.VMEM((2, 64, 128), F32)
    mixed, spectra = call(
        mix_kernel, (lifted, spectral_weight, x_table), (), [shape(512, 128), shape(2, 64, 128)], [pair, pair]
    )
    mixed = exchange(mixed, everywhere)
    message, *slope = call(
        inverse_kernel,
        (mixed, margin, z_inverse, y_table, scalars, *local),
        (),
        [shape(COLS, 40, 128)] + fields,
        [
            pltpu.VMEM((128, 512), F32),
            line_scratch,
            pltpu.VMEM((GRID, GRID), F32),
            pltpu.VMEM((GRID, GRID), F32),
            pltpu.VMEM((GRID + 8, GRID), F32),
        ],
    )
    message = exchange(message, COL)
    wide, first, second = call(
        edge_kernel, (message, field, ring), (), [shape(PLANES, 24, GRID), shape(80, 128), shape(80, 128)], []
    )
    odd_pairs = [(r, r + 1 if r % 2 else r - 1) for r in range(1, ROWS - 1)]
    even_pairs = [(r, r - 1 if r % 2 else r + 1) for r in range(ROWS)]
    first = lax.ppermute(first, ROW, odd_pairs)
    second = lax.ppermute(second, ROW, even_pairs)
    rest = call(
        inner_kernel,
        (wide, field, ring),
        (),
        shape(PLANES, 24, GRID),
        [],
        flops=1 << 22,
    )
    rest, adjoint = call(
        stencil_kernel,
        (rest, wide, first, second, ring),
        (),
        [shape(PLANES, COLS, GRID), shape(2 * PLANES, COLS, GRID)],
        [],
    )
    adjoint = exchange(adjoint, COL).reshape(GRID, GRID)
    grads, residual = call(
        grad_kernel,
        (adjoint, rest, z_forward, y_table, *slope),
        (),
        [shape(512, 128), shape(PLANES, COLS, GRID)],
        plane_scratch + [pltpu.SemaphoreType.DMA],
        far_out=(1,),
    )
    grads = exchange(grads, everywhere)
    spectral_grad = call(
        outer_kernel,
        (grads, spectra, x_table, doubling),
        (),
        jax.ShapeDtypeStruct(spectral_weight.shape, BF16),
        [pair, pair, pltpu.VMEM(spectral_weight.shape, BF16), pltpu.SemaphoreType.DMA((8,))],
        far_out=(0,),
    )
    return residual[None], spectral_grad


def solution(mesh):
    fine = Mesh(mesh.devices.reshape(8, 4, 2, 4, 2), ROW + COL)
    in_specs = (P(None, ROW, COL, None), P(), P(), P(ROW, COL, None, None, None), P(), P(), P())
    out_specs = (P(None, ROW, COL, None), P(ROW, COL, None, None, None))
    return jax.shard_map(shards, mesh=fine, in_specs=in_specs, out_specs=out_specs, check_vma=False)
```

```python
import math

import jax
import jax.numpy as jnp
import numpy as np
from jax import lax
from jax.experimental import pallas as pl
from jax.experimental.pallas import tpu as pltpu
from jax.sharding import Mesh
from jax.sharding import PartitionSpec as P

MODES = 64
GRID = 256
WIDTH = 16
HALF = 8
ROWS = 32
PLANES = 8
COLS = 16
ROW = ("y", "zh")
COL = ("zl", "x", "core")
F32 = jnp.float32
BF16 = jnp.bfloat16
VMEM_LIMIT = 40 * 1024 * 1024


def halves(table):
    high = table.astype(jnp.bfloat16)
    low = (table - high.astype(np.float64)).astype(jnp.bfloat16)
    return high, low


def wave(frequencies, points):
    phase = (np.outer(frequencies, points) % GRID) * (2.0 * math.pi / GRID)
    return np.cos(phase) / 16.0, np.sin(phase) / 16.0


def tables():
    points = np.arange(GRID)
    cos_z, sin_z = wave(np.arange(MODES), points)
    z_forward = np.concatenate(halves(np.concatenate([cos_z, -sin_z], axis=0)), axis=0)
    weight = np.where(np.arange(MODES) == 0, 1.0, 2.0)[:, None]
    high, low = halves(np.concatenate([cos_z * weight, -sin_z * weight], axis=0).T)
    z_inverse = np.block([[high, high], [low, np.zeros_like(low)]])
    ky = np.array([2 * r + a - MODES // 2 for a in range(2) for r in range(ROWS)])
    cos_y, sin_y = wave(ky, points)
    y_table = np.concatenate(
        [np.concatenate([cos_y, sin_y], axis=1), np.concatenate([-sin_y, cos_y], axis=1)], axis=0
    )
    y_table = np.concatenate(halves(y_table), axis=0)
    places = np.array([8 * r + q for q in range(PLANES) for r in range(ROWS)])
    cos_x, sin_x = wave(np.arange(MODES) - MODES // 2, places)
    x_table = np.concatenate(halves(np.concatenate([cos_x.T, -sin_x.T], axis=1)), axis=1)
    return z_forward, z_inverse, y_table, x_table


def split(value):
    high = value.astype(BF16)
    return high, (value - high.astype(F32)).astype(BF16)


def dot(left, right, dims):
    return lax.dot_general(left, right, (dims, ((), ())), preferred_element_type=F32)


NN = ((1,), (0,))
NT = ((1,), (1,))


ROOT = math.sqrt(2.0 / math.pi)
CUBE = 0.044715


def gelu(value):
    inner = value * (ROOT + (ROOT * CUBE) * (value * value))
    half = 0.5 * value
    return half + half * jnp.tanh(inner)


def gelu_both(value):
    square = value * value
    bent = jnp.tanh(value * (ROOT + (ROOT * CUBE) * square))
    slope = ROOT + (3.0 * ROOT * CUBE) * square
    cdf = 0.5 + 0.5 * bent
    return value * cdf, cdf + (0.5 * value) * ((1.0 - bent * bent) * slope)


def bent_half(half):
    return half * jnp.tanh(half * (2.0 * ROOT + (8.0 * ROOT * CUBE) * (half * half)))


def lift(field, half_scale, half_shift):
    scaled = half_scale * field
    return (scaled + scaled) + (bent_half(half_shift + scaled) - bent_half(half_shift - scaled))


def lane_index(shape):
    return lax.broadcasted_iota(jnp.int32, shape, len(shape) - 1)


def swapped(value):
    return pltpu.roll(value, MODES, 1)


def beside_z(value, lane):
    left = jnp.where(lane == 0, 0.0, pltpu.roll(value, 1, 1))
    return left + jnp.where(lane == GRID - 1, 0.0, pltpu.roll(value, GRID - 1, 1))


def plane_forward(fill, z_table, y_table, stage_high, stage_low, lines, out):
    for channel in range(HALF):
        fill(channel, stage_high, stage_low)
        z = dot(z_table[...], stage_high[...], NN)
        z = z[:128] + z[128:] + dot(z_table[0:128, :], stage_low[...], NN)
        lines[:, channel, 0:GRID] = z[:MODES]
        lines[:, channel, GRID:] = z[MODES:]
    high, low = split(lines[...].reshape(MODES * HALF, 2 * GRID))
    spectrum = dot(y_table[...], high, NT)
    spectrum = spectrum[:128] + spectrum[128:] + dot(y_table[0:128, :], low, NT)
    lane = lane_index((ROWS, 128)) // 32
    for tile in range(4):
        parts = [spectrum[b * 32 : b * 32 + 32, tile * 128 : tile * 128 + 128] for b in range(4)]
        for e in range(4):
            total = None
            for b in range(4):
                turn = ((b - e) % 4) * 32
                moved = pltpu.roll(parts[b], turn, 1) if turn else parts[b]
                total = moved if total is None else jnp.where(lane == b, moved, total)
            column = 4 * tile + e
            out[column * 32 : column * 32 + 32, :] = total


def lift_kernel(plane, z_table, y_table, scalars, out, turned, high, low, lines):
    turned[...] = plane[...].T

    def fill(channel, stage_high, stage_low):
        gain, offset = scalars[channel : channel + 1, :], scalars[HALF + channel : HALF + channel + 1, :]
        for t in range(8):
            rows = slice(32 * t, 32 * t + 32)
            stage_high[rows, :], stage_low[rows, :] = split(lift(turned[rows, :], gain, offset))

    plane_forward(fill, z_table, y_table, high, low, lines, out)


def grad_kernel(adjoint, rest, z_table, y_table, *refs):
    slope = refs[:HALF]
    out, residual, turned, high, low, lines, sem = refs[HALF:]
    copy = pltpu.make_async_copy(rest, residual, sem)
    copy.start()
    turned[...] = adjoint[...].T

    def fill(channel, stage_high, stage_low):
        for t in range(8):
            rows = slice(32 * t, 32 * t + 32)
            stage_high[rows, :], stage_low[rows, :] = split(turned[rows, :] * slope[channel][rows, :])

    plane_forward(fill, z_table, y_table, high, low, lines, out)
    copy.wait()


def first_kernel(
    far_field, far_z, far_y, far_scale, far_shift, far_readout, spread, z_table, y_table, scalars, ring, doubling, *scratch
):
    scale, shift, readout, sems = scratch
    core, row_place, col_place = lax.axis_index("core"), lax.axis_index(ROW), lax.axis_index(COL)
    pairs = [(far_scale, scale), (far_shift, shift), (far_readout, readout), (far_z, z_table), (far_y, y_table)]
    pairs += [(far_field, spread.at[:, k]) for k in range(2)]
    copies = [pltpu.make_async_copy(source, target, sems.at[n]) for n, (source, target) in enumerate(pairs)]
    for copy in copies:
        copy.start()
    row = lax.broadcasted_iota(jnp.int32, (24, GRID), 0)
    first_row = jnp.where(col_place == 0, 4, 3)
    last_row = jnp.where(col_place == COLS - 1, 19, 20)
    ring[0:24, :] = jnp.where(jnp.logical_and(row >= first_row, row <= last_row), 1.0, 0.0).astype(F32)
    row = lax.broadcasted_iota(jnp.int32, (8, GRID), 0)
    before, after = jnp.where(row_place > 0, 1.0, 0.0), jnp.where(row_place < ROWS - 1, 1.0, 0.0)
    odd = jnp.where(row_place % 2 == 1, 1.0, 0.0)
    ring[24:32, :] = jnp.where(row == 0, before, jnp.where(row == 1, after, odd)).astype(F32)
    row = lax.broadcasted_iota(jnp.int32, (64, 128), 0)
    zero_mode = jnp.logical_and((row // HALF) % 4 == 0, col_place == 0)
    doubling[...] = jnp.where(zero_mode, 1.0, 2.0).astype(F32)
    for copy in copies[:3]:
        copy.wait()
    first = core * HALF
    for n in range(HALF):
        for m, value in enumerate((0.5 * scale[first + n], 0.5 * shift[first + n], readout[first + n])):
            scalars[HALF * m + n : HALF * m + n + 1, :] = jnp.full((1, GRID), value, F32)
    for copy in copies[3:]:
        copy.wait()


def local_kernel(scale, shift, bias, weight, plane, margin, *refs):
    out, turned = refs[:HALF], refs[HALF]
    core = lax.axis_index("core")
    first = core * HALF
    keep = jnp.where(core == 0, 1.0, 0.0).astype(F32)
    turned[...] = plane[...].T
    margin[...] = jnp.zeros(margin.shape, F32)
    for c in range(1, COLS):
        margin[c : c + 1, :] = plane[16 * c - 1 : 16 * c, :] * keep
        margin[COLS + c - 1 : COLS + c, :] = plane[16 * c : 16 * c + 1, :] * keep

    def step(t, carry):
        rows = pl.ds(pl.multiple_of(t * 16, 16), 16)
        field = turned[rows, :]
        sums = [jnp.full((16, GRID), bias[first + o], F32) for o in range(HALF)]
        for i in range(WIDTH):
            lifted = lift(field, 0.5 * scale[i], 0.5 * shift[i])
            sums = [sums[o] + weight[i, first + o] * lifted for o in range(HALF)]
        for o in range(HALF):
            out[o][rows, :] = sums[o]
        return carry

    lax.fori_loop(0, GRID // 16, step, 0)


def inverse_kernel(received, margin, z_table, y_table, scalars, *refs):
    local, out, slope = refs[:HALF], refs[HALF], refs[HALF + 1 : 2 * HALF + 1]
    grid, lines, spectral, total, padded = refs[2 * HALF + 1 :]
    lane = lane_index((ROWS, 128)) // 32
    for tile in range(4):
        parts = [received[(4 * tile + e) * 32 : (4 * tile + e) * 32 + 32, :] for e in range(4)]
        for b in range(4):
            whole = None
            for e in range(4):
                turn = ((e - b) % 4) * 32
                moved = pltpu.roll(parts[e], turn, 1) if turn else parts[e]
                whole = moved if whole is None else jnp.where(lane == e, moved, whole)
            grid[b * 32 : b * 32 + 32, tile * 128 : tile * 128 + 128] = whole
    high, low = split(grid[...].T)
    modes = dot(jnp.concatenate([high, high], axis=1), y_table[...], NN) + dot(low, y_table[0:128, :], NN)
    lines[...] = modes.reshape(MODES, HALF, 2 * GRID)
    for o in range(HALF):
        modes = jnp.concatenate([lines[:, o, 0:GRID], lines[:, o, GRID:]], axis=0)
        product = dot(z_table[...], jnp.concatenate(split(modes), axis=0), NN)
        spectral[...] = product[:GRID] + product[GRID:]
        read = scalars[2 * HALF + o : 2 * HALF + o + 1, :]
        for t in range(8):
            rows = slice(32 * t, 32 * t + 32)
            value = spectral[rows, :] + local[o][rows, :]
            value, derivative = gelu_both(value)
            slope[o][rows, :] = read * derivative
            if o == 0:
                total[rows, :] = read * value
            else:
                total[rows, :] += read * value
    padded[0:8, :] = jnp.zeros((8, GRID), F32)
    padded[256:264, :] = jnp.zeros((8, GRID), F32)
    value = total[...].T
    padded[4:260, :] = value
    beside = pltpu.roll(value, 1, 0) + pltpu.roll(value, GRID - 1, 0) + beside_z(value, lane_index((GRID, GRID)))
    spectral[...] = 6.0 * value - beside
    blank = jnp.zeros((1, GRID), F32)
    for c in range(COLS):
        before, after = blank, blank
        if c > 0:
            before = spectral[16 * c - 1 : 16 * c, :] - margin[c : c + 1, :]
        if c < COLS - 1:
            after = spectral[16 * c + 16 : 16 * c + 17, :] - margin[COLS + c : COLS + c + 1, :]
        for h in range(2):
            lanes = slice(128 * h, 128 * h + 128)
            out[c, 20 * h : 20 * h + 1, :] = before[:, lanes]
            out[c, 20 * h + 1 : 20 * h + 19, :] = padded[16 * c + 3 : 16 * c + 21, lanes]
            out[c, 20 * h + 19 : 20 * h + 20, :] = after[:, lanes]


def gather_spectra(received, x_table, sign):
    lines = []
    for k in range(2):
        parts = [received[(2 * q + k) * 32 : (2 * q + k) * 32 + 32, :] for q in range(PLANES)]
        lines.append(jnp.concatenate(parts, axis=0).T)
    product = dot(jnp.concatenate(split(jnp.concatenate(lines, axis=0)), axis=0), x_table[...], NN)
    product = product[:, :128] + product[:, 128:]
    product = product[:256] + product[256:]
    first = [product[128 * k : 128 * k + 64] for k in range(2)]
    second = [product[128 * k + 64 : 128 * k + 128] for k in range(2)]
    return [first[k] + sign * swapped(second[k]) for k in range(2)]


def mix_kernel(received, weight, x_table, out, spectra_out, real, imag):
    low = lane_index((64, 128)) < MODES
    sign = jnp.where(low, -1.0, 1.0).astype(F32)
    for k, spectra in enumerate(gather_spectra(received, x_table, sign)):
        spectra_out[k] = spectra
        other = swapped(spectra)
        real[k] = jnp.where(low, spectra, other)
        imag[k] = jnp.where(low, other, spectra)
    parts = [[], []]
    for group in range(8):
        a, j = group // 4, group % 4
        first = jnp.zeros((WIDTH, 128), F32)
        second = jnp.zeros((WIDTH, 128), F32)
        for i in range(WIDTH):
            k, row = i // HALF, group * HALF + i % HALF
            tile = weight[a, j, i].astype(F32)
            first = first + tile * real[k, row : row + 1, :]
            second = second + tile * imag[k, row : row + 1, :]
        mixed = first + sign[:WIDTH] * swapped(second)
        parts[0].append(mixed[:HALF])
        parts[1].append(mixed[HALF:])
    both = []
    for k in range(2):
        mixed = jnp.concatenate(parts[k], axis=0)
        both += [mixed, -sign * swapped(mixed)]
    high, low = split(jnp.concatenate(both, axis=0))
    result = dot(x_table[...], jnp.concatenate([high, high], axis=1), NT) + dot(x_table[:, 0:128], low, NT)
    for q in range(PLANES):
        for k in range(2):
            place = (2 * q + k) * 32
            out[place : place + 32, :] = result[q * 32 : q * 32 + 32, k * 128 : k * 128 + 128]


def outer_kernel(received, spectra_in, x_table, doubling, out, real, imag, stage, sems):
    low = lane_index((64, 128)) < MODES
    sign = jnp.where(low, -1.0, 1.0).astype(F32)
    grads = [doubling[...] * g for g in gather_spectra(received, x_table, sign)]
    turned = [-sign * swapped(g) for g in grads]
    for k in range(2):
        spectra = spectra_in[k]
        other = swapped(spectra)
        real[k] = jnp.where(low, spectra, other)
        imag[k] = jnp.where(low, other, spectra)
    copies = []
    for group in range(8):
        a, j = group // 4, group % 4
        rows = slice(group * HALF, group * HALF + HALF)
        straight = jnp.concatenate([grads[0][rows], grads[1][rows]], axis=0)
        crossed = jnp.concatenate([turned[0][rows], turned[1][rows]], axis=0)
        for i in range(WIDTH):
            k, line = i // HALF, group * HALF + i % HALF
            value = straight * real[k, line : line + 1, :] + crossed * imag[k, line : line + 1, :]
            stage[a, j, i] = value.astype(BF16)
        copies.append(pltpu.make_async_copy(stage.at[a, j], out.at[a, j], sems.at[group]))
        copies[-1].start()
    for copy in copies:
        copy.wait()


def beside_y(value):
    return pltpu.roll(value, 1, 0) + pltpu.roll(value, 23, 0)


def edge_kernel(received, field, ring, wide, first, second):
    lane = lane_index((24, GRID))
    for q in range(PLANES):
        wide[q] = jnp.zeros((24, GRID), F32)
        for h in range(2):
            lanes = slice(128 * h, 128 * h + 128)
            both = received[2 * q, 20 * h : 20 * h + 20, :] + received[2 * q + 1, 20 * h : 20 * h + 20, :]
            wide[q, 3:21, lanes] = both[1:19]
            wide[q, 1:2, lanes] = both[0:1]
            wide[q, 22:23, lanes] = both[19:20]
    sent = []
    for edge, inner in ((0, 1), (PLANES - 1, PLANES - 2)):
        value = wide[edge]
        rest = 6.0 * value - (wide[inner] + beside_y(value) + beside_z(value, lane))
        rest = rest[4:20] - field[edge]
        sent.append(jnp.concatenate([value[:, :128], value[:, 128:], rest[:, :128], rest[:, 128:]], axis=0))
    odd = jnp.broadcast_to(ring[26:27, 0:128], (80, 128)) > 0.5
    first[...] = jnp.where(odd, sent[1], sent[0])
    second[...] = jnp.where(odd, sent[0], sent[1])


def inner_kernel(wide, field, ring, rest):
    lane = lane_index((24, GRID))
    for q in range(PLANES):
        centre = wide[q]
        across = jnp.zeros((24, GRID), F32)
        if q > 0:
            across = across + wide[q - 1]
        if q < PLANES - 1:
            across = across + wide[q + 1]
        value = 6.0 * centre - (beside_y(centre) + beside_z(centre, lane) + across)
        rest[q] = value
        rest[q, 4:20, :] = value[4:20] - field[q]
        rest[q, 3:4, :] = ring[3:4, :] * (wide[q, 1:2, :] - across[3:4])
        rest[q, 20:21, :] = ring[20:21, :] * (wide[q, 22:23, :] - across[20:21])


def stencil_kernel(rest, wide, first, second, ring, residual, adjoint):
    lane = lane_index((24, GRID))
    inside = ring[0:24, :]
    values = [rest[q] for q in range(PLANES)]
    odd = jnp.broadcast_to(ring[26:27, 0:128], (80, 128)) > 0.5
    before, after = jnp.where(odd, second[...], first[...]), jnp.where(odd, first[...], second[...])
    outer = []
    for n, ref, edge in ((0, before, 0), (1, after, PLANES - 1)):
        beyond = jnp.concatenate([ref[0:24], ref[24:48]], axis=1)
        values[edge] = values[edge] - inside * beyond
        part = jnp.concatenate([ref[48:64], ref[64:80]], axis=1) - wide[edge, 4:20, :]
        outer.append(ring[24 + n : 25 + n, :] * part)
    for q in range(PLANES):
        low = outer[0] if q == 0 else values[q - 1][4:20]
        high = outer[1] if q == PLANES - 1 else values[q + 1][4:20]
        residual[q] = values[q][4:20]
        near = (beside_y(values[q]) + beside_z(values[q], lane))[4:20]
        value = 6.0 * values[q][4:20] - (low + high + near)
        adjoint[2 * q] = value
        adjoint[2 * q + 1] = value


def call(kernel, operands, scalars, outputs, scratch, flops=0, far=0, far_out=()):
    many = isinstance(outputs, list)
    vmem = pl.BlockSpec(memory_space=pltpu.VMEM)
    smem = pl.BlockSpec(memory_space=pltpu.SMEM)
    hbm = pl.BlockSpec(memory_space=pltpu.HBM)
    out_specs = [hbm if n in far_out else vmem for n in range(len(outputs) if many else 1)]
    operands = list(operands)
    for n in range(len(operands) - far, len(operands)):
        operands[n] = pltpu.with_memory_space_constraint(operands[n], pltpu.HBM)
    cost = pl.CostEstimate(flops=flops, bytes_accessed=4 << 20, transcendentals=flops // 16)
    return pl.pallas_call(
        kernel,
        in_specs=[smem] * len(scalars) + [vmem] * (len(operands) - far) + [hbm] * far,
        out_specs=out_specs if many else out_specs[0],
        out_shape=outputs,
        scratch_shapes=scratch,
        compiler_params=pltpu.CompilerParams(vmem_limit_bytes=VMEM_LIMIT),
        cost_estimate=cost if flops else None,
    )(*scalars, *operands)


def exchange(value, axes):
    return lax.all_to_all(value, axes, split_axis=0, concat_axis=0, tiled=True)


def shape(*sizes):
    return jax.ShapeDtypeStruct(sizes, F32)


def shards(right_side, lift_scale, lift_shift, spectral_weight, local_weight, local_bias, readout):
    z_forward, z_inverse, y_table, x_table = tables()
    everywhere = COL + ROW
    field = right_side[0]
    fields = [shape(GRID, GRID)] * HALF

    row_of = pltpu.SMEM((WIDTH,), F32)
    spread, z_near, y_near, scalars, ring, doubling = call(
        first_kernel,
        (field, z_forward, y_table, lift_scale, lift_shift, readout),
        (),
        [
            shape(PLANES, 2, COLS, GRID),
            jax.ShapeDtypeStruct(z_forward.shape, BF16),
            jax.ShapeDtypeStruct(y_table.shape, BF16),
            shape(24, GRID),
            shape(32, GRID),
            shape(64, 128),
        ],
        [row_of, row_of, row_of, pltpu.SemaphoreType.DMA((7,))],
        far=6,
    )
    plane = exchange(spread.reshape(COLS, COLS, GRID), COL).reshape(GRID, GRID)
    line_scratch = pltpu.VMEM((MODES, HALF, 2 * GRID), F32)
    plane_scratch = [
        pltpu.VMEM((GRID, GRID), F32),
        pltpu.VMEM((GRID, GRID), BF16),
        pltpu.VMEM((GRID, GRID), BF16),
        line_scratch,
    ]
    lifted = call(lift_kernel, (plane, z_near, y_near, scalars), (), shape(512, 128), plane_scratch)
    lifted = exchange(lifted, everywhere)
    margin, *local = call(
        local_kernel,
        (plane,),
        (lift_scale, lift_shift, local_bias, local_weight),
        [shape(2 * COLS, GRID)] + fields,
        [pltpu.VMEM((GRID, GRID), F32)],
        flops=1 << 27,
    )
    pair = pltpu.VMEM((2, 64, 128), F32)
    mixed, spectra = call(
        mix_kernel, (lifted, spectral_weight, x_table), (), [shape(512, 128), shape(2, 64, 128)], [pair, pair]
    )
    mixed = exchange(mixed, everywhere)
    message, *slope = call(
        inverse_kernel,
        (mixed, margin, z_inverse, y_table, scalars, *local),
        (),
        [shape(COLS, 40, 128)] + fields,
        [
            pltpu.VMEM((128, 512), F32),
            line_scratch,
            pltpu.VMEM((GRID, GRID), F32),
            pltpu.VMEM((GRID, GRID), F32),
            pltpu.VMEM((GRID + 8, GRID), F32),
        ],
    )
    message = exchange(message, COL)
    wide, first, second = call(
        edge_kernel, (message, field, ring), (), [shape(PLANES, 24, GRID), shape(80, 128), shape(80, 128)], []
    )
    odd_pairs = [(r, r + 1 if r % 2 else r - 1) for r in range(1, ROWS - 1)]
    even_pairs = [(r, r - 1 if r % 2 else r + 1) for r in range(ROWS)]
    first = lax.ppermute(first, ROW, odd_pairs)
    second = lax.ppermute(second, ROW, even_pairs)
    rest = call(
        inner_kernel,
        (wide, field, ring),
        (),
        shape(PLANES, 24, GRID),
        [],
        flops=1 << 22,
    )
    rest, adjoint = call(
        stencil_kernel,
        (rest, wide, first, second, ring),
        (),
        [shape(PLANES, COLS, GRID), shape(2 * PLANES, COLS, GRID)],
        [],
    )
    adjoint = exchange(adjoint, COL).reshape(GRID, GRID)
    grads, residual = call(
        grad_kernel,
        (adjoint, rest, z_forward, y_table, *slope),
        (),
        [shape(512, 128), shape(PLANES, COLS, GRID)],
        plane_scratch + [pltpu.SemaphoreType.DMA],
        far_out=(1,),
    )
    grads = exchange(grads, everywhere)
    spectral_grad = call(
        outer_kernel,
        (grads, spectra, x_table, doubling),
        (),
        jax.ShapeDtypeStruct(spectral_weight.shape, BF16),
        [pair, pair, pltpu.VMEM(spectral_weight.shape, BF16), pltpu.SemaphoreType.DMA((8,))],
        far_out=(0,),
    )
    return residual[None], spectral_grad


def solution(mesh):
    fine = Mesh(mesh.devices.reshape(8, 4, 2, 4, 2), ROW + COL)
    in_specs = (P(None, ROW, COL, None), P(), P(), P(ROW, COL, None, None, None), P(), P(), P())
    out_specs = (P(None, ROW, COL, None), P(ROW, COL, None, None, None))
    return jax.shard_map(shards, mesh=fine, in_specs=in_specs, out_specs=out_specs, check_vma=False)
```

```python
import math

import jax
import jax.numpy as jnp
import numpy as np
from jax import lax
from jax.experimental import pallas as pl
from jax.experimental.pallas import tpu as pltpu
from jax.sharding import Mesh
from jax.sharding import PartitionSpec as P

MODES = 64
GRID = 256
WIDTH = 16
HALF = 8
ROWS = 32
PLANES = 8
COLS = 16
ROW = ("y", "zh")
COL = ("zl", "x", "core")
F32 = jnp.float32
BF16 = jnp.bfloat16
VMEM_LIMIT = 40 * 1024 * 1024


def halves(table):
    high = table.astype(jnp.bfloat16)
    low = (table - high.astype(np.float64)).astype(jnp.bfloat16)
    return high, low


def wave(frequencies, points):
    phase = (np.outer(frequencies, points) % GRID) * (2.0 * math.pi / GRID)
    return np.cos(phase) / 16.0, np.sin(phase) / 16.0


def tables():
    points = np.arange(GRID)
    cos_z, sin_z = wave(np.arange(MODES), points)
    z_forward = np.concatenate(halves(np.concatenate([cos_z, -sin_z], axis=0)), axis=0)
    weight = np.where(np.arange(MODES) == 0, 1.0, 2.0)[:, None]
    high, low = halves(np.concatenate([cos_z * weight, -sin_z * weight], axis=0).T)
    z_inverse = np.block([[high, high], [low, np.zeros_like(low)]])
    ky = np.array([2 * r + a - MODES // 2 for a in range(2) for r in range(ROWS)])
    cos_y, sin_y = wave(ky, points)
    y_table = np.concatenate(
        [np.concatenate([cos_y, sin_y], axis=1), np.concatenate([-sin_y, cos_y], axis=1)], axis=0
    )
    y_table = np.concatenate(halves(y_table), axis=0)
    places = np.array([8 * r + q for q in range(PLANES) for r in range(ROWS)])
    cos_x, sin_x = wave(np.arange(MODES) - MODES // 2, places)
    x_table = np.concatenate(halves(np.concatenate([cos_x.T, -sin_x.T], axis=1)), axis=1)
    return z_forward, z_inverse, y_table, x_table


def split(value):
    high = value.astype(BF16)
    return high, (value - high.astype(F32)).astype(BF16)


def dot(left, right, dims):
    return lax.dot_general(left, right, (dims, ((), ())), preferred_element_type=F32)


NN = ((1,), (0,))
NT = ((1,), (1,))


ROOT = math.sqrt(2.0 / math.pi)
CUBE = 0.044715


def gelu_double(value, square):
    return 1.0 + jnp.tanh(value * (ROOT + (ROOT * CUBE) * square))


def gelu_slope(value):
    square = value * value
    double = gelu_double(value, square)
    slope = (0.5 * ROOT) + (1.5 * ROOT * CUBE) * square
    return double * (0.5 + (value * slope) * (2.0 - double))


def bent_half(half):
    return half * jnp.tanh(half * (2.0 * ROOT + (8.0 * ROOT * CUBE) * (half * half)))


def lift(field, half_scale, half_shift):
    scaled = half_scale * field
    return (scaled + scaled) + (bent_half(half_shift + scaled) - bent_half(half_shift - scaled))


def lane_index(shape):
    return lax.broadcasted_iota(jnp.int32, shape, len(shape) - 1)


def swapped(value):
    return pltpu.roll(value, MODES, 1)


def beside_z(value, lane):
    left = jnp.where(lane == 0, 0.0, pltpu.roll(value, 1, 1))
    return left + jnp.where(lane == GRID - 1, 0.0, pltpu.roll(value, GRID - 1, 1))


def plane_forward(fill, z_table, y_table, stage_high, stage_low, lines, out):
    for channel in range(HALF):
        fill(channel, stage_high, stage_low)
        z = dot(z_table[...], stage_high[...], NN)
        z = z[:128] + z[128:] + dot(z_table[0:128, :], stage_low[...], NN)
        lines[:, channel, 0:GRID] = z[:MODES]
        lines[:, channel, GRID:] = z[MODES:]
    high, low = split(lines[...].reshape(MODES * HALF, 2 * GRID))
    spectrum = dot(y_table[...], high, NT)
    spectrum = spectrum[:128] + spectrum[128:] + dot(y_table[0:128, :], low, NT)
    lane = lane_index((ROWS, 128)) // 32
    for tile in range(4):
        parts = [spectrum[b * 32 : b * 32 + 32, tile * 128 : tile * 128 + 128] for b in range(4)]
        for e in range(4):
            total = None
            for b in range(4):
                turn = ((b - e) % 4) * 32
                moved = pltpu.roll(parts[b], turn, 1) if turn else parts[b]
                total = moved if total is None else jnp.where(lane == b, moved, total)
            column = 4 * tile + e
            out[column * 32 : column * 32 + 32, :] = total


def lift_kernel(plane, z_table, y_table, scalars, out, turned, high, low, lines):
    turned[...] = plane[...].T

    def fill(channel, stage_high, stage_low):
        gain, offset = scalars[channel : channel + 1, :], scalars[HALF + channel : HALF + channel + 1, :]
        for t in range(8):
            rows = slice(32 * t, 32 * t + 32)
            stage_high[rows, :], stage_low[rows, :] = split(lift(turned[rows, :], gain, offset))

    plane_forward(fill, z_table, y_table, high, low, lines, out)


def grad_kernel(adjoint, rest, z_table, y_table, *refs):
    slope = refs[:HALF]
    out, residual, turned, high, low, lines, sem = refs[HALF:]
    copy = pltpu.make_async_copy(rest, residual, sem)
    copy.start()
    turned[...] = adjoint[...].T

    def fill(channel, stage_high, stage_low):
        for t in range(8):
            rows = slice(32 * t, 32 * t + 32)
            stage_high[rows, :], stage_low[rows, :] = split(turned[rows, :] * slope[channel][rows, :])

    plane_forward(fill, z_table, y_table, high, low, lines, out)
    copy.wait()


def first_kernel(
    far_field, far_z, far_y, far_scale, far_shift, far_readout, spread, z_table, y_table, scalars, ring, doubling, *scratch
):
    scale, shift, readout, sems = scratch
    core, row_place, col_place = lax.axis_index("core"), lax.axis_index(ROW), lax.axis_index(COL)
    pairs = [(far_scale, scale), (far_shift, shift), (far_readout, readout), (far_z, z_table), (far_y, y_table)]
    pairs += [(far_field, spread.at[:, k]) for k in range(2)]
    copies = [pltpu.make_async_copy(source, target, sems.at[n]) for n, (source, target) in enumerate(pairs)]
    for copy in copies:
        copy.start()
    row = lax.broadcasted_iota(jnp.int32, (24, GRID), 0)
    first_row = jnp.where(col_place == 0, 4, 3)
    last_row = jnp.where(col_place == COLS - 1, 19, 20)
    ring[0:24, :] = jnp.where(jnp.logical_and(row >= first_row, row <= last_row), 1.0, 0.0).astype(F32)
    row = lax.broadcasted_iota(jnp.int32, (8, GRID), 0)
    before, after = jnp.where(row_place > 0, 1.0, 0.0), jnp.where(row_place < ROWS - 1, 1.0, 0.0)
    odd = jnp.where(row_place % 2 == 1, 1.0, 0.0)
    ring[24:32, :] = jnp.where(row == 0, before, jnp.where(row == 1, after, odd)).astype(F32)
    row = lax.broadcasted_iota(jnp.int32, (64, 128), 0)
    zero_mode = jnp.logical_and((row // HALF) % 4 == 0, col_place == 0)
    doubling[...] = jnp.where(zero_mode, 1.0, 2.0).astype(F32)
    for copy in copies[:3]:
        copy.wait()
    first = core * HALF
    for n in range(HALF):
        for m, value in enumerate((0.5 * scale[first + n], 0.5 * shift[first + n], readout[first + n])):
            scalars[HALF * m + n : HALF * m + n + 1, :] = jnp.full((1, GRID), value, F32)
    for copy in copies[3:]:
        copy.wait()


def local_kernel(scale, shift, bias, weight, plane, margin, *refs):
    out, turned = refs[:HALF], refs[HALF]
    core = lax.axis_index("core")
    first = core * HALF
    keep = jnp.where(core == 0, 1.0, 0.0).astype(F32)
    turned[...] = plane[...].T
    margin[...] = jnp.zeros(margin.shape, F32)
    for c in range(1, COLS):
        margin[c : c + 1, :] = plane[16 * c - 1 : 16 * c, :] * keep
        margin[COLS + c - 1 : COLS + c, :] = plane[16 * c : 16 * c + 1, :] * keep

    def step(t, carry):
        rows = pl.ds(pl.multiple_of(t * 16, 16), 16)
        field = turned[rows, :]
        sums = [jnp.full((16, GRID), bias[first + o], F32) for o in range(HALF)]
        for i in range(WIDTH):
            lifted = lift(field, 0.5 * scale[i], 0.5 * shift[i])
            sums = [sums[o] + weight[i, first + o] * lifted for o in range(HALF)]
        for o in range(HALF):
            out[o][rows, :] = sums[o]
        return carry

    lax.fori_loop(0, GRID // 16, step, 0)


def inverse_kernel(received, margin, z_table, y_table, scalars, *refs):
    local, out, preact = refs[:HALF], refs[HALF], refs[HALF + 1 : 2 * HALF + 1]
    grid, lines, spectral, total, padded = refs[2 * HALF + 1 :]
    lane = lane_index((ROWS, 128)) // 32
    for tile in range(4):
        parts = [received[(4 * tile + e) * 32 : (4 * tile + e) * 32 + 32, :] for e in range(4)]
        for b in range(4):
            whole = None
            for e in range(4):
                turn = ((e - b) % 4) * 32
                moved = pltpu.roll(parts[e], turn, 1) if turn else parts[e]
                whole = moved if whole is None else jnp.where(lane == e, moved, whole)
            grid[b * 32 : b * 32 + 32, tile * 128 : tile * 128 + 128] = whole
    high, low = split(grid[...].T)
    modes = dot(jnp.concatenate([high, high], axis=1), y_table[...], NN) + dot(low, y_table[0:128, :], NN)
    lines[...] = modes.reshape(MODES, HALF, 2 * GRID)
    for o in range(HALF):
        modes = jnp.concatenate([lines[:, o, 0:GRID], lines[:, o, GRID:]], axis=0)
        product = dot(z_table[...], jnp.concatenate(split(modes), axis=0), NN)
        spectral[...] = product[:GRID] + product[GRID:]
        read = 0.5 * scalars[2 * HALF + o : 2 * HALF + o + 1, :]
        for t in range(8):
            rows = slice(32 * t, 32 * t + 32)
            value = spectral[rows, :] + local[o][rows, :]
            preact[o][rows, :] = value
            term = (read * value) * gelu_double(value, value * value)
            if o == 0:
                total[rows, :] = term
            else:
                total[rows, :] += term
    padded[0:8, :] = jnp.zeros((8, GRID), F32)
    padded[256:264, :] = jnp.zeros((8, GRID), F32)
    value = total[...].T
    padded[4:260, :] = value
    beside = pltpu.roll(value, 1, 0) + pltpu.roll(value, GRID - 1, 0) + beside_z(value, lane_index((GRID, GRID)))
    spectral[...] = 6.0 * value - beside
    blank = jnp.zeros((1, GRID), F32)
    for c in range(COLS):
        before, after = blank, blank
        if c > 0:
            before = spectral[16 * c - 1 : 16 * c, :] - margin[c : c + 1, :]
        if c < COLS - 1:
            after = spectral[16 * c + 16 : 16 * c + 17, :] - margin[COLS + c : COLS + c + 1, :]
        for h in range(2):
            lanes = slice(128 * h, 128 * h + 128)
            out[c, 20 * h : 20 * h + 1, :] = before[:, lanes]
            out[c, 20 * h + 1 : 20 * h + 19, :] = padded[16 * c + 3 : 16 * c + 21, lanes]
            out[c, 20 * h + 19 : 20 * h + 20, :] = after[:, lanes]


def slope_kernel(scalars, *refs):
    preact, out = refs[:HALF], refs[HALF:]
    for o in range(HALF):
        read = scalars[2 * HALF + o : 2 * HALF + o + 1, :]
        for t in range(8):
            rows = slice(32 * t, 32 * t + 32)
            out[o][rows, :] = read * gelu_slope(preact[o][rows, :])


def gather_spectra(received, x_table, sign):
    lines = []
    for k in range(2):
        parts = [received[(2 * q + k) * 32 : (2 * q + k) * 32 + 32, :] for q in range(PLANES)]
        lines.append(jnp.concatenate(parts, axis=0).T)
    product = dot(jnp.concatenate(split(jnp.concatenate(lines, axis=0)), axis=0), x_table[...], NN)
    product = product[:, :128] + product[:, 128:]
    product = product[:256] + product[256:]
    first = [product[128 * k : 128 * k + 64] for k in range(2)]
    second = [product[128 * k + 64 : 128 * k + 128] for k in range(2)]
    return [first[k] + sign * swapped(second[k]) for k in range(2)]


def mix_kernel(received, weight, x_table, out, spectra_out, real, imag):
    low = lane_index((64, 128)) < MODES
    sign = jnp.where(low, -1.0, 1.0).astype(F32)
    for k, spectra in enumerate(gather_spectra(received, x_table, sign)):
        spectra_out[k] = spectra
        other = swapped(spectra)
        real[k] = jnp.where(low, spectra, other)
        imag[k] = jnp.where(low, other, spectra)
    parts = [[], []]
    for group in range(8):
        a, j = group // 4, group % 4
        first = jnp.zeros((WIDTH, 128), F32)
        second = jnp.zeros((WIDTH, 128), F32)
        for i in range(WIDTH):
            k, row = i // HALF, group * HALF + i % HALF
            tile = weight[a, j, i].astype(F32)
            first = first + tile * real[k, row : row + 1, :]
            second = second + tile * imag[k, row : row + 1, :]
        mixed = first + sign[:WIDTH] * swapped(second)
        parts[0].append(mixed[:HALF])
        parts[1].append(mixed[HALF:])
    both = []
    for k in range(2):
        mixed = jnp.concatenate(parts[k], axis=0)
        both += [mixed, -sign * swapped(mixed)]
    high, low = split(jnp.concatenate(both, axis=0))
    result = dot(x_table[...], jnp.concatenate([high, high], axis=1), NT) + dot(x_table[:, 0:128], low, NT)
    for q in range(PLANES):
        for k in range(2):
            place = (2 * q + k) * 32
            out[place : place + 32, :] = result[q * 32 : q * 32 + 32, k * 128 : k * 128 + 128]


def outer_kernel(received, spectra_in, x_table, doubling, out, real, imag, stage, sems):
    low = lane_index((64, 128)) < MODES
    sign = jnp.where(low, -1.0, 1.0).astype(F32)
    grads = [doubling[...] * g for g in gather_spectra(received, x_table, sign)]
    turned = [-sign * swapped(g) for g in grads]
    for k in range(2):
        spectra = spectra_in[k]
        other = swapped(spectra)
        real[k] = jnp.where(low, spectra, other)
        imag[k] = jnp.where(low, other, spectra)
    copies = []
    for group in range(8):
        a, j = group // 4, group % 4
        rows = slice(group * HALF, group * HALF + HALF)
        straight = jnp.concatenate([grads[0][rows], grads[1][rows]], axis=0)
        crossed = jnp.concatenate([turned[0][rows], turned[1][rows]], axis=0)
        for i in range(WIDTH):
            k, line = i // HALF, group * HALF + i % HALF
            value = straight * real[k, line : line + 1, :] + crossed * imag[k, line : line + 1, :]
            stage[a, j, i] = value.astype(BF16)
        copies.append(pltpu.make_async_copy(stage.at[a, j], out.at[a, j], sems.at[group]))
        copies[-1].start()
    for copy in copies:
        copy.wait()


def beside_y(value):
    return pltpu.roll(value, 1, 0) + pltpu.roll(value, 23, 0)


def edge_kernel(received, field, ring, wide, first, second):
    lane = lane_index((24, GRID))
    for q in range(PLANES):
        wide[q] = jnp.zeros((24, GRID), F32)
        for h in range(2):
            lanes = slice(128 * h, 128 * h + 128)
            both = received[2 * q, 20 * h : 20 * h + 20, :] + received[2 * q + 1, 20 * h : 20 * h + 20, :]
            wide[q, 3:21, lanes] = both[1:19]
            wide[q, 1:2, lanes] = both[0:1]
            wide[q, 22:23, lanes] = both[19:20]
    sent = []
    for edge, inner in ((0, 1), (PLANES - 1, PLANES - 2)):
        value = wide[edge]
        rest = 6.0 * value - (wide[inner] + beside_y(value) + beside_z(value, lane))
        rest = rest[4:20] - field[edge]
        sent.append(jnp.concatenate([value[:, :128], value[:, 128:], rest[:, :128], rest[:, 128:]], axis=0))
    odd = jnp.broadcast_to(ring[26:27, 0:128], (80, 128)) > 0.5
    first[...] = jnp.where(odd, sent[1], sent[0])
    second[...] = jnp.where(odd, sent[0], sent[1])


def inner_kernel(wide, field, ring, rest):
    lane = lane_index((24, GRID))
    for q in range(PLANES):
        centre = wide[q]
        across = jnp.zeros((24, GRID), F32)
        if q > 0:
            across = across + wide[q - 1]
        if q < PLANES - 1:
            across = across + wide[q + 1]
        value = 6.0 * centre - (beside_y(centre) + beside_z(centre, lane) + across)
        rest[q] = value
        rest[q, 4:20, :] = value[4:20] - field[q]
        rest[q, 3:4, :] = ring[3:4, :] * (wide[q, 1:2, :] - across[3:4])
        rest[q, 20:21, :] = ring[20:21, :] * (wide[q, 22:23, :] - across[20:21])


def stencil_kernel(rest, wide, first, second, ring, residual, adjoint):
    lane = lane_index((24, GRID))
    inside = ring[0:24, :]
    values = [rest[q] for q in range(PLANES)]
    odd = jnp.broadcast_to(ring[26:27, 0:128], (80, 128)) > 0.5
    before, after = jnp.where(odd, second[...], first[...]), jnp.where(odd, first[...], second[...])
    outer = []
    for n, ref, edge in ((0, before, 0), (1, after, PLANES - 1)):
        beyond = jnp.concatenate([ref[0:24], ref[24:48]], axis=1)
        values[edge] = values[edge] - inside * beyond
        part = jnp.concatenate([ref[48:64], ref[64:80]], axis=1) - wide[edge, 4:20, :]
        outer.append(ring[24 + n : 25 + n, :] * part)
    for q in range(PLANES):
        low = outer[0] if q == 0 else values[q - 1][4:20]
        high = outer[1] if q == PLANES - 1 else values[q + 1][4:20]
        residual[q] = values[q][4:20]
        near = (beside_y(values[q]) + beside_z(values[q], lane))[4:20]
        value = 6.0 * values[q][4:20] - (low + high + near)
        adjoint[2 * q] = value
        adjoint[2 * q + 1] = value


def call(kernel, operands, scalars, outputs, scratch, flops=0, far=0, far_out=(), aliases=None):
    many = isinstance(outputs, list)
    vmem = pl.BlockSpec(memory_space=pltpu.VMEM)
    smem = pl.BlockSpec(memory_space=pltpu.SMEM)
    hbm = pl.BlockSpec(memory_space=pltpu.HBM)
    out_specs = [hbm if n in far_out else vmem for n in range(len(outputs) if many else 1)]
    operands = list(operands)
    for n in range(len(operands) - far, len(operands)):
        operands[n] = pltpu.with_memory_space_constraint(operands[n], pltpu.HBM)
    cost = pl.CostEstimate(flops=flops, bytes_accessed=4 << 20, transcendentals=flops // 16)
    return pl.pallas_call(
        kernel,
        in_specs=[smem] * len(scalars) + [vmem] * (len(operands) - far) + [hbm] * far,
        out_specs=out_specs if many else out_specs[0],
        out_shape=outputs,
        scratch_shapes=scratch,
        input_output_aliases=aliases or {},
        compiler_params=pltpu.CompilerParams(vmem_limit_bytes=VMEM_LIMIT),
        cost_estimate=cost if flops else None,
    )(*scalars, *operands)


def exchange(value, axes):
    return lax.all_to_all(value, axes, split_axis=0, concat_axis=0, tiled=True)


def shape(*sizes):
    return jax.ShapeDtypeStruct(sizes, F32)


def shards(right_side, lift_scale, lift_shift, spectral_weight, local_weight, local_bias, readout):
    z_forward, z_inverse, y_table, x_table = tables()
    everywhere = COL + ROW
    field = right_side[0]
    fields = [shape(GRID, GRID)] * HALF

    row_of = pltpu.SMEM((WIDTH,), F32)
    spread, z_near, y_near, scalars, ring, doubling = call(
        first_kernel,
        (field, z_forward, y_table, lift_scale, lift_shift, readout),
        (),
        [
            shape(PLANES, 2, COLS, GRID),
            jax.ShapeDtypeStruct(z_forward.shape, BF16),
            jax.ShapeDtypeStruct(y_table.shape, BF16),
            shape(24, GRID),
            shape(32, GRID),
            shape(64, 128),
        ],
        [row_of, row_of, row_of, pltpu.SemaphoreType.DMA((7,))],
        far=6,
    )
    plane = exchange(spread.reshape(COLS, COLS, GRID), COL).reshape(GRID, GRID)
    line_scratch = pltpu.VMEM((MODES, HALF, 2 * GRID), F32)
    plane_scratch = [
        pltpu.VMEM((GRID, GRID), F32),
        pltpu.VMEM((GRID, GRID), BF16),
        pltpu.VMEM((GRID, GRID), BF16),
        line_scratch,
    ]
    lifted = call(lift_kernel, (plane, z_near, y_near, scalars), (), shape(512, 128), plane_scratch)
    lifted = exchange(lifted, everywhere)
    margin, *local = call(
        local_kernel,
        (plane,),
        (lift_scale, lift_shift, local_bias, local_weight),
        [shape(2 * COLS, GRID)] + fields,
        [pltpu.VMEM((GRID, GRID), F32)],
        flops=1 << 27,
    )
    pair = pltpu.VMEM((2, 64, 128), F32)
    mixed, spectra = call(
        mix_kernel, (lifted, spectral_weight, x_table), (), [shape(512, 128), shape(2, 64, 128)], [pair, pair]
    )
    mixed = exchange(mixed, everywhere)
    message, *preact = call(
        inverse_kernel,
        (mixed, margin, z_inverse, y_table, scalars, *local),
        (),
        [shape(COLS, 40, 128)] + fields,
        [
            pltpu.VMEM((128, 512), F32),
            line_scratch,
            pltpu.VMEM((GRID, GRID), F32),
            pltpu.VMEM((GRID, GRID), F32),
            pltpu.VMEM((GRID + 8, GRID), F32),
        ],
    )
    message = exchange(message, COL)
    wide, first, second = call(
        edge_kernel, (message, field, ring), (), [shape(PLANES, 24, GRID), shape(80, 128), shape(80, 128)], []
    )
    odd_pairs = [(r, r + 1 if r % 2 else r - 1) for r in range(1, ROWS - 1)]
    even_pairs = [(r, r - 1 if r % 2 else r + 1) for r in range(ROWS)]
    first = lax.ppermute(first, ROW, odd_pairs)
    second = lax.ppermute(second, ROW, even_pairs)
    rest = call(
        inner_kernel,
        (wide, field, ring),
        (),
        shape(PLANES, 24, GRID),
        [],
        flops=1 << 22,
    )
    aliases = {1 + o: o for o in range(HALF)}
    slope = call(slope_kernel, (scalars, *preact), (), fields, [], flops=1 << 25, aliases=aliases)
    first, second, slope = lax.optimization_barrier((first, second, slope))
    rest, adjoint = call(
        stencil_kernel,
        (rest, wide, first, second, ring),
        (),
        [shape(PLANES, COLS, GRID), shape(2 * PLANES, COLS, GRID)],
        [],
    )
    adjoint = exchange(adjoint, COL).reshape(GRID, GRID)
    grads, residual = call(
        grad_kernel,
        (adjoint, rest, z_forward, y_table, *slope),
        (),
        [shape(512, 128), shape(PLANES, COLS, GRID)],
        plane_scratch + [pltpu.SemaphoreType.DMA],
        far_out=(1,),
    )
    grads = exchange(grads, everywhere)
    spectral_grad = call(
        outer_kernel,
        (grads, spectra, x_table, doubling),
        (),
        jax.ShapeDtypeStruct(spectral_weight.shape, BF16),
        [pair, pair, pltpu.VMEM(spectral_weight.shape, BF16), pltpu.SemaphoreType.DMA((8,))],
        far_out=(0,),
    )
    return residual[None], spectral_grad


def solution(mesh):
    fine = Mesh(mesh.devices.reshape(8, 4, 2, 4, 2), ROW + COL)
    in_specs = (P(None, ROW, COL, None), P(), P(), P(ROW, COL, None, None, None), P(), P(), P())
    out_specs = (P(None, ROW, COL, None), P(ROW, COL, None, None, None))
    return jax.shard_map(shards, mesh=fine, in_specs=in_specs, out_specs=out_specs, check_vma=False)
```

```python
import math

import jax
import jax.numpy as jnp
import numpy as np
from jax import lax
from jax.experimental import pallas as pl
from jax.experimental.pallas import tpu as pltpu
from jax.sharding import Mesh
from jax.sharding import PartitionSpec as P

MODES = 64
GRID = 256
WIDTH = 16
HALF = 8
ROWS = 32
PLANES = 8
COLS = 16
ROW = ("y", "zh")
COL = ("zl", "x", "core")
F32 = jnp.float32
BF16 = jnp.bfloat16
VMEM_LIMIT = 40 * 1024 * 1024


def halves(table):
    high = table.astype(jnp.bfloat16)
    low = (table - high.astype(np.float64)).astype(jnp.bfloat16)
    return high, low


def wave(frequencies, points):
    phase = (np.outer(frequencies, points) % GRID) * (2.0 * math.pi / GRID)
    return np.cos(phase) / 16.0, np.sin(phase) / 16.0


def tables():
    points = np.arange(GRID)
    cos_z, sin_z = wave(np.arange(MODES), points)
    z_forward = np.concatenate(halves(np.concatenate([cos_z, -sin_z], axis=0)), axis=0)
    weight = np.where(np.arange(MODES) == 0, 1.0, 2.0)[:, None]
    high, low = halves(np.concatenate([cos_z * weight, -sin_z * weight], axis=0).T)
    z_inverse = np.block([[high, high], [low, np.zeros_like(low)]])
    ky = np.array([2 * r + a - MODES // 2 for a in range(2) for r in range(ROWS)])
    cos_y, sin_y = wave(ky, points)
    y_table = np.concatenate(
        [np.concatenate([cos_y, sin_y], axis=1), np.concatenate([-sin_y, cos_y], axis=1)], axis=0
    )
    y_table = np.concatenate(halves(y_table), axis=0)
    places = np.array([8 * r + q for q in range(PLANES) for r in range(ROWS)])
    cos_x, sin_x = wave(np.arange(MODES) - MODES // 2, places)
    x_table = np.concatenate(halves(np.concatenate([cos_x.T, -sin_x.T], axis=1)), axis=1)
    return z_forward, z_inverse, y_table, x_table


def split(value):
    high = value.astype(BF16)
    return high, (value - high.astype(F32)).astype(BF16)


def dot(left, right, dims):
    return lax.dot_general(left, right, (dims, ((), ())), preferred_element_type=F32)


NN = ((1,), (0,))
NT = ((1,), (1,))


ROOT = math.sqrt(2.0 / math.pi)
CUBE = 0.044715


def gelu_double(value, square):
    return 1.0 + jnp.tanh(value * (ROOT + (ROOT * CUBE) * square))


def gelu_slope(value):
    square = value * value
    double = gelu_double(value, square)
    slope = (0.5 * ROOT) + (1.5 * ROOT * CUBE) * square
    return double * (0.5 + (value * slope) * (2.0 - double))


def bent_half(half):
    return half * jnp.tanh(half * (2.0 * ROOT + (8.0 * ROOT * CUBE) * (half * half)))


def lift(field, half_scale, half_shift):
    scaled = half_scale * field
    return (scaled + scaled) + (bent_half(half_shift + scaled) - bent_half(half_shift - scaled))


def lane_index(shape):
    return lax.broadcasted_iota(jnp.int32, shape, len(shape) - 1)


def swapped(value):
    return pltpu.roll(value, MODES, 1)


def beside_z(value, lane):
    left = jnp.where(lane == 0, 0.0, pltpu.roll(value, 1, 1))
    return left + jnp.where(lane == GRID - 1, 0.0, pltpu.roll(value, GRID - 1, 1))


def plane_forward(fill, z_table, y_table, stage_high, stage_low, lines, out):
    for channel in range(HALF):
        fill(channel, stage_high, stage_low)
        z = dot(z_table[...], stage_high[...], NN)
        z = z[:128] + z[128:] + dot(z_table[0:128, :], stage_low[...], NN)
        lines[:, channel, 0:GRID] = z[:MODES]
        lines[:, channel, GRID:] = z[MODES:]
    high, low = split(lines[...].reshape(MODES * HALF, 2 * GRID))
    spectrum = dot(y_table[...], high, NT)
    spectrum = spectrum[:128] + spectrum[128:] + dot(y_table[0:128, :], low, NT)
    lane = lane_index((ROWS, 128)) // 32
    for tile in range(4):
        parts = [spectrum[b * 32 : b * 32 + 32, tile * 128 : tile * 128 + 128] for b in range(4)]
        for e in range(4):
            total = None
            for b in range(4):
                turn = ((b - e) % 4) * 32
                moved = pltpu.roll(parts[b], turn, 1) if turn else parts[b]
                total = moved if total is None else jnp.where(lane == b, moved, total)
            column = 4 * tile + e
            out[column * 32 : column * 32 + 32, :] = total


def lift_kernel(plane, z_table, y_table, scalars, out, turned, high, low, lines):
    turned[...] = plane[...].T

    def fill(channel, stage_high, stage_low):
        gain, offset = scalars[channel : channel + 1, :], scalars[HALF + channel : HALF + channel + 1, :]
        for t in range(8):
            rows = slice(32 * t, 32 * t + 32)
            stage_high[rows, :], stage_low[rows, :] = split(lift(turned[rows, :], gain, offset))

    plane_forward(fill, z_table, y_table, high, low, lines, out)


def grad_kernel(adjoint, rest, z_table, y_table, *refs):
    slope = refs[:HALF]
    out, residual, turned, high, low, lines, sem = refs[HALF:]
    copy = pltpu.make_async_copy(rest, residual, sem)
    copy.start()
    turned[...] = adjoint[...].T

    def fill(channel, stage_high, stage_low):
        for t in range(8):
            rows = slice(32 * t, 32 * t + 32)
            stage_high[rows, :], stage_low[rows, :] = split(turned[rows, :] * slope[channel][rows, :])

    plane_forward(fill, z_table, y_table, high, low, lines, out)
    copy.wait()


def first_kernel(
    far_field,
    far_z,
    far_y,
    far_scale,
    far_shift,
    far_readout,
    far_bias,
    far_weight,
    spread,
    z_table,
    y_table,
    scalars,
    factors,
    ring,
    doubling,
    scale,
    shift,
    readout,
    bias,
    weight,
    sems,
):
    core, row_place, col_place = lax.axis_index("core"), lax.axis_index(ROW), lax.axis_index(COL)
    pairs = [(far_scale, scale), (far_shift, shift), (far_readout, readout), (far_bias, bias), (far_weight, weight)]
    pairs += [(far_z, z_table), (far_y, y_table)]
    pairs += [(far_field, spread.at[:, k]) for k in range(2)]
    copies = [pltpu.make_async_copy(source, target, sems.at[n]) for n, (source, target) in enumerate(pairs)]
    for copy in copies:
        copy.start()
    row = lax.broadcasted_iota(jnp.int32, (24, GRID), 0)
    first_row = jnp.where(col_place == 0, 4, 3)
    last_row = jnp.where(col_place == COLS - 1, 19, 20)
    ring[0:24, :] = jnp.where(jnp.logical_and(row >= first_row, row <= last_row), 1.0, 0.0).astype(F32)
    row = lax.broadcasted_iota(jnp.int32, (8, GRID), 0)
    before, after = jnp.where(row_place > 0, 1.0, 0.0), jnp.where(row_place < ROWS - 1, 1.0, 0.0)
    odd = jnp.where(row_place % 2 == 1, 1.0, 0.0)
    ring[24:32, :] = jnp.where(row == 0, before, jnp.where(row == 1, after, odd)).astype(F32)
    row = lax.broadcasted_iota(jnp.int32, (64, 128), 0)
    zero_mode = jnp.logical_and((row // HALF) % 4 == 0, col_place == 0)
    doubling[...] = jnp.where(zero_mode, 1.0, 2.0).astype(F32)
    for copy in copies[:5]:
        copy.wait()
    first = core * HALF
    for n in range(HALF):
        for m, value in enumerate((0.5 * scale[first + n], 0.5 * shift[first + n], readout[first + n])):
            scalars[HALF * m + n : HALF * m + n + 1, :] = jnp.full((1, GRID), value, F32)
    for i in range(WIDTH):
        factors[i : i + 1, :] = jnp.full((1, 128), 0.5 * scale[i], F32)
        factors[WIDTH + i : WIDTH + i + 1, :] = jnp.full((1, 128), 0.5 * shift[i], F32)
        for o in range(HALF):
            row = 40 + HALF * i + o
            factors[row : row + 1, :] = jnp.full((1, 128), weight[i, first + o], F32)
    for o in range(HALF):
        factors[32 + o : 33 + o, :] = jnp.full((1, 128), bias[first + o], F32)
    for copy in copies[5:]:
        copy.wait()


def local_kernel(plane, factors, margin, *refs):
    out, turned = refs[:HALF], refs[HALF]
    keep = jnp.where(lax.axis_index("core") == 0, 1.0, 0.0).astype(F32)
    turned[...] = plane[...].T
    margin[...] = jnp.zeros(margin.shape, F32)
    for c in range(1, COLS):
        margin[c : c + 1, :] = plane[16 * c - 1 : 16 * c, :] * keep
        margin[COLS + c - 1 : COLS + c, :] = plane[16 * c : 16 * c + 1, :] * keep

    def step(t, carry):
        rows = pl.ds(pl.multiple_of(t * 64, 64), 64)
        for lanes in (slice(0, 128), slice(128, 256)):
            field = turned[rows, lanes]
            sums = [jnp.broadcast_to(factors[32 + o : 33 + o, :], (64, 128)) for o in range(HALF)]
            for i in range(WIDTH):
                lifted = lift(field, factors[i : i + 1, :], factors[WIDTH + i : WIDTH + i + 1, :])
                for o in range(HALF):
                    row = 40 + HALF * i + o
                    sums[o] = sums[o] + factors[row : row + 1, :] * lifted
            for o in range(HALF):
                out[o][rows, lanes] = sums[o]
        return carry

    lax.fori_loop(0, GRID // 64, step, 0)


def inverse_kernel(received, margin, z_table, y_table, scalars, *refs):
    local, out, preact = refs[:HALF], refs[HALF], refs[HALF + 1 : 2 * HALF + 1]
    grid, lines, spectral, total, padded = refs[2 * HALF + 1 :]
    lane = lane_index((ROWS, 128)) // 32
    for tile in range(4):
        parts = [received[(4 * tile + e) * 32 : (4 * tile + e) * 32 + 32, :] for e in range(4)]
        for b in range(4):
            whole = None
            for e in range(4):
                turn = ((e - b) % 4) * 32
                moved = pltpu.roll(parts[e], turn, 1) if turn else parts[e]
                whole = moved if whole is None else jnp.where(lane == e, moved, whole)
            grid[b * 32 : b * 32 + 32, tile * 128 : tile * 128 + 128] = whole
    high, low = split(grid[...].T)
    modes = dot(jnp.concatenate([high, high], axis=1), y_table[...], NN) + dot(low, y_table[0:128, :], NN)
    lines[...] = modes.reshape(MODES, HALF, 2 * GRID)
    for o in range(HALF):
        modes = jnp.concatenate([lines[:, o, 0:GRID], lines[:, o, GRID:]], axis=0)
        product = dot(z_table[...], jnp.concatenate(split(modes), axis=0), NN)
        spectral[...] = product[:GRID] + product[GRID:]
        read = 0.5 * scalars[2 * HALF + o : 2 * HALF + o + 1, :]
        for t in range(8):
            rows = slice(32 * t, 32 * t + 32)
            value = spectral[rows, :] + local[o][rows, :]
            preact[o][rows, :] = value
            term = (read * value) * gelu_double(value, value * value)
            if o == 0:
                total[rows, :] = term
            else:
                total[rows, :] += term
    padded[0:8, :] = jnp.zeros((8, GRID), F32)
    padded[256:264, :] = jnp.zeros((8, GRID), F32)
    value = total[...].T
    padded[4:260, :] = value
    beside = pltpu.roll(value, 1, 0) + pltpu.roll(value, GRID - 1, 0) + beside_z(value, lane_index((GRID, GRID)))
    spectral[...] = 6.0 * value - beside
    blank = jnp.zeros((1, GRID), F32)
    for c in range(COLS):
        before, after = blank, blank
        if c > 0:
            before = spectral[16 * c - 1 : 16 * c, :] - margin[c : c + 1, :]
        if c < COLS - 1:
            after = spectral[16 * c + 16 : 16 * c + 17, :] - margin[COLS + c : COLS + c + 1, :]
        for h in range(2):
            lanes = slice(128 * h, 128 * h + 128)
            out[c, 20 * h : 20 * h + 1, :] = before[:, lanes]
            out[c, 20 * h + 1 : 20 * h + 19, :] = padded[16 * c + 3 : 16 * c + 21, lanes]
            out[c, 20 * h + 19 : 20 * h + 20, :] = after[:, lanes]


def slope_kernel(scalars, *refs):
    preact, out = refs[:HALF], refs[HALF:]
    for o in range(HALF):
        read = scalars[2 * HALF + o : 2 * HALF + o + 1, :]
        for t in range(8):
            rows = slice(32 * t, 32 * t + 32)
            out[o][rows, :] = read * gelu_slope(preact[o][rows, :])


def gather_spectra(received, x_table, sign):
    lines = []
    for k in range(2):
        parts = [received[(2 * q + k) * 32 : (2 * q + k) * 32 + 32, :] for q in range(PLANES)]
        lines.append(jnp.concatenate(parts, axis=0).T)
    product = dot(jnp.concatenate(split(jnp.concatenate(lines, axis=0)), axis=0), x_table[...], NN)
    product = product[:, :128] + product[:, 128:]
    product = product[:256] + product[256:]
    first = [product[128 * k : 128 * k + 64] for k in range(2)]
    second = [product[128 * k + 64 : 128 * k + 128] for k in range(2)]
    return [first[k] + sign * swapped(second[k]) for k in range(2)]


def mix_kernel(received, weight, x_table, out, spectra_out, real, imag):
    low = lane_index((64, 128)) < MODES
    sign = jnp.where(low, -1.0, 1.0).astype(F32)
    for k, spectra in enumerate(gather_spectra(received, x_table, sign)):
        spectra_out[k] = spectra
        other = swapped(spectra)
        real[k] = jnp.where(low, spectra, other)
        imag[k] = jnp.where(low, other, spectra)
    parts = [[], []]
    for group in range(8):
        a, j = group // 4, group % 4
        first = jnp.zeros((WIDTH, 128), F32)
        second = jnp.zeros((WIDTH, 128), F32)
        for i in range(WIDTH):
            k, row = i // HALF, group * HALF + i % HALF
            tile = weight[a, j, i].astype(F32)
            first = first + tile * real[k, row : row + 1, :]
            second = second + tile * imag[k, row : row + 1, :]
        mixed = first + sign[:WIDTH] * swapped(second)
        parts[0].append(mixed[:HALF])
        parts[1].append(mixed[HALF:])
    both = []
    for k in range(2):
        mixed = jnp.concatenate(parts[k], axis=0)
        both += [mixed, -sign * swapped(mixed)]
    high, low = split(jnp.concatenate(both, axis=0))
    result = dot(x_table[...], jnp.concatenate([high, high], axis=1), NT) + dot(x_table[:, 0:128], low, NT)
    for q in range(PLANES):
        for k in range(2):
            place = (2 * q + k) * 32
            out[place : place + 32, :] = result[q * 32 : q * 32 + 32, k * 128 : k * 128 + 128]


def outer_kernel(received, spectra_in, x_table, doubling, out, real, imag, stage, sems):
    low = lane_index((64, 128)) < MODES
    sign = jnp.where(low, -1.0, 1.0).astype(F32)
    grads = [doubling[...] * g for g in gather_spectra(received, x_table, sign)]
    turned = [-sign * swapped(g) for g in grads]
    for k in range(2):
        spectra = spectra_in[k]
        other = swapped(spectra)
        real[k] = jnp.where(low, spectra, other)
        imag[k] = jnp.where(low, other, spectra)
    copies = []
    for group in range(8):
        a, j = group // 4, group % 4
        rows = slice(group * HALF, group * HALF + HALF)
        straight = jnp.concatenate([grads[0][rows], grads[1][rows]], axis=0)
        crossed = jnp.concatenate([turned[0][rows], turned[1][rows]], axis=0)
        for i in range(WIDTH):
            k, line = i // HALF, group * HALF + i % HALF
            value = straight * real[k, line : line + 1, :] + crossed * imag[k, line : line + 1, :]
            stage[a, j, i] = value.astype(BF16)
        copies.append(pltpu.make_async_copy(stage.at[a, j], out.at[a, j], sems.at[group]))
        copies[-1].start()
    for copy in copies:
        copy.wait()


def beside_y(value):
    return pltpu.roll(value, 1, 0) + pltpu.roll(value, 23, 0)


def edge_kernel(received, field, ring, wide, first, second):
    lane = lane_index((24, GRID))
    for q in range(PLANES):
        wide[q] = jnp.zeros((24, GRID), F32)
        for h in range(2):
            lanes = slice(128 * h, 128 * h + 128)
            both = received[2 * q, 20 * h : 20 * h + 20, :] + received[2 * q + 1, 20 * h : 20 * h + 20, :]
            wide[q, 3:21, lanes] = both[1:19]
            wide[q, 1:2, lanes] = both[0:1]
            wide[q, 22:23, lanes] = both[19:20]
    sent = []
    for edge, inner in ((0, 1), (PLANES - 1, PLANES - 2)):
        value = wide[edge]
        rest = 6.0 * value - (wide[inner] + beside_y(value) + beside_z(value, lane))
        rest = rest[4:20] - field[edge]
        sent.append(jnp.concatenate([value[:, :128], value[:, 128:], rest[:, :128], rest[:, 128:]], axis=0))
    odd = jnp.broadcast_to(ring[26:27, 0:128], (80, 128)) > 0.5
    first[...] = jnp.where(odd, sent[1], sent[0])
    second[...] = jnp.where(odd, sent[0], sent[1])


def inner_kernel(wide, field, ring, rest):
    lane = lane_index((24, GRID))
    for q in range(PLANES):
        centre = wide[q]
        across = jnp.zeros((24, GRID), F32)
        if q > 0:
            across = across + wide[q - 1]
        if q < PLANES - 1:
            across = across + wide[q + 1]
        value = 6.0 * centre - (beside_y(centre) + beside_z(centre, lane) + across)
        rest[q] = value
        rest[q, 4:20, :] = value[4:20] - field[q]
        rest[q, 3:4, :] = ring[3:4, :] * (wide[q, 1:2, :] - across[3:4])
        rest[q, 20:21, :] = ring[20:21, :] * (wide[q, 22:23, :] - across[20:21])


def stencil_kernel(rest, wide, first, second, ring, residual, adjoint):
    lane = lane_index((24, GRID))
    inside = ring[0:24, :]
    values = [rest[q] for q in range(PLANES)]
    odd = jnp.broadcast_to(ring[26:27, 0:128], (80, 128)) > 0.5
    before, after = jnp.where(odd, second[...], first[...]), jnp.where(odd, first[...], second[...])
    outer = []
    for n, ref, edge in ((0, before, 0), (1, after, PLANES - 1)):
        beyond = jnp.concatenate([ref[0:24], ref[24:48]], axis=1)
        values[edge] = values[edge] - inside * beyond
        part = jnp.concatenate([ref[48:64], ref[64:80]], axis=1) - wide[edge, 4:20, :]
        outer.append(ring[24 + n : 25 + n, :] * part)
    for q in range(PLANES):
        low = outer[0] if q == 0 else values[q - 1][4:20]
        high = outer[1] if q == PLANES - 1 else values[q + 1][4:20]
        residual[q] = values[q][4:20]
        near = (beside_y(values[q]) + beside_z(values[q], lane))[4:20]
        value = 6.0 * values[q][4:20] - (low + high + near)
        adjoint[2 * q] = value
        adjoint[2 * q + 1] = value


def call(kernel, operands, scalars, outputs, scratch, flops=0, far=0, far_out=(), aliases=None):
    many = isinstance(outputs, list)
    vmem = pl.BlockSpec(memory_space=pltpu.VMEM)
    smem = pl.BlockSpec(memory_space=pltpu.SMEM)
    hbm = pl.BlockSpec(memory_space=pltpu.HBM)
    out_specs = [hbm if n in far_out else vmem for n in range(len(outputs) if many else 1)]
    operands = list(operands)
    for n in range(len(operands) - far, len(operands)):
        operands[n] = pltpu.with_memory_space_constraint(operands[n], pltpu.HBM)
    cost = pl.CostEstimate(flops=flops, bytes_accessed=4 << 20, transcendentals=flops // 16)
    return pl.pallas_call(
        kernel,
        in_specs=[smem] * len(scalars) + [vmem] * (len(operands) - far) + [hbm] * far,
        out_specs=out_specs if many else out_specs[0],
        out_shape=outputs,
        scratch_shapes=scratch,
        input_output_aliases=aliases or {},
        compiler_params=pltpu.CompilerParams(vmem_limit_bytes=VMEM_LIMIT),
        cost_estimate=cost if flops else None,
    )(*scalars, *operands)


def exchange(value, axes):
    return lax.all_to_all(value, axes, split_axis=0, concat_axis=0, tiled=True)


def shape(*sizes):
    return jax.ShapeDtypeStruct(sizes, F32)


def shards(right_side, lift_scale, lift_shift, spectral_weight, local_weight, local_bias, readout):
    z_forward, z_inverse, y_table, x_table = tables()
    everywhere = COL + ROW
    field = right_side[0]
    fields = [shape(GRID, GRID)] * HALF

    row_of = pltpu.SMEM((WIDTH,), F32)
    spread, z_near, y_near, scalars, factors, ring, doubling = call(
        first_kernel,
        (field, z_forward, y_table, lift_scale, lift_shift, readout, local_bias, local_weight),
        (),
        [
            shape(PLANES, 2, COLS, GRID),
            jax.ShapeDtypeStruct(z_forward.shape, BF16),
            jax.ShapeDtypeStruct(y_table.shape, BF16),
            shape(24, GRID),
            shape(168, 128),
            shape(32, GRID),
            shape(64, 128),
        ],
        [row_of] * 4 + [pltpu.SMEM((WIDTH, WIDTH), F32), pltpu.SemaphoreType.DMA((9,))],
        far=8,
    )
    plane = exchange(spread.reshape(COLS, COLS, GRID), COL).reshape(GRID, GRID)
    line_scratch = pltpu.VMEM((MODES, HALF, 2 * GRID), F32)
    plane_scratch = [
        pltpu.VMEM((GRID, GRID), F32),
        pltpu.VMEM((GRID, GRID), BF16),
        pltpu.VMEM((GRID, GRID), BF16),
        line_scratch,
    ]
    lifted = call(lift_kernel, (plane, z_near, y_near, scalars), (), shape(512, 128), plane_scratch)
    lifted = exchange(lifted, everywhere)
    margin, *local = call(
        local_kernel,
        (plane, factors),
        (),
        [shape(2 * COLS, GRID)] + fields,
        [pltpu.VMEM((GRID, GRID), F32)],
        flops=1 << 27,
    )
    pair = pltpu.VMEM((2, 64, 128), F32)
    mixed, spectra = call(
        mix_kernel, (lifted, spectral_weight, x_table), (), [shape(512, 128), shape(2, 64, 128)], [pair, pair]
    )
    mixed = exchange(mixed, everywhere)
    message, *preact = call(
        inverse_kernel,
        (mixed, margin, z_inverse, y_table, scalars, *local),
        (),
        [shape(COLS, 40, 128)] + fields,
        [
            pltpu.VMEM((128, 512), F32),
            line_scratch,
            pltpu.VMEM((GRID, GRID), F32),
            pltpu.VMEM((GRID, GRID), F32),
            pltpu.VMEM((GRID + 8, GRID), F32),
        ],
    )
    message = exchange(message, COL)
    wide, first, second = call(
        edge_kernel, (message, field, ring), (), [shape(PLANES, 24, GRID), shape(80, 128), shape(80, 128)], []
    )
    odd_pairs = [(r, r + 1 if r % 2 else r - 1) for r in range(1, ROWS - 1)]
    even_pairs = [(r, r - 1 if r % 2 else r + 1) for r in range(ROWS)]
    first = lax.ppermute(first, ROW, odd_pairs)
    second = lax.ppermute(second, ROW, even_pairs)
    rest = call(
        inner_kernel,
        (wide, field, ring),
        (),
        shape(PLANES, 24, GRID),
        [],
        flops=1 << 22,
    )
    aliases = {1 + o: o for o in range(HALF)}
    slope = call(slope_kernel, (scalars, *preact), (), fields, [], flops=1 << 25, aliases=aliases)
    first, second, slope = lax.optimization_barrier((first, second, slope))
    rest, adjoint = call(
        stencil_kernel,
        (rest, wide, first, second, ring),
        (),
        [shape(PLANES, COLS, GRID), shape(2 * PLANES, COLS, GRID)],
        [],
    )
    adjoint = exchange(adjoint, COL).reshape(GRID, GRID)
    grads, residual = call(
        grad_kernel,
        (adjoint, rest, z_forward, y_table, *slope),
        (),
        [shape(512, 128), shape(PLANES, COLS, GRID)],
        plane_scratch + [pltpu.SemaphoreType.DMA],
        far_out=(1,),
    )
    grads = exchange(grads, everywhere)
    spectral_grad = call(
        outer_kernel,
        (grads, spectra, x_table, doubling),
        (),
        jax.ShapeDtypeStruct(spectral_weight.shape, BF16),
        [pair, pair, pltpu.VMEM(spectral_weight.shape, BF16), pltpu.SemaphoreType.DMA((8,))],
        far_out=(0,),
    )
    return residual[None], spectral_grad


def solution(mesh):
    fine = Mesh(mesh.devices.reshape(8, 4, 2, 4, 2), ROW + COL)
    in_specs = (P(None, ROW, COL, None), P(), P(), P(ROW, COL, None, None, None), P(), P(), P())
    out_specs = (P(None, ROW, COL, None), P(ROW, COL, None, None, None))
    return jax.shard_map(shards, mesh=fine, in_specs=in_specs, out_specs=out_specs, check_vma=False)
```

```python
import math

import jax
import jax.numpy as jnp
import numpy as np
from jax import lax
from jax.experimental import pallas as pl
from jax.experimental.pallas import tpu as pltpu
from jax.sharding import Mesh
from jax.sharding import PartitionSpec as P

MODES = 64
GRID = 256
WIDTH = 16
HALF = 8
ROWS = 32
PLANES = 8
COLS = 16
ROW = ("y", "zh")
COL = ("zl", "x", "core")
F32 = jnp.float32
BF16 = jnp.bfloat16
VMEM_LIMIT = 40 * 1024 * 1024


def halves(table):
    high = table.astype(jnp.bfloat16)
    low = (table - high.astype(np.float64)).astype(jnp.bfloat16)
    return high, low


def wave(frequencies, points):
    phase = (np.outer(frequencies, points) % GRID) * (2.0 * math.pi / GRID)
    return np.cos(phase) / 16.0, np.sin(phase) / 16.0


def tables():
    points = np.arange(GRID)
    cos_z, sin_z = wave(np.arange(MODES), points)
    z_forward = np.concatenate(halves(np.concatenate([cos_z, -sin_z], axis=0)), axis=0)
    weight = np.where(np.arange(MODES) == 0, 1.0, 2.0)[:, None]
    high, low = halves(np.concatenate([cos_z * weight, -sin_z * weight], axis=0).T)
    z_inverse = np.block([[high, high], [low, np.zeros_like(low)]])
    ky = np.array([2 * r + a - MODES // 2 for a in range(2) for r in range(ROWS)])
    cos_y, sin_y = wave(ky, points)
    y_table = np.concatenate(
        [np.concatenate([cos_y, sin_y], axis=1), np.concatenate([-sin_y, cos_y], axis=1)], axis=0
    )
    y_table = np.concatenate(halves(y_table), axis=0)
    places = np.array([8 * r + q for q in range(PLANES) for r in range(ROWS)])
    cos_x, sin_x = wave(np.arange(MODES) - MODES // 2, places)
    x_table = np.concatenate(halves(np.concatenate([cos_x.T, -sin_x.T], axis=1)), axis=1)
    return z_forward, z_inverse, y_table, x_table


def split(value):
    high = value.astype(BF16)
    return high, (value - high.astype(F32)).astype(BF16)


def dot(left, right, dims):
    return lax.dot_general(left, right, (dims, ((), ())), preferred_element_type=F32)


NN = ((1,), (0,))
NT = ((1,), (1,))


ROOT = math.sqrt(2.0 / math.pi)
CUBE = 0.044715


def gelu_double(value, square):
    return 1.0 + jnp.tanh(value * (ROOT + (ROOT * CUBE) * square))


def gelu_slope(value):
    square = value * value
    double = gelu_double(value, square)
    slope = (0.5 * ROOT) + (1.5 * ROOT * CUBE) * square
    return double * (0.5 + (value * slope) * (2.0 - double))


def bent_half(half):
    return half * jnp.tanh(half * (2.0 * ROOT + (8.0 * ROOT * CUBE) * (half * half)))


def lift(field, half_scale, half_shift):
    scaled = half_scale * field
    return (scaled + scaled) + (bent_half(half_shift + scaled) - bent_half(half_shift - scaled))


def lane_index(shape):
    return lax.broadcasted_iota(jnp.int32, shape, len(shape) - 1)


def swapped(value):
    return pltpu.roll(value, MODES, 1)


def beside_z(value, lane):
    left = jnp.where(lane == 0, 0.0, pltpu.roll(value, 1, 1))
    return left + jnp.where(lane == GRID - 1, 0.0, pltpu.roll(value, GRID - 1, 1))


def plane_forward(fill, z_table, y_table, stage_high, stage_low, lines, out):
    for channel in range(HALF):
        fill(channel, stage_high, stage_low)
        z = dot(z_table[...], stage_high[...], NN)
        z = z[:128] + z[128:] + dot(z_table[0:128, :], stage_low[...], NN)
        lines[:, channel, 0:GRID] = z[:MODES]
        lines[:, channel, GRID:] = z[MODES:]
    high, low = split(lines[...].reshape(MODES * HALF, 2 * GRID))
    spectrum = dot(y_table[...], high, NT)
    spectrum = spectrum[:128] + spectrum[128:] + dot(y_table[0:128, :], low, NT)
    lane = lane_index((ROWS, 128)) // 32
    for tile in range(4):
        parts = [spectrum[b * 32 : b * 32 + 32, tile * 128 : tile * 128 + 128] for b in range(4)]
        for e in range(4):
            total = None
            for b in range(4):
                turn = ((b - e) % 4) * 32
                moved = pltpu.roll(parts[b], turn, 1) if turn else parts[b]
                total = moved if total is None else jnp.where(lane == b, moved, total)
            column = 4 * tile + e
            out[column * 32 : column * 32 + 32, :] = total


def lift_kernel(plane, z_table, y_table, scalars, out, turned, high, low, lines):
    turned[...] = plane[...].T

    def fill(channel, stage_high, stage_low):
        gain, offset = scalars[channel : channel + 1, :], scalars[HALF + channel : HALF + channel + 1, :]
        for t in range(8):
            rows = slice(32 * t, 32 * t + 32)
            stage_high[rows, :], stage_low[rows, :] = split(lift(turned[rows, :], gain, offset))

    plane_forward(fill, z_table, y_table, high, low, lines, out)


def grad_kernel(adjoint, rest, z_table, y_table, *refs):
    slope = refs[:HALF]
    out, residual, turned, high, low, lines, sem = refs[HALF:]
    copy = pltpu.make_async_copy(rest, residual, sem)
    copy.start()
    turned[...] = adjoint[...].T

    def fill(channel, stage_high, stage_low):
        for t in range(8):
            rows = slice(32 * t, 32 * t + 32)
            stage_high[rows, :], stage_low[rows, :] = split(turned[rows, :] * slope[channel][rows, :])

    plane_forward(fill, z_table, y_table, high, low, lines, out)
    copy.wait()


def first_kernel(
    far_field,
    far_z,
    far_y,
    far_scale,
    far_shift,
    far_readout,
    far_bias,
    far_weight,
    spread,
    z_table,
    y_table,
    scalars,
    factors,
    ring,
    doubling,
    scale,
    shift,
    readout,
    bias,
    weight,
    sems,
):
    core, row_place, col_place = lax.axis_index("core"), lax.axis_index(ROW), lax.axis_index(COL)
    pairs = [(far_scale, scale), (far_shift, shift), (far_readout, readout), (far_bias, bias), (far_weight, weight)]
    pairs += [(far_z, z_table), (far_y, y_table)]
    pairs += [(far_field, spread.at[:, k]) for k in range(2)]
    copies = [pltpu.make_async_copy(source, target, sems.at[n]) for n, (source, target) in enumerate(pairs)]
    for copy in copies:
        copy.start()
    row = lax.broadcasted_iota(jnp.int32, (24, GRID), 0)
    first_row = jnp.where(col_place == 0, 4, 3)
    last_row = jnp.where(col_place == COLS - 1, 19, 20)
    ring[0:24, :] = jnp.where(jnp.logical_and(row >= first_row, row <= last_row), 1.0, 0.0).astype(F32)
    row = lax.broadcasted_iota(jnp.int32, (8, GRID), 0)
    before, after = jnp.where(row_place > 0, 1.0, 0.0), jnp.where(row_place < ROWS - 1, 1.0, 0.0)
    odd = jnp.where(row_place % 2 == 1, 1.0, 0.0)
    ring[24:32, :] = jnp.where(row == 0, before, jnp.where(row == 1, after, odd)).astype(F32)
    row = lax.broadcasted_iota(jnp.int32, (64, 128), 0)
    zero_mode = jnp.logical_and((row // HALF) % 4 == 0, col_place == 0)
    doubling[...] = jnp.where(zero_mode, 1.0, 2.0).astype(F32)
    for copy in copies[:5]:
        copy.wait()
    first = core * HALF
    for n in range(HALF):
        for m, value in enumerate((0.5 * scale[first + n], 0.5 * shift[first + n], readout[first + n])):
            scalars[HALF * m + n : HALF * m + n + 1, :] = jnp.full((1, GRID), value, F32)
    for i in range(WIDTH):
        factors[i : i + 1, :] = jnp.full((1, 128), 0.5 * scale[i], F32)
        factors[WIDTH + i : WIDTH + i + 1, :] = jnp.full((1, 128), 0.5 * shift[i], F32)
        for o in range(HALF):
            row = 40 + HALF * i + o
            factors[row : row + 1, :] = jnp.full((1, 128), weight[i, first + o], F32)
    for o in range(HALF):
        factors[32 + o : 33 + o, :] = jnp.full((1, 128), bias[first + o], F32)
    for copy in copies[5:]:
        copy.wait()


def local_kernel(plane, factors, margin, *refs):
    out, turned = refs[:HALF], refs[HALF]
    keep = jnp.where(lax.axis_index("core") == 0, 1.0, 0.0).astype(F32)
    turned[...] = plane[...].T
    margin[...] = jnp.zeros(margin.shape, F32)
    for c in range(1, COLS):
        margin[c : c + 1, :] = plane[16 * c - 1 : 16 * c, :] * keep
        margin[COLS + c - 1 : COLS + c, :] = plane[16 * c : 16 * c + 1, :] * keep

    def step(t, carry):
        rows = pl.ds(pl.multiple_of(t * 64, 64), 64)
        for lanes in (slice(0, 128), slice(128, 256)):
            field = turned[rows, lanes]
            sums = [jnp.broadcast_to(factors[32 + o : 33 + o, :], (64, 128)) for o in range(HALF)]
            for i in range(WIDTH):
                lifted = lift(field, factors[i : i + 1, :], factors[WIDTH + i : WIDTH + i + 1, :])
                for o in range(HALF):
                    row = 40 + HALF * i + o
                    sums[o] = sums[o] + factors[row : row + 1, :] * lifted
            for o in range(HALF):
                out[o][rows, lanes] = sums[o]
        return carry

    lax.fori_loop(0, GRID // 64, step, 0)


def inverse_kernel(received, margin, z_table, y_table, scalars, *refs):
    local, out, preact = refs[:HALF], refs[HALF], refs[HALF + 1 : 2 * HALF + 1]
    grid, lines, spectral, total, padded = refs[2 * HALF + 1 :]
    lane = lane_index((ROWS, 128)) // 32
    for tile in range(4):
        parts = [received[(4 * tile + e) * 32 : (4 * tile + e) * 32 + 32, :] for e in range(4)]
        for b in range(4):
            whole = None
            for e in range(4):
                turn = ((e - b) % 4) * 32
                moved = pltpu.roll(parts[e], turn, 1) if turn else parts[e]
                whole = moved if whole is None else jnp.where(lane == e, moved, whole)
            grid[b * 32 : b * 32 + 32, tile * 128 : tile * 128 + 128] = whole
    high, low = split(grid[...].T)
    modes = dot(jnp.concatenate([high, high], axis=1), y_table[...], NN) + dot(low, y_table[0:128, :], NN)
    lines[...] = modes.reshape(MODES, HALF, 2 * GRID)
    for o in range(HALF):
        modes = jnp.concatenate([lines[:, o, 0:GRID], lines[:, o, GRID:]], axis=0)
        product = dot(z_table[...], jnp.concatenate(split(modes), axis=0), NN)
        spectral[...] = product[:GRID] + product[GRID:]
        read = 0.5 * scalars[2 * HALF + o : 2 * HALF + o + 1, :]
        for t in range(8):
            rows = slice(32 * t, 32 * t + 32)
            value = spectral[rows, :] + local[o][rows, :]
            preact[o][rows, :] = value
            term = (read * value) * gelu_double(value, value * value)
            if o == 0:
                total[rows, :] = term
            else:
                total[rows, :] += term
    padded[0:8, :] = jnp.zeros((8, GRID), F32)
    padded[256:264, :] = jnp.zeros((8, GRID), F32)
    value = total[...].T
    padded[4:260, :] = value
    blank = jnp.zeros((1, GRID), F32)
    lane = lane_index((8, GRID))
    tiles = [None]
    for m in range(1, COLS):
        tile = padded[16 * m : 16 * m + 8, :]
        beside = pltpu.roll(tile, 1, 0) + pltpu.roll(tile, 7, 0) + beside_z(tile, lane)
        tiles.append(6.0 * tile - beside)
    for c in range(COLS):
        before, after = blank, blank
        if c > 0:
            before = tiles[c][3:4] - margin[c : c + 1, :]
        if c < COLS - 1:
            after = tiles[c + 1][4:5] - margin[COLS + c : COLS + c + 1, :]
        for h in range(2):
            lanes = slice(128 * h, 128 * h + 128)
            out[c, 20 * h : 20 * h + 1, :] = before[:, lanes]
            out[c, 20 * h + 1 : 20 * h + 19, :] = padded[16 * c + 3 : 16 * c + 21, lanes]
            out[c, 20 * h + 19 : 20 * h + 20, :] = after[:, lanes]


def slope_kernel(scalars, *refs):
    preact, out = refs[:HALF], refs[HALF:]
    for o in range(HALF):
        read = scalars[2 * HALF + o : 2 * HALF + o + 1, :]
        for t in range(8):
            rows = slice(32 * t, 32 * t + 32)
            out[o][rows, :] = read * gelu_slope(preact[o][rows, :])


def gather_spectra(received, x_table, sign):
    lines = []
    for k in range(2):
        parts = [received[(2 * q + k) * 32 : (2 * q + k) * 32 + 32, :] for q in range(PLANES)]
        lines.append(jnp.concatenate(parts, axis=0).T)
    product = dot(jnp.concatenate(split(jnp.concatenate(lines, axis=0)), axis=0), x_table[...], NN)
    product = product[:, :128] + product[:, 128:]
    product = product[:256] + product[256:]
    first = [product[128 * k : 128 * k + 64] for k in range(2)]
    second = [product[128 * k + 64 : 128 * k + 128] for k in range(2)]
    return [first[k] + sign * swapped(second[k]) for k in range(2)]


def mix_kernel(received, weight, x_table, out, spectra_out, real, imag):
    low = lane_index((64, 128)) < MODES
    sign = jnp.where(low, -1.0, 1.0).astype(F32)
    for k, spectra in enumerate(gather_spectra(received, x_table, sign)):
        spectra_out[k] = spectra
        other = swapped(spectra)
        real[k] = jnp.where(low, spectra, other)
        imag[k] = jnp.where(low, other, spectra)
    parts = [[], []]
    for group in range(8):
        a, j = group // 4, group % 4
        first = jnp.zeros((WIDTH, 128), F32)
        second = jnp.zeros((WIDTH, 128), F32)
        for i in range(WIDTH):
            k, row = i // HALF, group * HALF + i % HALF
            tile = weight[a, j, i].astype(F32)
            first = first + tile * real[k, row : row + 1, :]
            second = second + tile * imag[k, row : row + 1, :]
        mixed = first + sign[:WIDTH] * swapped(second)
        parts[0].append(mixed[:HALF])
        parts[1].append(mixed[HALF:])
    both = []
    for k in range(2):
        mixed = jnp.concatenate(parts[k], axis=0)
        both += [mixed, -sign * swapped(mixed)]
    high, low = split(jnp.concatenate(both, axis=0))
    result = dot(x_table[...], jnp.concatenate([high, high], axis=1), NT) + dot(x_table[:, 0:128], low, NT)
    for q in range(PLANES):
        for k in range(2):
            place = (2 * q + k) * 32
            out[place : place + 32, :] = result[q * 32 : q * 32 + 32, k * 128 : k * 128 + 128]


def outer_kernel(received, spectra_in, x_table, doubling, out, real, imag, stage, sems):
    low = lane_index((64, 128)) < MODES
    sign = jnp.where(low, -1.0, 1.0).astype(F32)
    grads = [doubling[...] * g for g in gather_spectra(received, x_table, sign)]
    turned = [-sign * swapped(g) for g in grads]
    for k in range(2):
        spectra = spectra_in[k]
        other = swapped(spectra)
        real[k] = jnp.where(low, spectra, other)
        imag[k] = jnp.where(low, other, spectra)
    copies = []
    for group in range(8):
        a, j = group // 4, group % 4
        rows = slice(group * HALF, group * HALF + HALF)
        straight = jnp.concatenate([grads[0][rows], grads[1][rows]], axis=0)
        crossed = jnp.concatenate([turned[0][rows], turned[1][rows]], axis=0)
        for i in range(WIDTH):
            k, line = i // HALF, group * HALF + i % HALF
            value = straight * real[k, line : line + 1, :] + crossed * imag[k, line : line + 1, :]
            stage[a, j, i] = value.astype(BF16)
        copies.append(pltpu.make_async_copy(stage.at[a, j], out.at[a, j], sems.at[group]))
        copies[-1].start()
    for copy in copies:
        copy.wait()


def beside_y(value):
    return pltpu.roll(value, 1, 0) + pltpu.roll(value, 23, 0)


def edge_kernel(received, field, ring, wide, first, second):
    lane = lane_index((24, GRID))
    for q in range(PLANES):
        wide[q] = jnp.zeros((24, GRID), F32)
        for h in range(2):
            lanes = slice(128 * h, 128 * h + 128)
            both = received[2 * q, 20 * h : 20 * h + 20, :] + received[2 * q + 1, 20 * h : 20 * h + 20, :]
            wide[q, 3:21, lanes] = both[1:19]
            wide[q, 1:2, lanes] = both[0:1]
            wide[q, 22:23, lanes] = both[19:20]
    sent = []
    for edge, inner in ((0, 1), (PLANES - 1, PLANES - 2)):
        value = wide[edge]
        rest = 6.0 * value - (wide[inner] + beside_y(value) + beside_z(value, lane))
        rest = rest[4:20] - field[edge]
        sent.append(jnp.concatenate([value[:, :128], value[:, 128:], rest[:, :128], rest[:, 128:]], axis=0))
    odd = jnp.broadcast_to(ring[26:27, 0:128], (80, 128)) > 0.5
    first[...] = jnp.where(odd, sent[1], sent[0])
    second[...] = jnp.where(odd, sent[0], sent[1])


def inner_kernel(wide, field, ring, rest):
    lane = lane_index((24, GRID))
    for q in range(PLANES):
        centre = wide[q]
        across = jnp.zeros((24, GRID), F32)
        if q > 0:
            across = across + wide[q - 1]
        if q < PLANES - 1:
            across = across + wide[q + 1]
        value = 6.0 * centre - (beside_y(centre) + beside_z(centre, lane) + across)
        rest[q] = value
        rest[q, 4:20, :] = value[4:20] - field[q]
        rest[q, 3:4, :] = ring[3:4, :] * (wide[q, 1:2, :] - across[3:4])
        rest[q, 20:21, :] = ring[20:21, :] * (wide[q, 22:23, :] - across[20:21])


def stencil_kernel(rest, wide, first, second, ring, residual, adjoint):
    lane = lane_index((24, GRID))
    inside = ring[0:24, :]
    values = [rest[q] for q in range(PLANES)]
    odd = jnp.broadcast_to(ring[26:27, 0:128], (80, 128)) > 0.5
    before, after = jnp.where(odd, second[...], first[...]), jnp.where(odd, first[...], second[...])
    outer = []
    for n, ref, edge in ((0, before, 0), (1, after, PLANES - 1)):
        beyond = jnp.concatenate([ref[0:24], ref[24:48]], axis=1)
        values[edge] = values[edge] - inside * beyond
        part = jnp.concatenate([ref[48:64], ref[64:80]], axis=1) - wide[edge, 4:20, :]
        outer.append(ring[24 + n : 25 + n, :] * part)
    for q in range(PLANES):
        low = outer[0] if q == 0 else values[q - 1][4:20]
        high = outer[1] if q == PLANES - 1 else values[q + 1][4:20]
        residual[q] = values[q][4:20]
        near = (beside_y(values[q]) + beside_z(values[q], lane))[4:20]
        value = 6.0 * values[q][4:20] - (low + high + near)
        adjoint[2 * q] = value
        adjoint[2 * q + 1] = value


def call(kernel, operands, scalars, outputs, scratch, flops=0, far=0, far_out=(), aliases=None):
    many = isinstance(outputs, list)
    vmem = pl.BlockSpec(memory_space=pltpu.VMEM)
    smem = pl.BlockSpec(memory_space=pltpu.SMEM)
    hbm = pl.BlockSpec(memory_space=pltpu.HBM)
    out_specs = [hbm if n in far_out else vmem for n in range(len(outputs) if many else 1)]
    operands = list(operands)
    for n in range(len(operands) - far, len(operands)):
        operands[n] = pltpu.with_memory_space_constraint(operands[n], pltpu.HBM)
    cost = pl.CostEstimate(flops=flops, bytes_accessed=4 << 20, transcendentals=flops // 16)
    return pl.pallas_call(
        kernel,
        in_specs=[smem] * len(scalars) + [vmem] * (len(operands) - far) + [hbm] * far,
        out_specs=out_specs if many else out_specs[0],
        out_shape=outputs,
        scratch_shapes=scratch,
        input_output_aliases=aliases or {},
        compiler_params=pltpu.CompilerParams(vmem_limit_bytes=VMEM_LIMIT),
        cost_estimate=cost if flops else None,
    )(*scalars, *operands)


def exchange(value, axes):
    return lax.all_to_all(value, axes, split_axis=0, concat_axis=0, tiled=True)


def shape(*sizes):
    return jax.ShapeDtypeStruct(sizes, F32)


def shards(right_side, lift_scale, lift_shift, spectral_weight, local_weight, local_bias, readout):
    z_forward, z_inverse, y_table, x_table = tables()
    everywhere = COL + ROW
    field = right_side[0]
    fields = [shape(GRID, GRID)] * HALF

    row_of = pltpu.SMEM((WIDTH,), F32)
    spread, z_near, y_near, scalars, factors, ring, doubling = call(
        first_kernel,
        (field, z_forward, y_table, lift_scale, lift_shift, readout, local_bias, local_weight),
        (),
        [
            shape(PLANES, 2, COLS, GRID),
            jax.ShapeDtypeStruct(z_forward.shape, BF16),
            jax.ShapeDtypeStruct(y_table.shape, BF16),
            shape(24, GRID),
            shape(168, 128),
            shape(32, GRID),
            shape(64, 128),
        ],
        [row_of] * 4 + [pltpu.SMEM((WIDTH, WIDTH), F32), pltpu.SemaphoreType.DMA((9,))],
        far=8,
    )
    plane = exchange(spread.reshape(COLS, COLS, GRID), COL).reshape(GRID, GRID)
    line_scratch = pltpu.VMEM((MODES, HALF, 2 * GRID), F32)
    plane_scratch = [
        pltpu.VMEM((GRID, GRID), F32),
        pltpu.VMEM((GRID, GRID), BF16),
        pltpu.VMEM((GRID, GRID), BF16),
        line_scratch,
    ]
    lifted = call(lift_kernel, (plane, z_near, y_near, scalars), (), shape(512, 128), plane_scratch)
    lifted = exchange(lifted, everywhere)
    margin, *local = call(
        local_kernel,
        (plane, factors),
        (),
        [shape(2 * COLS, GRID)] + fields,
        [pltpu.VMEM((GRID, GRID), F32)],
        flops=1 << 27,
    )
    pair = pltpu.VMEM((2, 64, 128), F32)
    mixed, spectra = call(
        mix_kernel, (lifted, spectral_weight, x_table), (), [shape(512, 128), shape(2, 64, 128)], [pair, pair]
    )
    mixed = exchange(mixed, everywhere)
    message, *preact = call(
        inverse_kernel,
        (mixed, margin, z_inverse, y_table, scalars, *local),
        (),
        [shape(COLS, 40, 128)] + fields,
        [
            pltpu.VMEM((128, 512), F32),
            line_scratch,
            pltpu.VMEM((GRID, GRID), F32),
            pltpu.VMEM((GRID, GRID), F32),
            pltpu.VMEM((GRID + 8, GRID), F32),
        ],
    )
    message = exchange(message, COL)
    wide, first, second = call(
        edge_kernel, (message, field, ring), (), [shape(PLANES, 24, GRID), shape(80, 128), shape(80, 128)], []
    )
    odd_pairs = [(r, r + 1 if r % 2 else r - 1) for r in range(1, ROWS - 1)]
    even_pairs = [(r, r - 1 if r % 2 else r + 1) for r in range(ROWS)]
    first = lax.ppermute(first, ROW, odd_pairs)
    second = lax.ppermute(second, ROW, even_pairs)
    rest = call(
        inner_kernel,
        (wide, field, ring),
        (),
        shape(PLANES, 24, GRID),
        [],
        flops=1 << 22,
    )
    aliases = {1 + o: o for o in range(HALF)}
    slope = call(slope_kernel, (scalars, *preact), (), fields, [], flops=1 << 25, aliases=aliases)
    first, second, slope = lax.optimization_barrier((first, second, slope))
    rest, adjoint = call(
        stencil_kernel,
        (rest, wide, first, second, ring),
        (),
        [shape(PLANES, COLS, GRID), shape(2 * PLANES, COLS, GRID)],
        [],
    )
    adjoint = exchange(adjoint, COL).reshape(GRID, GRID)
    grads, residual = call(
        grad_kernel,
        (adjoint, rest, z_forward, y_table, *slope),
        (),
        [shape(512, 128), shape(PLANES, COLS, GRID)],
        plane_scratch + [pltpu.SemaphoreType.DMA],
        far_out=(1,),
    )
    grads = exchange(grads, everywhere)
    spectral_grad = call(
        outer_kernel,
        (grads, spectra, x_table, doubling),
        (),
        jax.ShapeDtypeStruct(spectral_weight.shape, BF16),
        [pair, pair, pltpu.VMEM(spectral_weight.shape, BF16), pltpu.SemaphoreType.DMA((8,))],
        far_out=(0,),
    )
    return residual[None], spectral_grad


def solution(mesh):
    fine = Mesh(mesh.devices.reshape(8, 4, 2, 4, 2), ROW + COL)
    in_specs = (P(None, ROW, COL, None), P(), P(), P(ROW, COL, None, None, None), P(), P(), P())
    out_specs = (P(None, ROW, COL, None), P(ROW, COL, None, None, None))
    return jax.shard_map(shards, mesh=fine, in_specs=in_specs, out_specs=out_specs, check_vma=False)
```

```python
import math

import jax
import jax.numpy as jnp
import numpy as np
from jax import lax
from jax.experimental import pallas as pl
from jax.experimental.pallas import tpu as pltpu
from jax.sharding import Mesh
from jax.sharding import PartitionSpec as P

MODES = 64
GRID = 256
WIDTH = 16
HALF = 8
ROWS = 32
PLANES = 8
COLS = 16
ROW = ("y", "zh")
COL = ("zl", "x", "core")
F32 = jnp.float32
BF16 = jnp.bfloat16
VMEM_LIMIT = 40 * 1024 * 1024


def halves(table):
    high = table.astype(jnp.bfloat16)
    low = (table - high.astype(np.float64)).astype(jnp.bfloat16)
    return high, low


def wave(frequencies, points):
    phase = (np.outer(frequencies, points) % GRID) * (2.0 * math.pi / GRID)
    return np.cos(phase) / 16.0, np.sin(phase) / 16.0


def tables():
    points = np.arange(GRID)
    cos_z, sin_z = wave(np.arange(MODES), points)
    z_forward = np.concatenate(halves(np.concatenate([cos_z, -sin_z], axis=0)), axis=0)
    weight = np.where(np.arange(MODES) == 0, 1.0, 2.0)[:, None]
    high, low = halves(np.concatenate([cos_z * weight, -sin_z * weight], axis=0).T)
    z_inverse = np.block([[high, high], [low, np.zeros_like(low)]])
    ky = np.array([2 * r + a - MODES // 2 for a in range(2) for r in range(ROWS)])
    cos_y, sin_y = wave(ky, points)
    y_table = np.concatenate(
        [np.concatenate([cos_y, sin_y], axis=1), np.concatenate([-sin_y, cos_y], axis=1)], axis=0
    )
    y_table = np.concatenate(halves(y_table), axis=0)
    places = np.array([8 * r + q for q in range(PLANES) for r in range(ROWS)])
    cos_x, sin_x = wave(np.arange(MODES) - MODES // 2, places)
    x_table = np.concatenate(halves(np.concatenate([cos_x.T, -sin_x.T], axis=1)), axis=1)
    return z_forward, z_inverse, y_table, x_table


def split(value):
    high = value.astype(BF16)
    return high, (value - high.astype(F32)).astype(BF16)


def dot(left, right, dims):
    return lax.dot_general(left, right, (dims, ((), ())), preferred_element_type=F32)


NN = ((1,), (0,))
NT = ((1,), (1,))


ROOT = math.sqrt(2.0 / math.pi)
CUBE = 0.044715


def gelu_double(value, square):
    return 1.0 + jnp.tanh(value * (ROOT + (ROOT * CUBE) * square))


def gelu_slope(value):
    square = value * value
    double = gelu_double(value, square)
    slope = (0.5 * ROOT) + (1.5 * ROOT * CUBE) * square
    return double * (0.5 + (value * slope) * (2.0 - double))


def bent_half(half):
    return half * jnp.tanh(half * (2.0 * ROOT + (8.0 * ROOT * CUBE) * (half * half)))


def lift(field, half_scale, half_shift):
    scaled = half_scale * field
    return (scaled + scaled) + (bent_half(half_shift + scaled) - bent_half(half_shift - scaled))


def lane_index(shape):
    return lax.broadcasted_iota(jnp.int32, shape, len(shape) - 1)


def swapped(value):
    return pltpu.roll(value, MODES, 1)


def beside_z(value, lane):
    left = jnp.where(lane == 0, 0.0, pltpu.roll(value, 1, 1))
    return left + jnp.where(lane == GRID - 1, 0.0, pltpu.roll(value, GRID - 1, 1))


def plane_forward(fill, z_table, y_table, stage_high, stage_low, lines, out):
    for channel in range(HALF):
        fill(channel, stage_high, stage_low)
        z = dot(z_table[...], stage_high[...], NN)
        z = z[:128] + z[128:] + dot(z_table[0:128, :], stage_low[...], NN)
        lines[:, channel, 0:GRID] = z[:MODES]
        lines[:, channel, GRID:] = z[MODES:]
    high, low = split(lines[...].reshape(MODES * HALF, 2 * GRID))
    spectrum = dot(y_table[...], high, NT)
    spectrum = spectrum[:128] + spectrum[128:] + dot(y_table[0:128, :], low, NT)
    lane = lane_index((ROWS, 128)) // 32
    for tile in range(4):
        parts = [spectrum[b * 32 : b * 32 + 32, tile * 128 : tile * 128 + 128] for b in range(4)]
        for e in range(4):
            total = None
            for b in range(4):
                turn = ((b - e) % 4) * 32
                moved = pltpu.roll(parts[b], turn, 1) if turn else parts[b]
                total = moved if total is None else jnp.where(lane == b, moved, total)
            column = 4 * tile + e
            out[column * 32 : column * 32 + 32, :] = total


def lift_kernel(plane, z_table, y_table, scalars, out, turned, high, low, lines):
    turned[...] = plane[...].T

    def fill(channel, stage_high, stage_low):
        gain, offset = scalars[channel : channel + 1, :], scalars[HALF + channel : HALF + channel + 1, :]
        for t in range(8):
            rows = slice(32 * t, 32 * t + 32)
            stage_high[rows, :], stage_low[rows, :] = split(lift(turned[rows, :], gain, offset))

    plane_forward(fill, z_table, y_table, high, low, lines, out)


def grad_kernel(adjoint, rest, z_table, y_table, *refs):
    slope = refs[:HALF]
    out, residual, turned, high, low, lines, sem = refs[HALF:]
    copy = pltpu.make_async_copy(rest, residual, sem)
    copy.start()
    turned[...] = adjoint[...].T

    def fill(channel, stage_high, stage_low):
        for t in range(8):
            rows = slice(32 * t, 32 * t + 32)
            stage_high[rows, :], stage_low[rows, :] = split(turned[rows, :] * slope[channel][rows, :])

    plane_forward(fill, z_table, y_table, high, low, lines, out)
    copy.wait()


def first_kernel(
    far_field,
    far_z,
    far_y,
    far_scale,
    far_shift,
    far_readout,
    far_bias,
    far_weight,
    spread,
    z_table,
    y_table,
    scalars,
    factors,
    ring,
    doubling,
    scale,
    shift,
    readout,
    bias,
    weight,
    sems,
):
    core, row_place, col_place = lax.axis_index("core"), lax.axis_index(ROW), lax.axis_index(COL)
    pairs = [(far_scale, scale), (far_shift, shift), (far_readout, readout), (far_bias, bias), (far_weight, weight)]
    pairs += [(far_z, z_table), (far_y, y_table)]
    pairs += [(far_field, spread.at[:, k]) for k in range(2)]
    copies = [pltpu.make_async_copy(source, target, sems.at[n]) for n, (source, target) in enumerate(pairs)]
    for copy in copies:
        copy.start()
    row = lax.broadcasted_iota(jnp.int32, (24, GRID), 0)
    first_row = jnp.where(col_place == 0, 4, 3)
    last_row = jnp.where(col_place == COLS - 1, 19, 20)
    ring[0:24, :] = jnp.where(jnp.logical_and(row >= first_row, row <= last_row), 1.0, 0.0).astype(F32)
    row = lax.broadcasted_iota(jnp.int32, (8, GRID), 0)
    before, after = jnp.where(row_place > 0, 1.0, 0.0), jnp.where(row_place < ROWS - 1, 1.0, 0.0)
    odd = jnp.where(row_place % 2 == 1, 1.0, 0.0)
    ring[24:32, :] = jnp.where(row == 0, before, jnp.where(row == 1, after, odd)).astype(F32)
    row = lax.broadcasted_iota(jnp.int32, (64, 128), 0)
    zero_mode = jnp.logical_and((row // HALF) % 4 == 0, col_place == 0)
    doubling[...] = jnp.where(zero_mode, 1.0, 2.0).astype(F32)
    for copy in copies[:5]:
        copy.wait()
    first = core * HALF
    for n in range(HALF):
        for m, value in enumerate((0.5 * scale[first + n], 0.5 * shift[first + n], readout[first + n])):
            scalars[HALF * m + n : HALF * m + n + 1, :] = jnp.full((1, GRID), value, F32)
    for i in range(WIDTH):
        factors[i : i + 1, :] = jnp.full((1, 128), 0.5 * scale[i], F32)
        factors[WIDTH + i : WIDTH + i + 1, :] = jnp.full((1, 128), 0.5 * shift[i], F32)
        for o in range(HALF):
            row = 40 + HALF * i + o
            factors[row : row + 1, :] = jnp.full((1, 128), weight[i, first + o], F32)
    for o in range(HALF):
        factors[32 + o : 33 + o, :] = jnp.full((1, 128), bias[first + o], F32)
    for copy in copies[5:]:
        copy.wait()


def local_kernel(plane, factors, margin, *refs):
    out, turned = refs[:HALF], refs[HALF]
    keep = jnp.where(lax.axis_index("core") == 0, 1.0, 0.0).astype(F32)
    turned[...] = plane[...].T
    margin[...] = jnp.zeros(margin.shape, F32)
    for c in range(1, COLS):
        margin[c : c + 1, :] = plane[16 * c - 1 : 16 * c, :] * keep
        margin[COLS + c - 1 : COLS + c, :] = plane[16 * c : 16 * c + 1, :] * keep

    def step(t, carry):
        rows = pl.ds(pl.multiple_of(t * 64, 64), 64)
        for lanes in (slice(0, 128), slice(128, 256)):
            field = turned[rows, lanes]
            sums = [jnp.broadcast_to(factors[32 + o : 33 + o, :], (64, 128)) for o in range(HALF)]
            for i in range(WIDTH):
                lifted = lift(field, factors[i : i + 1, :], factors[WIDTH + i : WIDTH + i + 1, :])
                for o in range(HALF):
                    row = 40 + HALF * i + o
                    sums[o] = sums[o] + factors[row : row + 1, :] * lifted
            for o in range(HALF):
                out[o][rows, lanes] = sums[o]
        return carry

    lax.fori_loop(0, GRID // 64, step, 0)


def inverse_kernel(received, margin, z_table, y_table, scalars, *refs):
    local, out, preact = refs[:HALF], refs[HALF], refs[HALF + 1 : 2 * HALF + 1]
    grid, lines, spectral, total, padded = refs[2 * HALF + 1 :]
    lane = lane_index((ROWS, 128)) // 32
    for tile in range(4):
        parts = [received[(4 * tile + e) * 32 : (4 * tile + e) * 32 + 32, :] for e in range(4)]
        for b in range(4):
            whole = None
            for e in range(4):
                turn = ((e - b) % 4) * 32
                moved = pltpu.roll(parts[e], turn, 1) if turn else parts[e]
                whole = moved if whole is None else jnp.where(lane == e, moved, whole)
            grid[b * 32 : b * 32 + 32, tile * 128 : tile * 128 + 128] = whole
    high, low = split(grid[...].T)
    modes = dot(jnp.concatenate([high, high], axis=1), y_table[...], NN) + dot(low, y_table[0:128, :], NN)
    lines[...] = modes.reshape(MODES, HALF, 2 * GRID)
    for o in range(HALF):
        modes = jnp.concatenate([lines[:, o, 0:GRID], lines[:, o, GRID:]], axis=0)
        product = dot(z_table[...], jnp.concatenate(split(modes), axis=0), NN)
        spectral[...] = product[:GRID] + product[GRID:]
        read = 0.5 * scalars[2 * HALF + o : 2 * HALF + o + 1, :]
        for t in range(8):
            rows = slice(32 * t, 32 * t + 32)
            value = spectral[rows, :] + local[o][rows, :]
            preact[o][rows, :] = value
            term = (read * value) * gelu_double(value, value * value)
            if o == 0:
                total[rows, :] = term
            else:
                total[rows, :] += term
    padded[0:8, :] = jnp.zeros((8, GRID), F32)
    padded[256:264, :] = jnp.zeros((8, GRID), F32)
    value = total[...].T
    padded[4:260, :] = value
    blank = jnp.zeros((1, GRID), F32)
    lane = lane_index((8, GRID))
    tiles = [None]
    for m in range(1, COLS):
        tile = padded[16 * m : 16 * m + 8, :]
        beside = pltpu.roll(tile, 1, 0) + pltpu.roll(tile, 7, 0) + beside_z(tile, lane)
        tiles.append(6.0 * tile - beside)
    for c in range(COLS):
        before, after = blank, blank
        if c > 0:
            before = tiles[c][3:4] - margin[c : c + 1, :]
        if c < COLS - 1:
            after = tiles[c + 1][4:5] - margin[COLS + c : COLS + c + 1, :]
        for h in range(2):
            lanes = slice(128 * h, 128 * h + 128)
            out[c, 20 * h : 20 * h + 1, :] = before[:, lanes]
            out[c, 20 * h + 1 : 20 * h + 19, :] = padded[16 * c + 3 : 16 * c + 21, lanes]
            out[c, 20 * h + 19 : 20 * h + 20, :] = after[:, lanes]


def slope_kernel(scalars, *refs):
    preact, out = refs[:HALF], refs[HALF:]
    for o in range(HALF):
        read = scalars[2 * HALF + o : 2 * HALF + o + 1, :]
        for t in range(8):
            rows = slice(32 * t, 32 * t + 32)
            out[o][rows, :] = read * gelu_slope(preact[o][rows, :])


def gather_spectra(received, x_table, sign):
    lines = []
    for k in range(2):
        parts = [received[(2 * q + k) * 32 : (2 * q + k) * 32 + 32, :] for q in range(PLANES)]
        lines.append(jnp.concatenate(parts, axis=0).T)
    product = dot(jnp.concatenate(split(jnp.concatenate(lines, axis=0)), axis=0), x_table[...], NN)
    product = product[:, :128] + product[:, 128:]
    product = product[:256] + product[256:]
    first = [product[128 * k : 128 * k + 64] for k in range(2)]
    second = [product[128 * k + 64 : 128 * k + 128] for k in range(2)]
    return [first[k] + sign * swapped(second[k]) for k in range(2)]


def mix_kernel(received, weight, x_table, out, spectra_out, real, imag):
    low = lane_index((64, 128)) < MODES
    sign = jnp.where(low, -1.0, 1.0).astype(F32)
    for k, spectra in enumerate(gather_spectra(received, x_table, sign)):
        spectra_out[k] = spectra
        other = swapped(spectra)
        real[k] = jnp.where(low, spectra, other)
        imag[k] = jnp.where(low, other, spectra)
    parts = [[], []]
    for group in range(8):
        a, j = group // 4, group % 4
        first = jnp.zeros((WIDTH, 128), F32)
        second = jnp.zeros((WIDTH, 128), F32)
        for i in range(WIDTH):
            k, row = i // HALF, group * HALF + i % HALF
            tile = weight[a, j, i].astype(F32)
            first = first + tile * real[k, row : row + 1, :]
            second = second + tile * imag[k, row : row + 1, :]
        mixed = first + sign[:WIDTH] * swapped(second)
        parts[0].append(mixed[:HALF])
        parts[1].append(mixed[HALF:])
    both = []
    for k in range(2):
        mixed = jnp.concatenate(parts[k], axis=0)
        both += [mixed, -sign * swapped(mixed)]
    high, low = split(jnp.concatenate(both, axis=0))
    result = dot(x_table[...], jnp.concatenate([high, high], axis=1), NT) + dot(x_table[:, 0:128], low, NT)
    for q in range(PLANES):
        for k in range(2):
            place = (2 * q + k) * 32
            out[place : place + 32, :] = result[q * 32 : q * 32 + 32, k * 128 : k * 128 + 128]


def outer_kernel(received, spectra_in, x_table, doubling, out, real, imag, stage, sems):
    low = lane_index((64, 128)) < MODES
    sign = jnp.where(low, -1.0, 1.0).astype(F32)
    grads = [doubling[...] * g for g in gather_spectra(received, x_table, sign)]
    turned = [-sign * swapped(g) for g in grads]
    for k in range(2):
        spectra = spectra_in[k]
        other = swapped(spectra)
        real[k] = jnp.where(low, spectra, other)
        imag[k] = jnp.where(low, other, spectra)
    copies = []
    for group in range(8):
        a, j = group // 4, group % 4
        rows = slice(group * HALF, group * HALF + HALF)
        straight = jnp.concatenate([grads[0][rows], grads[1][rows]], axis=0)
        crossed = jnp.concatenate([turned[0][rows], turned[1][rows]], axis=0)
        for i in range(WIDTH):
            k, line = i // HALF, group * HALF + i % HALF
            value = straight * real[k, line : line + 1, :] + crossed * imag[k, line : line + 1, :]
            stage[a, j, i] = value.astype(BF16)
        copies.append(pltpu.make_async_copy(stage.at[a, j], out.at[a, j], sems.at[group]))
        copies[-1].start()
    for copy in copies:
        copy.wait()


def beside_y(value):
    return pltpu.roll(value, 1, 0) + pltpu.roll(value, 23, 0)


def edge_kernel(received, field, ring, wide, first, second):
    lane = lane_index((24, GRID))
    for q in range(PLANES):
        wide[q] = jnp.zeros((24, GRID), F32)
        for h in range(2):
            lanes = slice(128 * h, 128 * h + 128)
            both = received[2 * q, 20 * h : 20 * h + 20, :] + received[2 * q + 1, 20 * h : 20 * h + 20, :]
            wide[q, 3:21, lanes] = both[1:19]
            wide[q, 1:2, lanes] = both[0:1]
            wide[q, 22:23, lanes] = both[19:20]
    sent = []
    for edge, inner in ((0, 1), (PLANES - 1, PLANES - 2)):
        value = wide[edge]
        rest = 6.0 * value - (wide[inner] + beside_y(value) + beside_z(value, lane))
        rest = rest[4:20] - field[edge]
        value = value[2:22]
        sent.append(jnp.concatenate([value[:, :128], value[:, 128:], rest[:, :128], rest[:, 128:]], axis=0))
    odd = jnp.broadcast_to(ring[26:27, 0:128], (72, 128)) > 0.5
    first[...] = jnp.where(odd, sent[1], sent[0])
    second[...] = jnp.where(odd, sent[0], sent[1])


def inner_kernel(wide, field, ring, rest):
    lane = lane_index((24, GRID))
    for q in range(PLANES):
        centre = wide[q]
        across = jnp.zeros((24, GRID), F32)
        if q > 0:
            across = across + wide[q - 1]
        if q < PLANES - 1:
            across = across + wide[q + 1]
        value = 6.0 * centre - (beside_y(centre) + beside_z(centre, lane) + across)
        rest[q] = value
        rest[q, 4:20, :] = value[4:20] - field[q]
        rest[q, 3:4, :] = ring[3:4, :] * (wide[q, 1:2, :] - across[3:4])
        rest[q, 20:21, :] = ring[20:21, :] * (wide[q, 22:23, :] - across[20:21])


def stencil_kernel(rest, wide, first, second, ring, residual, adjoint):
    lane = lane_index((24, GRID))
    inside = ring[0:24, :]
    values = [rest[q] for q in range(PLANES)]
    odd = jnp.broadcast_to(ring[26:27, 0:128], (72, 128)) > 0.5
    before, after = jnp.where(odd, second[...], first[...]), jnp.where(odd, first[...], second[...])
    outer = []
    blank = jnp.zeros((2, GRID), F32)
    for n, ref, edge in ((0, before, 0), (1, after, PLANES - 1)):
        beyond = jnp.concatenate([blank, jnp.concatenate([ref[0:20], ref[20:40]], axis=1), blank], axis=0)
        values[edge] = values[edge] - inside * beyond
        part = jnp.concatenate([ref[40:56], ref[56:72]], axis=1) - wide[edge, 4:20, :]
        outer.append(ring[24 + n : 25 + n, :] * part)
    for q in range(PLANES):
        low = outer[0] if q == 0 else values[q - 1][4:20]
        high = outer[1] if q == PLANES - 1 else values[q + 1][4:20]
        residual[q] = values[q][4:20]
        near = (beside_y(values[q]) + beside_z(values[q], lane))[4:20]
        value = 6.0 * values[q][4:20] - (low + high + near)
        adjoint[2 * q] = value
        adjoint[2 * q + 1] = value


def call(kernel, operands, scalars, outputs, scratch, flops=0, far=0, far_out=(), aliases=None):
    many = isinstance(outputs, list)
    vmem = pl.BlockSpec(memory_space=pltpu.VMEM)
    smem = pl.BlockSpec(memory_space=pltpu.SMEM)
    hbm = pl.BlockSpec(memory_space=pltpu.HBM)
    out_specs = [hbm if n in far_out else vmem for n in range(len(outputs) if many else 1)]
    operands = list(operands)
    for n in range(len(operands) - far, len(operands)):
        operands[n] = pltpu.with_memory_space_constraint(operands[n], pltpu.HBM)
    cost = pl.CostEstimate(flops=flops, bytes_accessed=4 << 20, transcendentals=flops // 16)
    return pl.pallas_call(
        kernel,
        in_specs=[smem] * len(scalars) + [vmem] * (len(operands) - far) + [hbm] * far,
        out_specs=out_specs if many else out_specs[0],
        out_shape=outputs,
        scratch_shapes=scratch,
        input_output_aliases=aliases or {},
        compiler_params=pltpu.CompilerParams(vmem_limit_bytes=VMEM_LIMIT),
        cost_estimate=cost if flops else None,
    )(*scalars, *operands)


def exchange(value, axes):
    return lax.all_to_all(value, axes, split_axis=0, concat_axis=0, tiled=True)


def shape(*sizes):
    return jax.ShapeDtypeStruct(sizes, F32)


def shards(right_side, lift_scale, lift_shift, spectral_weight, local_weight, local_bias, readout):
    z_forward, z_inverse, y_table, x_table = tables()
    everywhere = COL + ROW
    field = right_side[0]
    fields = [shape(GRID, GRID)] * HALF

    row_of = pltpu.SMEM((WIDTH,), F32)
    spread, z_near, y_near, scalars, factors, ring, doubling = call(
        first_kernel,
        (field, z_forward, y_table, lift_scale, lift_shift, readout, local_bias, local_weight),
        (),
        [
            shape(PLANES, 2, COLS, GRID),
            jax.ShapeDtypeStruct(z_forward.shape, BF16),
            jax.ShapeDtypeStruct(y_table.shape, BF16),
            shape(24, GRID),
            shape(168, 128),
            shape(32, GRID),
            shape(64, 128),
        ],
        [row_of] * 4 + [pltpu.SMEM((WIDTH, WIDTH), F32), pltpu.SemaphoreType.DMA((9,))],
        far=8,
    )
    plane = exchange(spread.reshape(COLS, COLS, GRID), COL).reshape(GRID, GRID)
    line_scratch = pltpu.VMEM((MODES, HALF, 2 * GRID), F32)
    plane_scratch = [
        pltpu.VMEM((GRID, GRID), F32),
        pltpu.VMEM((GRID, GRID), BF16),
        pltpu.VMEM((GRID, GRID), BF16),
        line_scratch,
    ]
    lifted = call(lift_kernel, (plane, z_near, y_near, scalars), (), shape(512, 128), plane_scratch)
    lifted = exchange(lifted, everywhere)
    margin, *local = call(
        local_kernel,
        (plane, factors),
        (),
        [shape(2 * COLS, GRID)] + fields,
        [pltpu.VMEM((GRID, GRID), F32)],
        flops=1 << 27,
    )
    pair = pltpu.VMEM((2, 64, 128), F32)
    mixed, spectra = call(
        mix_kernel, (lifted, spectral_weight, x_table), (), [shape(512, 128), shape(2, 64, 128)], [pair, pair]
    )
    mixed = exchange(mixed, everywhere)
    message, *preact = call(
        inverse_kernel,
        (mixed, margin, z_inverse, y_table, scalars, *local),
        (),
        [shape(COLS, 40, 128)] + fields,
        [
            pltpu.VMEM((128, 512), F32),
            line_scratch,
            pltpu.VMEM((GRID, GRID), F32),
            pltpu.VMEM((GRID, GRID), F32),
            pltpu.VMEM((GRID + 8, GRID), F32),
        ],
    )
    message = exchange(message, COL)
    wide, first, second = call(
        edge_kernel, (message, field, ring), (), [shape(PLANES, 24, GRID), shape(72, 128), shape(72, 128)], []
    )
    odd_pairs = [(r, r + 1 if r % 2 else r - 1) for r in range(1, ROWS - 1)]
    even_pairs = [(r, r - 1 if r % 2 else r + 1) for r in range(ROWS)]
    first = lax.ppermute(first, ROW, odd_pairs)
    second = lax.ppermute(second, ROW, even_pairs)
    rest = call(
        inner_kernel,
        (wide, field, ring),
        (),
        shape(PLANES, 24, GRID),
        [],
        flops=1 << 22,
    )
    aliases = {1 + o: o for o in range(HALF)}
    slope = call(slope_kernel, (scalars, *preact), (), fields, [], flops=1 << 25, aliases=aliases)
    first, second, slope = lax.optimization_barrier((first, second, slope))
    rest, adjoint = call(
        stencil_kernel,
        (rest, wide, first, second, ring),
        (),
        [shape(PLANES, COLS, GRID), shape(2 * PLANES, COLS, GRID)],
        [],
    )
    adjoint = exchange(adjoint, COL).reshape(GRID, GRID)
    grads, residual = call(
        grad_kernel,
        (adjoint, rest, z_forward, y_table, *slope),
        (),
        [shape(512, 128), shape(PLANES, COLS, GRID)],
        plane_scratch + [pltpu.SemaphoreType.DMA],
        far_out=(1,),
    )
    grads = exchange(grads, everywhere)
    spectral_grad = call(
        outer_kernel,
        (grads, spectra, x_table, doubling),
        (),
        jax.ShapeDtypeStruct(spectral_weight.shape, BF16),
        [pair, pair, pltpu.VMEM(spectral_weight.shape, BF16), pltpu.SemaphoreType.DMA((8,))],
        far_out=(0,),
    )
    return residual[None], spectral_grad


def solution(mesh):
    fine = Mesh(mesh.devices.reshape(8, 4, 2, 4, 2), ROW + COL)
    in_specs = (P(None, ROW, COL, None), P(), P(), P(ROW, COL, None, None, None), P(), P(), P())
    out_specs = (P(None, ROW, COL, None), P(ROW, COL, None, None, None))
    return jax.shard_map(shards, mesh=fine, in_specs=in_specs, out_specs=out_specs, check_vma=False)
```
